128 devices in a mesh: dom: 8 (over x, core), band: 16 (over z, y).
Axes of the slice: x: 4, y: 4, z: 4, core: 2. Of those that a mesh axis runs over, the one named last changes fastest.
Arguments:
- wavefunctions: bfloat16 [128, 64, 128, 128], P('band', 'dom'), may hold values from -6 to 6
- potential: float32 [64, 128, 128], P('dom'), may hold values from -3 to 1
- projectors: bfloat16 [288, 8, 1024], P('dom'), may hold values from -0.1875 to 0.1875
- margin_atoms: int32 [288], P('dom'), may hold values from 0 to 95, as said below
- tile_rows: int32 [288], P('dom'), may hold values from 0 to 1016
- coupling: float32 [8, 8], replicated, may hold values from -4 to 4
- band_weights: float32 [128], P('band'), may hold values from 0.005 to 0.03
Outputs:
- applied: bfloat16 [128, 64, 128, 128], P('band', 'dom')
- forces: float32 [3, 96], P(None, 'dom')
The draws below stay inside these ranges and needn't reach their ends.
Inputs may be any that keep to these rules, and one draw needn't show every extreme that they name: `margin_atoms`: the list of domain d holds each atom a with a // 12 equal to d - 1, d or d + 1 (cyclically over the domains) exactly once, in an order drawn from the seed; so every atom is listed in three domains.
All inputs are finite; a program needn't handle non-finite values.
Results may differ from the reference program's by a relative error of at most 0.0095.
Values may be sent and summed in bfloat16 or wider, within the bound.
No kernel may reach another device: no remote copies, remote signals or barrier semaphores. Data moves between devices by JAX's collectives and lax.ppermute only.
A program may use at most 64 MiB of HBM per device.

```python
import jax
import jax.numpy as jnp
from jax import lax

NB = 128
NPROJ = 8
CX = 8
NY = 128
NZ = 128
TROWS = 8
ATOM_DEV = 12
ENT_DEV = 36
NX = 64
ATOMS = 96
ENTRIES = 288
N_DOM = 8


def draw_margin_atoms(key, part):
    key = jax.random.fold_in(key, 5)
    atom_count = ATOM_DEV * N_DOM
    domain = jnp.arange(N_DOM, dtype=jnp.int32)[:, None]
    position = jnp.arange(3 * ATOM_DEV, dtype=jnp.int32)[None, :]
    source = ((domain - 1) * ATOM_DEV + position + atom_count) % atom_count
    keys = jax.random.split(key, N_DOM)
    orders = jax.vmap(lambda one_key: jax.random.permutation(one_key, 3 * ATOM_DEV))(keys).astype(jnp.int32)
    return jnp.take_along_axis(source, orders, 1).reshape(-1).astype(jnp.int32)


def place_ends(drawn, key, low, high):
    index_at = [jax.random.randint(jax.random.fold_in(key, axis), (), 0, length) for axis, length in enumerate(drawn.shape)]
    main_axis = drawn.shape.index(max(drawn.shape))
    neighbour = index_at[:main_axis] + [(index_at[main_axis] + 1) % drawn.shape[main_axis]] + index_at[main_axis + 1:]
    return drawn.at[tuple(index_at)].set(low).at[tuple(neighbour)].set(high)


def level_of(key, shape, cuts, least, high):
    level, own = 1.0, jax.random.fold_in(key, 6)
    for dim, parts in cuts:
        heights = jnp.exp(jax.random.uniform(jax.random.fold_in(own, dim), (parts,), jnp.float32, least / len(cuts), high / len(cuts)))
        level = level * jnp.repeat(heights, shape[dim] // parts).reshape([-1 if axis == dim else 1 for axis in range(len(shape))])
    return level


def noise(own_key, shape, spread, bound, pieces=(), held_as=jnp.bfloat16):
    loudness = level_of(own_key, shape, pieces, -0.22, 0.18) if pieces else 1.0
    entries = jax.random.normal(own_key, shape, jnp.float32) * spread * loudness
    return jnp.minimum(jnp.maximum(entries, -bound), bound).astype(held_as)


def setup_inputs(seed: int = 0) -> dict:
    key_of = jax.random.split(jax.random.key(seed), 8)
    wavefunctions = noise(key_of[0], (NB, NX, NY, NZ), 1.0, 6.0, ((0, 16), (1, 8)))
    potential = jnp.clip(-3.0 + 4.0 * jax.random.uniform(key_of[1], (NX, NY, NZ), jnp.float32) ** level_of(key_of[1], (NX, NY, NZ), ((0, 8),), -0.2, 0.2), -3.0, 1.0)
    projectors = noise(key_of[2], (ENTRIES, NPROJ, TROWS * NZ), (TROWS * NZ) ** -0.5, 0.1875, ((0, 8),))
    margin_atoms = draw_margin_atoms(jax.random.fold_in(key_of[7], 71), 0)
    tile_rows = place_ends(jax.random.randint(key_of[4], (ENTRIES,), 0, CX * NY - TROWS + 1), jax.random.fold_in(key_of[4], 1), 0, CX * NY - TROWS).astype(jnp.int32)
    coupling = noise(key_of[5], (NPROJ, NPROJ), 1.0, 4.0, (), jnp.float32)
    band_weights = jnp.clip(0.005 + 0.024999999 * jax.random.uniform(key_of[6], (NB,), jnp.float32) ** level_of(key_of[6], (NB,), ((0, 16),), -0.2, 0.2), 0.005, 0.03)
    return {"wavefunctions": wavefunctions, "potential": potential, "projectors": projectors, "margin_atoms": margin_atoms, "tile_rows": tile_rows, "coupling": coupling, "band_weights": band_weights}


second_coef = (-1.0 / 12.0, 4.0 / 3.0, -2.5, 4.0 / 3.0, -1.0 / 12.0)
first_coef = (1.0 / 12.0, -2.0 / 3.0, 0.0, 2.0 / 3.0, -1.0 / 12.0)


def derivative(real_band, along_axis, stencil):
    summed = jnp.zeros_like(real_band)
    for offset in range(-2, 3):
        if stencil[offset + 2] != 0.0:
            summed = summed + stencil[offset + 2] * jnp.roll(real_band, -offset, along_axis)
    return summed


def tile_index(tile_rows):
    entry_count = tile_rows.shape[0]
    domain = jnp.arange(entry_count, dtype=jnp.int32) // ENT_DEV
    first_row = domain * (CX * NY) + tile_rows
    return (first_row[:, None] + jnp.arange(TROWS, dtype=jnp.int32)[None, :]).reshape(-1)


def reference(wavefunctions, potential, projectors, margin_atoms, tile_rows, coupling, band_weights):
    gather_rows = tile_index(tile_rows)
    entry_count = tile_rows.shape[0]
    proj_real = projectors.astype(jnp.float32)

    def measure_band(one_band):
        real_band = one_band.astype(jnp.float32)
        gradients = [derivative(real_band, along_axis, first_coef).astype(jnp.bfloat16) for along_axis in range(3)]
        stacked = jnp.stack([one_band] + gradients)
        tile_values = stacked.reshape(4, NX * NY, NZ)[:, gather_rows].reshape(4, entry_count, TROWS * NZ)
        return jnp.einsum('qet,eit->eqi', tile_values.astype(jnp.float32), proj_real)

    measured = lax.map(measure_band, wavefunctions)
    atom_table = jax.ops.segment_sum(measured.transpose(1, 2, 0, 3), margin_atoms, num_segments=ATOMS)
    margins = atom_table[:, 0]
    force_margins = atom_table[:, 1:4]
    symmetric = 0.5 * (coupling + coupling.T)
    scaled = jnp.einsum('abj,ij->abi', margins, symmetric, precision=lax.Precision.HIGHEST)
    forces = -2.0 * jnp.einsum('abi,akbi,b->ka', scaled, force_margins, band_weights, precision=lax.Precision.HIGHEST)
    scaled_half = scaled.astype(jnp.bfloat16)
    entry_coef = scaled_half[margin_atoms].astype(jnp.float32).transpose(1, 0, 2)

    def apply_band(inputs):
        one_band, coef_band = inputs
        real_band = one_band.astype(jnp.float32)
        laplace_term = derivative(real_band, 0, second_coef) + derivative(real_band, 1, second_coef) + derivative(real_band, 2, second_coef)
        local_part = -0.5 * laplace_term + potential * real_band
        tile_terms = jnp.einsum('ei,eit->et', coef_band, proj_real).reshape(entry_count * TROWS, NZ)
        nonlocal_part = jnp.zeros((NX * NY, NZ), jnp.float32).at[gather_rows].add(tile_terms)
        return (local_part + nonlocal_part.reshape(NX, NY, NZ)).astype(jnp.bfloat16)

    applied = lax.map(apply_band, (wavefunctions, entry_coef))
    return applied, forces
```

```python
import functools

import jax
import jax.numpy as jnp
from jax import lax
from jax.experimental import pallas as pl
from jax.experimental.pallas import tpu as pltpu
from jax.sharding import PartitionSpec as P

ATOM_DEV = 12
GROUPS = 3
LANES = 128
PAD = 2

f32 = jnp.float32
bf16 = jnp.bfloat16


def ring(x, axis, step):
    count = lax.axis_size(axis)
    return lax.ppermute(x, axis, [(i, (i + step) % count) for i in range(count)])


def to_rows(src, b, plane, y0, dst, base):
    part = src[b, plane, pl.ds(y0, 16), :].astype(f32)
    dst[pl.ds(base + b, 16, stride=8), :] = part


def tile_base(first_row, k, width_y):
    row = first_row + k
    plane = lax.shift_right_logical(row, 7)
    return (row + plane * (2 * PAD) + PAD + PAD * (width_y + 2 * PAD)) * 8


def at_row(ref, base):
    return ref[pl.ds(pl.multiple_of(base, 8), 8), :]


def diagonal_blocks(product, field):
    lane = lax.broadcasted_iota(jnp.int32, (8, LANES), 1)
    total = jnp.zeros((8, LANES), f32)
    for s in range(ATOM_DEV):
        start = (field * ATOM_DEV + s) * 8
        total = total + jnp.where(
            lax.shift_right_logical(lane, 3) == s, product[start : start + 8, :], 0.0
        )
    return total


def measure(rows_ref, group, table, width_y, fields):
    stacked = []
    for field in fields:
        for s in range(ATOM_DEV):
            first = rows_ref[group * ATOM_DEV + s]
            stacked.append(
                jnp.concatenate(
                    [field(tile_base(first, k, width_y)) for k in range(8)], axis=1
                )
            )
    values = jnp.concatenate(stacked, axis=0).astype(bf16)
    product = lax.dot_general(
        values, table, (((1,), (1,)), ((), ())), preferred_element_type=f32
    )
    return [diagonal_blocks(product, q) for q in range(len(fields))]


def relayout_kernel(
    rows_ref, entry_ref, wave_ref, proj_ref, grid_ref, table_ref, margin_ref, proj_scr, *, width_y
):
    stride = width_y + 2 * PAD
    planes = wave_ref.shape[1]
    chunks = width_y // 16

    def convert(step, carry):
        plane = step // chunks
        y0 = pl.multiple_of((step % chunks) * 16, 16)
        base = ((plane + PAD) * stride + PAD + y0) * 8
        for b in range(8):
            to_rows(wave_ref, b, plane, y0, grid_ref, base)
        return carry

    lax.fori_loop(0, planes * chunks, convert, 0)

    def wrap(plane, carry):
        base = pl.multiple_of((plane + PAD) * stride * 8, 8)
        grid_ref[pl.ds(base, 8 * PAD), :] = grid_ref[pl.ds(base + width_y * 8, 8 * PAD), :]
        grid_ref[pl.ds(base + (width_y + PAD) * 8, 8 * PAD), :] = grid_ref[
            pl.ds(base + PAD * 8, 8 * PAD), :
        ]
        return carry

    lax.fori_loop(0, planes, wrap, 0)

    def clear(step, carry):
        for plane in (0, 1, planes + PAD, planes + PAD + 1):
            base = pl.multiple_of((plane * stride + PAD + step * 8) * 8, 8)
            grid_ref[pl.ds(base, 64), :] = jnp.zeros((64, LANES), f32)
        return carry

    lax.fori_loop(0, width_y // 8, clear, 0)

    def one_group(group, carry):
        proj_scr[ATOM_DEV * 8 :, :] = jnp.zeros((LANES - ATOM_DEV * 8, proj_scr.shape[1]), f32)
        for s in range(ATOM_DEV):
            entry = entry_ref[group * ATOM_DEV + s]
            proj_scr[s * 8 : s * 8 + 8, :] = proj_ref[entry].astype(f32)
        table = proj_scr[...].astype(bf16)
        table_ref[group] = table
        (margin_ref[group],) = measure(
            rows_ref, group, table, width_y, [lambda base: at_row(grid_ref, base)]
        )
        return carry

    lax.fori_loop(0, GROUPS, one_group, 0)


def third_shift(center, offset):
    return pltpu.roll(center, (-offset) % center.shape[-1], 1)


def local_kernel(rows_ref, grid_ref, pot_ref, table_ref, local_ref, margin_ref, *, width_y):
    stride = width_y + 2 * PAD
    planes = pot_ref.shape[0]
    chunk = 8

    def one_chunk(step, carry):
        plane = step // (width_y // chunk)
        y0 = pl.multiple_of((step % (width_y // chunk)) * chunk, chunk)
        base = ((plane + PAD) * stride + PAD + y0) * 8
        column = [at_row(grid_ref, base + (k - 2) * 8) for k in range(chunk + 4)]
        out_base = pl.multiple_of((plane * width_y + y0) * 8, 8)
        hop = stride * 8
        for k in range(chunk):
            here = base + k * 8
            center = column[k + 2]
            near = column[k + 1] + column[k + 3]
            far = column[k] + column[k + 4]
            near = near + at_row(grid_ref, here - hop)
            near = near + at_row(grid_ref, here + hop)
            far = far + at_row(grid_ref, here - 2 * hop)
            far = far + at_row(grid_ref, here + 2 * hop)
            near = near + (third_shift(center, -1) + third_shift(center, 1))
            far = far + (third_shift(center, -2) + third_shift(center, 2))
            weight = pot_ref[plane, pl.ds(y0 + k, 1), :] + 3.75
            local_ref[pl.ds(out_base + k * 8, 8), :] = (
                weight * center - (2.0 / 3.0) * near + (1.0 / 24.0) * far
            )
        return carry

    lax.fori_loop(0, planes * (width_y // chunk), one_chunk, 0)

    def along_y(base):
        near = at_row(grid_ref, base + 8) - at_row(grid_ref, base - 8)
        far = at_row(grid_ref, base + 16) - at_row(grid_ref, base - 16)
        return (2.0 / 3.0) * near - (1.0 / 12.0) * far

    def along_z(base):
        center = at_row(grid_ref, base)
        near = third_shift(center, 1) - third_shift(center, -1)
        far = third_shift(center, 2) - third_shift(center, -2)
        return (2.0 / 3.0) * near - (1.0 / 12.0) * far

    def one_group(group, carry):
        second, third = measure(rows_ref, group, table_ref[group], width_y, [along_y, along_z])
        margin_ref[0, group] = second
        margin_ref[1, group] = third
        return carry

    lax.fori_loop(0, GROUPS, one_group, 0)


def first_kernel(
    rows_ref, grid_in, low_ref, high_ref, table_ref, yz_ref, grid_ref, margin_ref, *, width_y
):
    del grid_in
    stride = width_y + 2 * PAD
    planes = grid_ref.shape[0] // (8 * stride) - 2 * PAD
    chunks = width_y // 16
    hop = stride * 8

    def convert(step, carry):
        y0 = pl.multiple_of(step * 16, 16)
        for plane in range(PAD):
            low = (plane * stride + PAD + y0) * 8
            high = ((plane + planes + PAD) * stride + PAD + y0) * 8
            for b in range(8):
                to_rows(low_ref, b, plane, y0, grid_ref, low)
                to_rows(high_ref, b, plane, y0, grid_ref, high)
        return carry

    lax.fori_loop(0, chunks, convert, 0)

    def along_x(base):
        near = at_row(grid_ref, base + hop) - at_row(grid_ref, base - hop)
        far = at_row(grid_ref, base + 2 * hop) - at_row(grid_ref, base - 2 * hop)
        return (2.0 / 3.0) * near - (1.0 / 12.0) * far

    def one_group(group, carry):
        (first,) = measure(rows_ref, group, table_ref[group], width_y, [along_x])
        margin_ref[group, 0] = first
        margin_ref[group, 1] = yz_ref[0, group]
        margin_ref[group, 2] = yz_ref[1, group]
        return carry

    lax.fori_loop(0, GROUPS, one_group, 0)


def apply_kernel(
    rows_ref, local_in, low_ref, high_ref, table_ref, scaled_ref, local_ref, out_ref, *, width_y
):
    del local_in
    planes = out_ref.shape[1]
    chunks = width_y // 16
    lane = lax.broadcasted_iota(jnp.int32, (8, LANES), 1)

    def one_group(group, carry):
        scaled = scaled_ref[group]
        blocks = [
            jnp.where(lax.shift_right_logical(lane, 3) == s, scaled, 0.0)
            for s in range(ATOM_DEV)
        ]
        coef = jnp.concatenate(blocks, axis=0).astype(bf16)
        terms = jnp.dot(coef, table_ref[group], preferred_element_type=f32)
        for s in range(ATOM_DEV):
            base = pl.multiple_of(rows_ref[group * ATOM_DEV + s] * 8, 8)
            for k in range(8):
                where = pl.ds(base + k * 8, 8)
                local_ref[where, :] = (
                    local_ref[where, :] + terms[s * 8 : s * 8 + 8, k * LANES : (k + 1) * LANES]
                )
        return carry

    lax.fori_loop(0, GROUPS, one_group, 0)

    def read(plane, y0, b):
        base = (plane * width_y + y0) * 8
        return local_ref[pl.ds(base + b, 16, stride=8), :]

    def edges(step, carry):
        y0 = pl.multiple_of(step * 16, 16)
        at_y = pl.ds(y0, 16)
        for b in range(8):
            low2 = low_ref[b, 0, at_y, :].astype(f32)
            low1 = low_ref[b, 1, at_y, :].astype(f32)
            high1 = high_ref[b, 0, at_y, :].astype(f32)
            high2 = high_ref[b, 1, at_y, :].astype(f32)
            out_ref[b, 0, at_y, :] = (
                read(0, y0, b) - (2.0 / 3.0) * low1 + (1.0 / 24.0) * low2
            ).astype(bf16)
            out_ref[b, 1, at_y, :] = (read(1, y0, b) + (1.0 / 24.0) * low1).astype(bf16)
            out_ref[b, planes - 2, at_y, :] = (
                read(planes - 2, y0, b) + (1.0 / 24.0) * high1
            ).astype(bf16)
            out_ref[b, planes - 1, at_y, :] = (
                read(planes - 1, y0, b) - (2.0 / 3.0) * high1 + (1.0 / 24.0) * high2
            ).astype(bf16)
        return carry

    lax.fori_loop(0, chunks, edges, 0)

    def inner(step, carry):
        plane = 2 + step // chunks
        y0 = pl.multiple_of((step % chunks) * 16, 16)
        for b in range(8):
            out_ref[b, plane, pl.ds(y0, 16), :] = read(plane, y0, b).astype(bf16)
        return carry

    lax.fori_loop(0, (planes - 4) * chunks, inner, 0)


def scale_kernel(own_ref, above_ref, below_ref, mixing_ref, scaled_ref):
    total = own_ref[...] + above_ref[...] + below_ref[...]
    scaled_ref[...] = jnp.dot(
        total, mixing_ref[...], precision=lax.Precision.HIGHEST, preferred_element_type=f32
    )


VMEM = pl.BlockSpec(memory_space=pltpu.VMEM)
SMEM = pl.BlockSpec(memory_space=pltpu.SMEM)
PARAMS = pltpu.CompilerParams(vmem_limit_bytes=24 * 1024 * 1024)


def cost(flops, moved):
    return pl.CostEstimate(flops=flops, bytes_accessed=moved, transcendentals=0)


def per_device(
    wavefunctions, potential, projectors, margin_atoms, tile_rows, coupling, band_weights
):
    band_count, plane_count, width_y, width_z = wavefunctions.shape
    proj_count, tile_len = projectors.shape[1:]
    assert (band_count, proj_count, width_y, width_z) == (8, 8, 128, LANES)
    grid_rows = (plane_count + 2 * PAD) * (width_y + 2 * PAD) * 8
    local_rows = plane_count * width_y * 8

    above = wavefunctions[:, plane_count - PAD :]
    below = wavefunctions[:, :PAD]
    low_halo = ring(above, "dom", 1)
    high_halo = ring(below, "dom", -1)

    domain_count = lax.axis_size("dom")
    own_index = lax.axis_index("dom")
    relative = (margin_atoms // ATOM_DEV - own_index + 1 + domain_count) % domain_count
    slots = relative * ATOM_DEV + margin_atoms % ATOM_DEV
    entry_count = slots.shape[0]
    assert entry_count == GROUPS * ATOM_DEV
    hit = slots[None, :] == jnp.arange(entry_count, dtype=jnp.int32)[:, None]
    entry_of = jnp.where(hit, jnp.arange(entry_count, dtype=jnp.int32)[None, :], 0).sum(1)
    row_of = jnp.where(hit, tile_rows[None, :], 0).sum(1)

    grid, table, margins = pl.pallas_call(
        functools.partial(relayout_kernel, width_y=width_y),
        out_shape=(
            jax.ShapeDtypeStruct((grid_rows, LANES), f32),
            jax.ShapeDtypeStruct((GROUPS, LANES, tile_len), bf16),
            jax.ShapeDtypeStruct((GROUPS, 8, LANES), f32),
        ),
        in_specs=[SMEM, SMEM, VMEM, VMEM],
        out_specs=(VMEM, VMEM, VMEM),
        scratch_shapes=[pltpu.VMEM((LANES, tile_len), f32)],
        compiler_params=PARAMS,
        cost_estimate=cost(10**7, 10 * 2**20),
        name="relayout",
    )(row_of, entry_of, wavefunctions, projectors)

    from_above = ring(margins[0], "dom", -1)
    from_below = ring(margins[2], "dom", 1)

    local, yz_margins = pl.pallas_call(
        functools.partial(local_kernel, width_y=width_y),
        out_shape=(
            jax.ShapeDtypeStruct((local_rows, LANES), f32),
            jax.ShapeDtypeStruct((2, GROUPS, 8, LANES), f32),
        ),
        in_specs=[SMEM, VMEM, VMEM, VMEM],
        out_specs=(VMEM, VMEM),
        compiler_params=PARAMS,
        cost_estimate=cost(10**7, 16 * 2**20),
        name="local",
    )(row_of, grid, potential, table)

    symmetric = 0.5 * (coupling + coupling.T)
    lane_atom = jnp.arange(LANES, dtype=jnp.int32) // proj_count
    same = (lane_atom[:, None] == lane_atom[None, :]) & (lane_atom[:, None] < ATOM_DEV)
    mixing = jnp.where(same, jnp.tile(symmetric, (LANES // proj_count,) * 2), 0.0)
    scaled = pl.pallas_call(
        scale_kernel,
        out_shape=jax.ShapeDtypeStruct((8, LANES), f32),
        in_specs=[VMEM] * 4,
        out_specs=VMEM,
        name="scale",
    )(margins[1], from_above, from_below, mixing)
    scaled_low = ring(scaled, "dom", 1)
    scaled_high = ring(scaled, "dom", -1)

    _, force_margins = pl.pallas_call(
        functools.partial(first_kernel, width_y=width_y),
        out_shape=(
            jax.ShapeDtypeStruct((grid_rows, LANES), f32),
            jax.ShapeDtypeStruct((GROUPS, 3, 8, LANES), f32),
        ),
        in_specs=[SMEM, VMEM, VMEM, VMEM, VMEM, VMEM],
        out_specs=(VMEM, VMEM),
        input_output_aliases={1: 0},
        compiler_params=PARAMS,
        cost_estimate=cost(10**7, 4 * 2**20),
        name="first",
    )(row_of, grid, low_halo, high_halo, table, yz_margins)
    force_above = ring(force_margins[0], "dom", -1)
    force_below = ring(force_margins[2], "dom", 1)

    _, applied = pl.pallas_call(
        functools.partial(apply_kernel, width_y=width_y),
        out_shape=(
            jax.ShapeDtypeStruct((local_rows, LANES), f32),
            jax.ShapeDtypeStruct(wavefunctions.shape, bf16),
        ),
        in_specs=[SMEM, VMEM, VMEM, VMEM, VMEM, VMEM],
        out_specs=(VMEM, VMEM),
        input_output_aliases={1: 0},
        compiler_params=PARAMS,
        cost_estimate=cost(10**7, 8 * 2**20),
        name="apply",
    )(row_of, local, low_halo, high_halo, table, jnp.stack([scaled_low, scaled, scaled_high]))

    owned = force_margins[1] + force_above + force_below
    weighted = -2.0 * band_weights[:, None] * scaled
    contribution = (owned * weighted[None]).sum(1)
    block_count = lax.axis_size("band")
    copies = jnp.broadcast_to(contribution[None], (block_count,) + contribution.shape)
    gathered = lax.all_to_all(copies, "band", 0, 0)
    summed = gathered.sum(0)[:, : ATOM_DEV * proj_count]
    forces = summed.reshape(3, ATOM_DEV, proj_count).sum(2)
    return (applied, forces)


def solution(mesh):
    placed = (
        P("band", "dom", None, None),
        P("dom", None, None),
        P("dom", None, None),
        P("dom"),
        P("dom"),
        P(),
        P("band"),
    )
    return jax.shard_map(
        per_device,
        mesh=mesh,
        in_specs=placed,
        out_specs=(P("band", "dom", None, None), P(None, "dom")),
        check_vma=False,
    )
```

```python
import functools

import jax
import jax.numpy as jnp
from jax import lax
from jax.experimental import pallas as pl
from jax.experimental.pallas import tpu as pltpu
from jax.sharding import PartitionSpec as P

ATOM_DEV = 12
GROUPS = 3
LANES = 128
PAD = 2

f32 = jnp.float32
bf16 = jnp.bfloat16


def ring(x, axis, step):
    count = lax.axis_size(axis)
    return lax.ppermute(x, axis, [(i, (i + step) % count) for i in range(count)])


def to_rows(src, b, plane, y0, dst, base):
    part = src[b, plane, pl.ds(y0, 16), :].astype(f32)
    dst[pl.ds(base + b, 16, stride=8), :] = part


def tile_base(first_row, k, width_y):
    row = first_row + k
    plane = lax.shift_right_logical(row, 7)
    return (row + plane * (2 * PAD) + PAD + PAD * (width_y + 2 * PAD)) * 8


def at_row(ref, base):
    return ref[pl.ds(pl.multiple_of(base, 8), 8), :]


def diagonal_blocks(product, field):
    lane = lax.broadcasted_iota(jnp.int32, (8, LANES), 1)
    total = jnp.zeros((8, LANES), f32)
    for s in range(ATOM_DEV):
        start = (field * ATOM_DEV + s) * 8
        total = total + jnp.where(
            lax.shift_right_logical(lane, 3) == s, product[start : start + 8, :], 0.0
        )
    return total


def measure(rows_ref, group, table, width_y, fields):
    stacked = []
    for field in fields:
        for s in range(ATOM_DEV):
            first = rows_ref[group * ATOM_DEV + s]
            stacked.append(
                jnp.concatenate(
                    [field(tile_base(first, k, width_y)) for k in range(8)], axis=1
                )
            )
    values = jnp.concatenate(stacked, axis=0).astype(bf16)
    product = lax.dot_general(
        values, table, (((1,), (1,)), ((), ())), preferred_element_type=f32
    )
    return [diagonal_blocks(product, q) for q in range(len(fields))]


def edge_kernel(wave_ref, below_ref, above_ref, sems):
    planes = wave_ref.shape[1]
    copies = [
        pltpu.make_async_copy(wave_ref.at[:, pl.ds(0, PAD)], below_ref, sems.at[0]),
        pltpu.make_async_copy(wave_ref.at[:, pl.ds(planes - PAD, PAD)], above_ref, sems.at[1]),
    ]
    for copy in copies:
        copy.start()
    for copy in copies:
        copy.wait()


def relayout_kernel(
    own_ref,
    atoms_hbm,
    first_rows_hbm,
    wave_hbm,
    proj_hbm,
    rows_ref,
    wave_ref,
    grid_ref,
    table_ref,
    low_ref,
    mid_ref,
    high_ref,
    entry_ref,
    atoms_ref,
    first_rows_ref,
    proj_ref,
    proj_scr,
    wave_sems,
    other_sems,
    *,
    width_y,
    domain_count,
):
    stride = width_y + 2 * PAD
    planes = wave_ref.shape[1]
    chunks = width_y // 16

    def plane_copy(plane):
        at_plane = (slice(None), pl.ds(plane, 1))
        return pltpu.make_async_copy(
            wave_hbm.at[at_plane], wave_ref.at[at_plane], wave_sems.at[plane]
        )

    proj_copy = pltpu.make_async_copy(proj_hbm, proj_ref, other_sems.at[0])
    atoms_copy = pltpu.make_async_copy(atoms_hbm, atoms_ref, other_sems.at[1])
    rows_copy = pltpu.make_async_copy(first_rows_hbm, first_rows_ref, other_sems.at[2])
    atoms_copy.start()
    rows_copy.start()
    for plane in range(planes):
        plane_copy(plane).start()
    proj_copy.start()

    def clear(step, carry):
        for plane in (0, 1, planes + PAD, planes + PAD + 1):
            base = pl.multiple_of((plane * stride + PAD + step * 8) * 8, 8)
            grid_ref[pl.ds(base, 64), :] = jnp.zeros((64, LANES), f32)
        return carry

    lax.fori_loop(0, width_y // 8, clear, 0)

    atoms_copy.wait()
    rows_copy.wait()

    def place(entry, carry):
        atom = atoms_ref[entry]
        owner = lax.shift_right_logical(atom * 171, 11)
        relative = lax.rem(owner - own_ref[0] + 1 + domain_count, domain_count)
        slot = relative * ATOM_DEV + atom - owner * ATOM_DEV
        entry_ref[slot] = entry
        rows_ref[slot] = first_rows_ref[entry]
        return carry

    lax.fori_loop(0, GROUPS * ATOM_DEV, place, 0)

    def one_plane(plane, carry):
        plane_copy(plane).wait()

        def convert(step, inner):
            y0 = pl.multiple_of(step * 16, 16)
            base = ((plane + PAD) * stride + PAD + y0) * 8
            for b in range(8):
                to_rows(wave_ref, b, plane, y0, grid_ref, base)
            return inner

        lax.fori_loop(0, chunks, convert, 0)
        base = pl.multiple_of((plane + PAD) * stride * 8, 8)
        grid_ref[pl.ds(base, 8 * PAD), :] = grid_ref[pl.ds(base + width_y * 8, 8 * PAD), :]
        grid_ref[pl.ds(base + (width_y + PAD) * 8, 8 * PAD), :] = grid_ref[
            pl.ds(base + PAD * 8, 8 * PAD), :
        ]
        return carry

    lax.fori_loop(0, planes, one_plane, 0)
    proj_copy.wait()
    proj_scr[ATOM_DEV * 8 :, :] = jnp.zeros((LANES - ATOM_DEV * 8, proj_scr.shape[1]), f32)
    for group, margin_ref in enumerate((low_ref, mid_ref, high_ref)):
        for s in range(ATOM_DEV):
            entry = entry_ref[group * ATOM_DEV + s]
            proj_scr[s * 8 : s * 8 + 8, :] = proj_ref[entry].astype(f32)
        table = proj_scr[...].astype(bf16)
        table_ref[group] = table
        (margin_ref[...],) = measure(
            rows_ref, group, table, width_y, [lambda base: at_row(grid_ref, base)]
        )


def third_shift(center, offset):
    return pltpu.roll(center, (-offset) % center.shape[-1], 1)


def circulant(near, far, center, length):
    row = lax.broadcasted_iota(jnp.int32, (length, length), 0)
    column = lax.broadcasted_iota(jnp.int32, (length, length), 1)
    distance = lax.bitwise_and(row - column, length - 1)
    table = jnp.where((distance == 1) | (distance == length - 1), near, 0.0)
    table = jnp.where((distance == 2) | (distance == length - 2), far, table)
    return jnp.where(distance == 0, center, table).astype(bf16)


def local_kernel(wave_ref, pot_ref, local_ref, token_ref):
    token_ref[...] = jnp.zeros(token_ref.shape, f32)
    bands, planes, width_y, width_z = wave_ref.shape
    along_y = circulant(-16.0, 1.0, 0.0, width_y)
    along_z = circulant(-16.0, 1.0, 90.0, width_z)

    def one_band(b, carry):
        for plane in range(planes):
            wave = wave_ref[b, plane]
            summed = jnp.dot(
                jnp.concatenate([wave, along_y], axis=1),
                jnp.concatenate([along_z, wave], axis=0),
                preferred_element_type=f32,
            )
            for offset, factor in ((1, -16.0), (2, 1.0)):
                sides = [q for q in (plane - offset, plane + offset) if 0 <= q < planes]
                side = wave_ref[b, sides[0]].astype(f32)
                for q in sides[1:]:
                    side = side + wave_ref[b, q].astype(f32)
                summed = summed + (side if factor == 1.0 else factor * side)
            local_ref[pl.ds(plane * width_y * bands + b, width_y, stride=bands), :] = (
                summed * (1.0 / 24.0) + pot_ref[plane] * wave.astype(f32)
            )
        return carry

    lax.fori_loop(0, bands, one_band, 0)


def gradient_kernel(rows_ref, grid_ref, table_ref, coupling_ref, margin_ref, mixing_ref, *, width_y):
    def along_y(base):
        near = at_row(grid_ref, base + 8) - at_row(grid_ref, base - 8)
        far = at_row(grid_ref, base + 16) - at_row(grid_ref, base - 16)
        return (2.0 / 3.0) * near - (1.0 / 12.0) * far

    def along_z(base):
        center = at_row(grid_ref, base)
        near = third_shift(center, 1) - third_shift(center, -1)
        far = third_shift(center, 2) - third_shift(center, -2)
        return (2.0 / 3.0) * near - (1.0 / 12.0) * far

    for group in range(GROUPS):
        second, third = measure(rows_ref, group, table_ref[group], width_y, [along_y, along_z])
        margin_ref[0, group] = second
        margin_ref[1, group] = third

    proj_count = coupling_ref.shape[0]
    symmetric = 0.5 * (coupling_ref[...] + coupling_ref[...].T)
    index = lax.broadcasted_iota(jnp.int32, (proj_count, LANES), 0)
    lane = lax.broadcasted_iota(jnp.int32, (proj_count, LANES), 1)
    spread = (lax.bitwise_and(lane, proj_count - 1) == index).astype(f32)
    tiled = jnp.dot(
        symmetric, spread, precision=lax.Precision.HIGHEST, preferred_element_type=f32
    )
    for a in range(LANES // proj_count):
        keep = (lax.shift_right_logical(lane, 3) == a) & (lane < ATOM_DEV * proj_count)
        mixing_ref[a * proj_count : (a + 1) * proj_count, :] = jnp.where(keep, tiled, 0.0)


def first_kernel(
    rows_ref,
    grid_in,
    low_ref,
    high_ref,
    table_ref,
    yz_ref,
    scaled_ref,
    grid_ref,
    low_out,
    mid_out,
    high_out,
    *,
    width_y,
):
    del grid_in
    stride = width_y + 2 * PAD
    planes = grid_ref.shape[0] // (8 * stride) - 2 * PAD
    chunks = width_y // 16
    hop = stride * 8

    def convert(step, carry):
        y0 = pl.multiple_of(step * 16, 16)
        for plane in range(PAD):
            low = (plane * stride + PAD + y0) * 8
            high = ((plane + planes + PAD) * stride + PAD + y0) * 8
            for b in range(8):
                to_rows(low_ref, b, plane, y0, grid_ref, low)
                to_rows(high_ref, b, plane, y0, grid_ref, high)
        return carry

    lax.fori_loop(0, chunks, convert, 0)

    def along_x(base):
        near = at_row(grid_ref, base + hop) - at_row(grid_ref, base - hop)
        far = at_row(grid_ref, base + 2 * hop) - at_row(grid_ref, base - 2 * hop)
        return (2.0 / 3.0) * near - (1.0 / 12.0) * far

    for group, margin_ref in enumerate((low_out, mid_out, high_out)):
        (first,) = measure(rows_ref, group, table_ref[group], width_y, [along_x])
        margin_ref[0] = first
        margin_ref[1] = yz_ref[0, group]
        margin_ref[2] = yz_ref[1, group]
        margin_ref[3] = scaled_ref[...]


def apply_kernel(
    rows_ref,
    local_in,
    low_ref,
    high_ref,
    table_ref,
    scaled_low_ref,
    scaled_ref,
    scaled_high_ref,
    local_ref,
    out_hbm,
    out_ref,
    sems,
):
    del local_in
    bands, planes, width_y, _ = out_ref.shape
    chunks = width_y // 16
    lane = lax.broadcasted_iota(jnp.int32, (8, LANES), 1)

    for group, source in enumerate((scaled_low_ref, scaled_ref, scaled_high_ref)):
        scaled = source[3]
        blocks = [
            jnp.where(lax.shift_right_logical(lane, 3) == s, scaled, 0.0)
            for s in range(ATOM_DEV)
        ]
        coef = jnp.concatenate(blocks, axis=0).astype(bf16)
        terms = jnp.dot(coef, table_ref[group], preferred_element_type=f32)
        for s in range(ATOM_DEV):
            base = pl.multiple_of(rows_ref[group * ATOM_DEV + s] * 8, 8)
            for k in range(8):
                where = pl.ds(base + k * 8, 8)
                local_ref[where, :] = (
                    local_ref[where, :] + terms[s * 8 : s * 8 + 8, k * LANES : (k + 1) * LANES]
                )

    def plane_copy(plane):
        at_plane = (slice(None), pl.ds(plane, 1))
        return pltpu.make_async_copy(out_ref.at[at_plane], out_hbm.at[at_plane], sems.at[plane])

    near, far = -2.0 / 3.0, 1.0 / 24.0
    halo_terms = {
        0: ((low_ref, 1, near), (low_ref, 0, far)),
        1: ((low_ref, 1, far),),
        planes - 2: ((high_ref, 0, far),),
        planes - 1: ((high_ref, 0, near), (high_ref, 1, far)),
    }
    for plane in range(planes):

        def finish(step, carry, plane=plane):
            y0 = pl.multiple_of(step * 16, 16)
            at_y = pl.ds(y0, 16)
            for b in range(bands):
                base = (plane * width_y + y0) * 8 + b
                value = local_ref[pl.ds(base, 16, stride=8), :]
                for ref, index, factor in halo_terms.get(plane, ()):
                    value = value + factor * ref[b, index, at_y, :].astype(f32)
                out_ref[b, plane, at_y, :] = value.astype(bf16)
            return carry

        lax.fori_loop(0, chunks, finish, 0)
        plane_copy(plane).start()
    for plane in range(planes):
        plane_copy(plane).wait()


def weigh_kernel(own_ref, above_ref, below_ref, weight_ref, _, copies_ref):
    weighted = -2.0 * weight_ref[...] * own_ref[3]
    parts = []
    for k in range(3):
        total = own_ref[k] + above_ref[k] + below_ref[k]
        parts.append(jnp.sum(total * weighted, axis=0, keepdims=True))
    parts = jnp.concatenate(parts, axis=0)
    for copy in range(copies_ref.shape[0]):
        copies_ref[copy] = parts


def scale_kernel(own_ref, above_ref, below_ref, mixing_ref, scaled_ref):
    total = own_ref[...] + above_ref[...] + below_ref[...]
    scaled_ref[...] = jnp.dot(
        total, mixing_ref[...], precision=lax.Precision.HIGHEST, preferred_element_type=f32
    )


VMEM = pl.BlockSpec(memory_space=pltpu.VMEM)
SMEM = pl.BlockSpec(memory_space=pltpu.SMEM)
HBM = pl.BlockSpec(memory_space=pltpu.HBM)
MIB = 2**20


def in_hbm(x):
    return pltpu.with_memory_space_constraint(x, pltpu.HBM)


def call(kernel, name, outs, ins, out_specs, scratch=(), limit=8, **kwargs):
    return pl.pallas_call(
        kernel,
        out_shape=tuple(
            pltpu.HBM(shape, dtype) if spec is HBM else jax.ShapeDtypeStruct(shape, dtype)
            for (shape, dtype), spec in zip(outs, out_specs)
        ),
        in_specs=ins,
        out_specs=tuple(out_specs),
        scratch_shapes=list(scratch),
        compiler_params=pltpu.CompilerParams(vmem_limit_bytes=limit * MIB),
        cost_estimate=pl.CostEstimate(flops=1000, bytes_accessed=1000, transcendentals=0),
        name=name,
        **kwargs,
    )


def per_device(
    wavefunctions, potential, projectors, margin_atoms, tile_rows, coupling, band_weights
):
    band_count, plane_count, width_y, width_z = wavefunctions.shape
    entry_count, proj_count, tile_len = projectors.shape
    assert (band_count, proj_count, width_y, width_z) == (8, 8, 128, LANES)
    assert entry_count == GROUPS * ATOM_DEV
    grid_rows = (plane_count + 2 * PAD) * (width_y + 2 * PAD) * 8
    block = ((8, LANES), f32)
    blocks = ((4, 8, LANES), f32)
    edge = ((band_count, PAD, width_y, width_z), bf16)

    below, above = call(
        edge_kernel,
        "edges",
        [edge, edge],
        [HBM],
        [VMEM, VMEM],
        [pltpu.SemaphoreType.DMA((2,))],
    )(in_hbm(wavefunctions))
    high_halo = ring(below, "dom", -1)
    low_halo = ring(above, "dom", 1)

    own_index = lax.axis_index("dom").astype(jnp.int32).reshape(1)
    rows, wave, grid, table, low, mid, high = call(
        functools.partial(
            relayout_kernel, width_y=width_y, domain_count=lax.axis_size("dom")
        ),
        "relayout",
        [
            ((entry_count,), jnp.int32),
            (wavefunctions.shape, bf16),
            ((grid_rows, LANES), f32),
            ((GROUPS, LANES, tile_len), bf16),
            block,
            block,
            block,
        ],
        [SMEM, HBM, HBM, HBM, HBM],
        [SMEM] + [VMEM] * 6,
        [
            pltpu.SMEM((entry_count,), jnp.int32),
            pltpu.SMEM((entry_count,), jnp.int32),
            pltpu.SMEM((entry_count,), jnp.int32),
            pltpu.VMEM(projectors.shape, bf16),
            pltpu.VMEM((LANES, tile_len), f32),
            pltpu.SemaphoreType.DMA((plane_count,)),
            pltpu.SemaphoreType.DMA((3,)),
        ],
    )(own_index, *map(in_hbm, (margin_atoms, tile_rows, wavefunctions, projectors)))

    from_above = ring(low, "dom", -1)
    from_below = ring(high, "dom", 1)

    yz_margins, mixing = call(
        functools.partial(gradient_kernel, width_y=width_y),
        "gradient",
        [((2, GROUPS, 8, LANES), f32), ((LANES, LANES), f32)],
        [SMEM] + [VMEM] * 3,
        [VMEM, VMEM],
    )(rows, grid, table, coupling)

    local, token = call(
        local_kernel,
        "local",
        [((plane_count * width_y * 8, LANES), f32), block],
        [VMEM, VMEM],
        [VMEM, VMEM],
    )(wave, potential)

    (scaled,) = call(scale_kernel, "scale", [block], [VMEM] * 4, [VMEM], limit=2)(
        mid, from_above, from_below, mixing
    )
    _, low_sums, mid_sums, high_sums = call(
        functools.partial(first_kernel, width_y=width_y),
        "first",
        [((grid_rows, LANES), f32), blocks, blocks, blocks],
        [SMEM] + [VMEM] * 6,
        [VMEM] * 4,
        input_output_aliases={1: 0},
    )(rows, grid, low_halo, high_halo, table, yz_margins, scaled)
    sums_above = ring(low_sums, "dom", -1)
    sums_below = ring(high_sums, "dom", 1)

    (copies,) = call(
        weigh_kernel,
        "weigh",
        [((lax.axis_size("band"), 3, LANES), f32)],
        [VMEM] * 5,
        [VMEM],
        limit=2,
    )(mid_sums, sums_above, sums_below, band_weights[:, None], token)

    _, applied = call(
        apply_kernel,
        "apply",
        [((plane_count * width_y * 8, LANES), f32), (wavefunctions.shape, bf16)],
        [SMEM] + [VMEM] * 7,
        [VMEM, HBM],
        [
            pltpu.VMEM(wavefunctions.shape, bf16),
            pltpu.SemaphoreType.DMA((plane_count,)),
        ],
        input_output_aliases={1: 0},
    )(rows, local, low_halo, high_halo, table, sums_below, mid_sums, sums_above)

    gathered = lax.all_to_all(copies, "band", 0, 0)
    summed = gathered.sum(0)[:, : ATOM_DEV * proj_count]
    forces = summed.reshape(3, ATOM_DEV, proj_count).sum(2)
    return (applied, forces)


def solution(mesh):
    placed = (
        P("band", "dom", None, None),
        P("dom", None, None),
        P("dom", None, None),
        P("dom"),
        P("dom"),
        P(),
        P("band"),
    )
    return jax.shard_map(
        per_device,
        mesh=mesh,
        in_specs=placed,
        out_specs=(P("band", "dom", None, None), P(None, "dom")),
        check_vma=False,
    )
```

```python
import functools

import jax
import jax.numpy as jnp
from jax import lax
from jax.experimental import pallas as pl
from jax.experimental.pallas import tpu as pltpu
from jax.sharding import PartitionSpec as P

ATOM_DEV = 12
GROUPS = 3
LANES = 128
PAD = 2

f32 = jnp.float32
bf16 = jnp.bfloat16


def ring(x, axis, step):
    count = lax.axis_size(axis)
    return lax.ppermute(x, axis, [(i, (i + step) % count) for i in range(count)])


def plane_to_rows(src, plane, dst, base):
    width_y = src.shape[2]
    for y0 in range(0, width_y, 16):
        for b in range(8):
            dst[pl.ds(base + y0 * 8 + b, 16, stride=8), :] = src[b, plane, y0 : y0 + 16, :].astype(f32)


def at_row(ref, base):
    return ref[pl.ds(pl.multiple_of(base, 8), 8), :]


def diagonal_blocks(product, field):
    lane = lax.broadcasted_iota(jnp.int32, (8, LANES), 1)
    total = jnp.zeros((8, LANES), f32)
    for s in range(ATOM_DEV):
        start = (field * ATOM_DEV + s) * 8
        total = total + jnp.where(
            lax.shift_right_logical(lane, 3) == s, product[start : start + 8, :], 0.0
        )
    return total


def measure(rows_ref, group, table, fields):
    stacked = []
    for field in fields:
        for s in range(ATOM_DEV):
            base = pl.multiple_of(rows_ref[group * ATOM_DEV + s] * 8, 8)
            stacked.append(jnp.concatenate([field(base + k * 8) for k in range(8)], axis=1))
    values = jnp.concatenate(stacked, axis=0).astype(bf16)
    product = lax.dot_general(
        values, table, (((1,), (1,)), ((), ())), preferred_element_type=f32
    )
    return [diagonal_blocks(product, q) for q in range(len(fields))]


def edge_kernel(wave_ref, below_ref, above_ref, sems):
    planes = wave_ref.shape[1]
    copies = [
        pltpu.make_async_copy(wave_ref.at[:, pl.ds(0, PAD)], below_ref, sems.at[0]),
        pltpu.make_async_copy(wave_ref.at[:, pl.ds(planes - PAD, PAD)], above_ref, sems.at[1]),
    ]
    for copy in copies:
        copy.start()
    for copy in copies:
        copy.wait()


def relayout_kernel(
    own_ref,
    atoms_hbm,
    first_rows_hbm,
    wave_hbm,
    proj_hbm,
    rows_ref,
    wave_ref,
    grid_ref,
    table_ref,
    low_ref,
    mid_ref,
    high_ref,
    entry_ref,
    atoms_ref,
    first_rows_ref,
    proj_ref,
    proj_scr,
    wave_sems,
    other_sems,
    *,
    domain_count,
):
    planes, width_y = wave_ref.shape[1:3]
    entry_count = entry_ref.shape[0]

    def plane_copy(plane):
        at_plane = (slice(None), pl.ds(plane, 1))
        return pltpu.make_async_copy(
            wave_hbm.at[at_plane], wave_ref.at[at_plane], wave_sems.at[plane]
        )

    proj_copy = pltpu.make_async_copy(proj_hbm, proj_ref, other_sems.at[0])
    atoms_copy = pltpu.make_async_copy(atoms_hbm, atoms_ref, other_sems.at[1])
    rows_copy = pltpu.make_async_copy(first_rows_hbm, first_rows_ref, other_sems.at[2])
    atoms_copy.start()
    rows_copy.start()
    for plane in range(planes):
        plane_copy(plane).start()
    proj_copy.start()
    atoms_copy.wait()
    rows_copy.wait()

    def place(entry):
        atom = atoms_ref[entry]
        owner = lax.shift_right_logical(atom * 171, 11)
        relative = lax.rem(owner - own_ref[0] + 1 + domain_count, domain_count)
        slot = relative * ATOM_DEV + atom - owner * ATOM_DEV
        entry_ref[slot] = entry
        rows_ref[slot] = first_rows_ref[entry]

    share = -(-entry_count // planes)

    def one_plane(plane, carry):
        plane_copy(plane).wait()
        plane_to_rows(wave_ref, plane, grid_ref, (plane + PAD) * width_y * 8)
        for i in range(share):
            place(jnp.minimum(plane * share + i, entry_count - 1))
        return carry

    lax.fori_loop(0, planes, one_plane, 0)
    proj_copy.wait()
    proj_scr[ATOM_DEV * 8 :, :] = jnp.zeros((LANES - ATOM_DEV * 8, proj_scr.shape[1]), f32)
    for group, margin_ref in enumerate((low_ref, mid_ref, high_ref)):
        for s in range(ATOM_DEV):
            entry = entry_ref[group * ATOM_DEV + s]
            proj_scr[s * 8 : s * 8 + 8, :] = proj_ref[entry].astype(f32)
        table = proj_scr[...].astype(bf16)
        table_ref[group] = table
        (margin_ref[...],) = measure(
            rows_ref, group, table, [lambda base: at_row(grid_ref, base + PAD * width_y * 8)]
        )


def third_shift(center, offset):
    return pltpu.roll(center, (-offset) % center.shape[-1], 1)


def circulant(near, far, center, length):
    row = lax.broadcasted_iota(jnp.int32, (length, length), 0)
    column = lax.broadcasted_iota(jnp.int32, (length, length), 1)
    distance = lax.bitwise_and(row - column, length - 1)
    table = jnp.where((distance == 1) | (distance == length - 1), near, 0.0)
    table = jnp.where((distance == 2) | (distance == length - 2), far, table)
    return jnp.where(distance == 0, center, table).astype(bf16)


def local_kernel(wave_ref, pot_ref, local_hbm, token_ref, local_ref, sems):
    token_ref[...] = jnp.zeros(token_ref.shape, f32)
    bands, planes, width_y, width_z = wave_ref.shape
    along_y = circulant(-16.0, 1.0, 0.0, width_y)
    along_z = circulant(-16.0, 1.0, 90.0, width_z)

    def band_copy(b):
        return pltpu.make_async_copy(local_ref.at[b], local_hbm.at[b], sems.at[b])

    def one_band(b, carry):
        for plane in range(planes):
            wave = wave_ref[b, plane]
            summed = jnp.dot(
                jnp.concatenate([wave, along_y], axis=1),
                jnp.concatenate([along_z, wave], axis=0),
                preferred_element_type=f32,
            )
            for offset, factor in ((1, -16.0), (2, 1.0)):
                sides = [q for q in (plane - offset, plane + offset) if 0 <= q < planes]
                side = wave_ref[b, sides[0]].astype(f32)
                for q in sides[1:]:
                    side = side + wave_ref[b, q].astype(f32)
                summed = summed + (side if factor == 1.0 else factor * side)
            local_ref[b, plane] = summed * (1.0 / 24.0) + pot_ref[plane] * wave.astype(f32)
        band_copy(b).start()
        return carry

    lax.fori_loop(0, bands, one_band, 0)
    for b in range(bands):
        band_copy(b).wait()


def gradient_kernel(
    rows_ref,
    grid_ref,
    table_ref,
    coupling_ref,
    weight_ref,
    margin_ref,
    mixing_ref,
    factor_ref,
    y_ref,
):
    width_y = LANES
    edge = PAD * width_y * 8
    planes = y_ref.shape[0] // (width_y * 8)

    def one_plane(plane, carry):
        base = pl.multiple_of(plane * width_y * 8, 8)
        row = [at_row(grid_ref, base + edge + (y % width_y) * 8) for y in range(-2, 2)]
        for y in range(width_y):
            row.append(at_row(grid_ref, base + edge + ((y + 2) % width_y) * 8))
            near = row[y + 3] - row[y + 1]
            far = row[y + 4] - row[y]
            y_ref[pl.ds(base + y * 8, 8), :] = (2.0 / 3.0) * near - (1.0 / 12.0) * far
        return carry

    lax.fori_loop(0, planes, one_plane, 0)

    def along_y(base):
        return at_row(y_ref, base)

    def along_z(base):
        center = at_row(grid_ref, base + edge)
        near = third_shift(center, 1) - third_shift(center, -1)
        far = third_shift(center, 2) - third_shift(center, -2)
        return (2.0 / 3.0) * near - (1.0 / 12.0) * far

    for group in range(GROUPS):
        second, third = measure(rows_ref, group, table_ref[group], [along_y, along_z])
        margin_ref[0, group] = second
        margin_ref[1, group] = third

    bands = weight_ref.shape[1]
    band = lax.broadcasted_iota(jnp.int32, (bands, bands), 0)
    other = lax.broadcasted_iota(jnp.int32, (bands, bands), 1)
    weights = jnp.broadcast_to(weight_ref[...], (bands, bands))
    column = jnp.sum(jnp.where(band == other, weights, 0.0), axis=1, keepdims=True)
    factor_ref[...] = jnp.broadcast_to(-2.0 * column, factor_ref.shape)

    proj_count = coupling_ref.shape[0]
    symmetric = 0.5 * (coupling_ref[...] + coupling_ref[...].T)
    index = lax.broadcasted_iota(jnp.int32, (proj_count, LANES), 0)
    lane = lax.broadcasted_iota(jnp.int32, (proj_count, LANES), 1)
    spread = (lax.bitwise_and(lane, proj_count - 1) == index).astype(f32)
    tiled = jnp.dot(
        symmetric, spread, precision=lax.Precision.HIGHEST, preferred_element_type=f32
    )
    for a in range(LANES // proj_count):
        keep = (lax.shift_right_logical(lane, 3) == a) & (lane < ATOM_DEV * proj_count)
        mixing_ref[a * proj_count : (a + 1) * proj_count, :] = jnp.where(keep, tiled, 0.0)


def first_kernel(
    rows_ref,
    grid_in,
    low_ref,
    high_ref,
    table_ref,
    yz_ref,
    scaled_ref,
    grid_ref,
    low_out,
    mid_out,
    high_out,
):
    del grid_in
    width_y = low_ref.shape[2]
    hop = width_y * 8
    planes = grid_ref.shape[0] // hop - 2 * PAD

    for index in range(PAD):
        plane_to_rows(low_ref, index, grid_ref, index * hop)
        plane_to_rows(high_ref, index, grid_ref, (planes + PAD + index) * hop)

    def along_x(base):
        near = at_row(grid_ref, base + 3 * hop) - at_row(grid_ref, base + hop)
        far = at_row(grid_ref, base + 4 * hop) - at_row(grid_ref, base)
        return (2.0 / 3.0) * near - (1.0 / 12.0) * far

    for group, margin_ref in enumerate((low_out, mid_out, high_out)):
        (first,) = measure(rows_ref, group, table_ref[group], [along_x])
        margin_ref[0] = first
        margin_ref[1] = yz_ref[0, group]
        margin_ref[2] = yz_ref[1, group]
        margin_ref[3] = scaled_ref[...]


def apply_kernel(
    rows_ref,
    local_hbm,
    low_ref,
    high_ref,
    table_ref,
    scaled_low_ref,
    scaled_ref,
    scaled_high_ref,
    out_hbm,
    out_ref,
    add_ref,
    local_ref,
    sems,
):
    bands, planes, width_y, _ = out_ref.shape
    lane = lax.broadcasted_iota(jnp.int32, (8, LANES), 1)

    def local_copy(plane):
        at_plane = (slice(None), pl.ds(plane, 1))
        return pltpu.make_async_copy(
            local_hbm.at[at_plane], local_ref.at[at_plane], sems.at[0, plane]
        )

    for plane in range(planes):
        local_copy(plane).start()

    def clear(plane, carry):
        size = width_y * 8
        add_ref[pl.ds(pl.multiple_of(plane * size, size), size), :] = jnp.zeros((size, LANES), f32)
        return carry

    lax.fori_loop(0, planes, clear, 0)

    for group, source in enumerate((scaled_low_ref, scaled_ref, scaled_high_ref)):
        scaled = source[3]
        blocks = [
            jnp.where(lax.shift_right_logical(lane, 3) == s, scaled, 0.0)
            for s in range(ATOM_DEV)
        ]
        coef = jnp.concatenate(blocks, axis=0).astype(bf16)
        terms = jnp.dot(coef, table_ref[group], preferred_element_type=f32)
        for s in range(ATOM_DEV):
            base = pl.multiple_of(rows_ref[group * ATOM_DEV + s] * 8, 8)
            for k in range(8):
                where = pl.ds(base + k * 8, 8)
                add_ref[where, :] = (
                    add_ref[where, :] + terms[s * 8 : s * 8 + 8, k * LANES : (k + 1) * LANES]
                )

    def plane_copy(plane):
        at_plane = (slice(None), pl.ds(plane, 1))
        return pltpu.make_async_copy(out_ref.at[at_plane], out_hbm.at[at_plane], sems.at[1, plane])

    near, far = -2.0 / 3.0, 1.0 / 24.0
    halo_terms = {
        0: ((low_ref, 1, near), (low_ref, 0, far)),
        1: ((low_ref, 1, far),),
        planes - 2: ((high_ref, 0, far),),
        planes - 1: ((high_ref, 0, near), (high_ref, 1, far)),
    }
    def finish(plane, terms):
        local_copy(plane).wait()
        base = plane * width_y * 8
        for y0 in range(0, width_y, 16):
            for b in range(bands):
                value = add_ref[pl.ds(base + y0 * 8 + b, 16, stride=8), :]
                value = value + local_ref[b, plane, y0 : y0 + 16, :]
                for ref, index, factor in terms:
                    value = value + factor * ref[b, index, y0 : y0 + 16, :].astype(f32)
                out_ref[b, plane, y0 : y0 + 16, :] = value.astype(bf16)
        plane_copy(plane).start()

    def inner(plane, carry):
        finish(plane, ())
        return carry

    lax.fori_loop(PAD, planes - PAD, inner, 0)
    for plane, terms in halo_terms.items():
        finish(plane, terms)
    for plane in range(planes):
        plane_copy(plane).wait()


def weigh_kernel(own_ref, above_ref, below_ref, factor_ref, _, copies_ref):
    weighted = factor_ref[...] * own_ref[3]
    parts = []
    for k in range(3):
        total = own_ref[k] + above_ref[k] + below_ref[k]
        parts.append(jnp.sum(total * weighted, axis=0, keepdims=True))
    parts = jnp.concatenate(parts, axis=0)
    for copy in range(copies_ref.shape[0]):
        copies_ref[copy] = parts


def scale_kernel(own_ref, above_ref, below_ref, mixing_ref, scaled_ref):
    total = own_ref[...] + above_ref[...] + below_ref[...]
    scaled_ref[...] = jnp.dot(
        total, mixing_ref[...], precision=lax.Precision.HIGHEST, preferred_element_type=f32
    )


VMEM = pl.BlockSpec(memory_space=pltpu.VMEM)
SMEM = pl.BlockSpec(memory_space=pltpu.SMEM)
HBM = pl.BlockSpec(memory_space=pltpu.HBM)
MIB = 2**20


def in_hbm(x):
    return pltpu.with_memory_space_constraint(x, pltpu.HBM)


def call(kernel, name, outs, ins, out_specs, scratch=(), limit=8, **kwargs):
    return pl.pallas_call(
        kernel,
        out_shape=tuple(
            pltpu.HBM(shape, dtype) if spec is HBM else jax.ShapeDtypeStruct(shape, dtype)
            for (shape, dtype), spec in zip(outs, out_specs)
        ),
        in_specs=ins,
        out_specs=tuple(out_specs),
        scratch_shapes=list(scratch),
        compiler_params=pltpu.CompilerParams(vmem_limit_bytes=limit * MIB),
        cost_estimate=pl.CostEstimate(flops=1000, bytes_accessed=1000, transcendentals=0),
        name=name,
        **kwargs,
    )


def per_device(
    wavefunctions, potential, projectors, margin_atoms, tile_rows, coupling, band_weights
):
    band_count, plane_count, width_y, width_z = wavefunctions.shape
    entry_count, proj_count, tile_len = projectors.shape
    assert (band_count, proj_count, width_y, width_z) == (8, 8, 128, LANES)
    assert entry_count == GROUPS * ATOM_DEV
    grid_rows = (plane_count + 2 * PAD) * width_y * 8
    block = ((8, LANES), f32)
    blocks = ((4, 8, LANES), f32)
    edge = ((band_count, PAD, width_y, width_z), bf16)

    below, above = call(
        edge_kernel,
        "edges",
        [edge, edge],
        [HBM],
        [VMEM, VMEM],
        [pltpu.SemaphoreType.DMA((2,))],
    )(in_hbm(wavefunctions))
    high_halo = ring(below, "dom", -1)
    low_halo = ring(above, "dom", 1)

    own_index = lax.axis_index("dom").astype(jnp.int32).reshape(1)
    rows, wave, grid, table, low, mid, high = call(
        functools.partial(relayout_kernel, domain_count=lax.axis_size("dom")),
        "relayout",
        [
            ((entry_count,), jnp.int32),
            (wavefunctions.shape, bf16),
            ((grid_rows, LANES), f32),
            ((GROUPS, LANES, tile_len), bf16),
            block,
            block,
            block,
        ],
        [SMEM, HBM, HBM, HBM, HBM],
        [SMEM] + [VMEM] * 6,
        [
            pltpu.SMEM((entry_count,), jnp.int32),
            pltpu.SMEM((entry_count,), jnp.int32),
            pltpu.SMEM((entry_count,), jnp.int32),
            pltpu.VMEM(projectors.shape, bf16),
            pltpu.VMEM((LANES, tile_len), f32),
            pltpu.SemaphoreType.DMA((plane_count,)),
            pltpu.SemaphoreType.DMA((3,)),
        ],
    )(own_index, *map(in_hbm, (margin_atoms, tile_rows, wavefunctions, projectors)))

    from_above = ring(low, "dom", -1)
    from_below = ring(high, "dom", 1)

    yz_margins, mixing, factor = call(
        gradient_kernel,
        "gradient",
        [((2, GROUPS, 8, LANES), f32), ((LANES, LANES), f32), block],
        [SMEM] + [VMEM] * 4,
        [VMEM] * 3,
        [pltpu.VMEM((plane_count * width_y * 8, LANES), f32)],
    )(rows, grid, table, coupling, band_weights[None, :])

    local, token = call(
        local_kernel,
        "local",
        [(wavefunctions.shape, f32), block],
        [VMEM, VMEM],
        [HBM, VMEM],
        [pltpu.VMEM(wavefunctions.shape, f32), pltpu.SemaphoreType.DMA((band_count,))],

    )(wave, potential)

    (scaled,) = call(scale_kernel, "scale", [block], [VMEM] * 4, [VMEM], limit=2)(
        mid, from_above, from_below, mixing
    )
    _, low_sums, mid_sums, high_sums = call(
        first_kernel,
        "first",
        [((grid_rows, LANES), f32), blocks, blocks, blocks],
        [SMEM] + [VMEM] * 6,
        [VMEM] * 4,
        input_output_aliases={1: 0},
    )(rows, grid, low_halo, high_halo, table, yz_margins, scaled)
    sums_above = ring(low_sums, "dom", -1)
    sums_below = ring(high_sums, "dom", 1)

    (copies,) = call(
        weigh_kernel,
        "weigh",
        [((lax.axis_size("band"), 3, LANES), f32)],
        [VMEM] * 5,
        [VMEM],
        limit=2,
    )(mid_sums, sums_above, sums_below, factor, token)

    (applied,) = call(
        apply_kernel,
        "apply",
        [(wavefunctions.shape, bf16)],
        [SMEM, HBM] + [VMEM] * 6,
        [HBM],
        [
            pltpu.VMEM(wavefunctions.shape, bf16),
            pltpu.VMEM((plane_count * width_y * 8, LANES), f32),
            pltpu.VMEM(wavefunctions.shape, f32),
            pltpu.SemaphoreType.DMA((2, plane_count)),
        ],
        limit=16,
    )(rows, in_hbm(local), low_halo, high_halo, table, sums_below, mid_sums, sums_above)

    gathered = lax.all_to_all(copies, "band", 0, 0)
    summed = gathered.sum(0)[:, : ATOM_DEV * proj_count]
    forces = summed.reshape(3, ATOM_DEV, proj_count).sum(2)
    return (applied, forces)


def solution(mesh):
    placed = (
        P("band", "dom", None, None),
        P("dom", None, None),
        P("dom", None, None),
        P("dom"),
        P("dom"),
        P(),
        P("band"),
    )
    return jax.shard_map(
        per_device,
        mesh=mesh,
        in_specs=placed,
        out_specs=(P("band", "dom", None, None), P(None, "dom")),
        check_vma=False,
    )
```

```python
import functools

import jax
import jax.numpy as jnp
from jax import lax
from jax.experimental import pallas as pl
from jax.experimental.pallas import tpu as pltpu
from jax.sharding import PartitionSpec as P

ATOM_DEV = 12
GROUPS = 3
LANES = 128
PAD = 2

f32 = jnp.float32
bf16 = jnp.bfloat16


def partner_a(i):
    return i ^ 1


def partner_b(i, count):
    return (i + 1 if i % 2 else i - 1) % count


def swap_a(x):
    return lax.ppermute(x, "dom", [(i, partner_a(i)) for i in range(lax.axis_size("dom"))])


def swap_b(x):
    count = lax.axis_size("dom")
    return lax.ppermute(x, "dom", [(i, partner_b(i, count)) for i in range(count)])


def send_c(x):
    count = lax.axis_size("dom")
    return lax.ppermute(x, "dom", [(i, partner_a(partner_b(i, count))) for i in range(count)])


def own_domain():
    index = lax.axis_index("dom")
    return index, lax.bitwise_and(index, 1)


def plane_to_rows(src, plane, dst, base):
    width_y = src.shape[2]
    for y0 in range(0, width_y, 16):
        for b in range(8):
            dst[pl.ds(base + y0 * 8 + b, 16, stride=8), :] = src[b, plane, y0 : y0 + 16, :].astype(f32)


def at_row(ref, base):
    return ref[pl.ds(pl.multiple_of(base, 8), 8), :]


def diagonal_blocks(product, field):
    lane = lax.broadcasted_iota(jnp.int32, (8, LANES), 1)
    total = jnp.zeros((8, LANES), f32)
    for s in range(ATOM_DEV):
        start = (field * ATOM_DEV + s) * 8
        total = total + jnp.where(
            lax.shift_right_logical(lane, 3) == s, product[start : start + 8, :], 0.0
        )
    return total


def measure(rows_ref, group, table, fields):
    stacked = []
    for field in fields:
        for s in range(ATOM_DEV):
            base = pl.multiple_of(rows_ref[group * ATOM_DEV + s] * 8, 8)
            stacked.append(jnp.concatenate([field(base + k * 8) for k in range(8)], axis=1))
    values = jnp.concatenate(stacked, axis=0).astype(bf16)
    product = lax.dot_general(
        values, table, (((1,), (1,)), ((), ())), preferred_element_type=f32
    )
    return [diagonal_blocks(product, q) for q in range(len(fields))]


def start_rows(rows_in, rows_ref, sem):
    copy = pltpu.make_async_copy(rows_in, rows_ref, sem)
    copy.start()
    return copy


def edge_kernel(wave_ref, to_a_ref, to_b_ref, sems):
    planes = wave_ref.shape[1]
    _, odd = own_domain()
    upper = planes - PAD
    copies = [
        start_rows(wave_ref.at[:, pl.ds(upper * (1 - odd), PAD)], to_a_ref, sems.at[0]),
        start_rows(wave_ref.at[:, pl.ds(upper * odd, PAD)], to_b_ref, sems.at[1]),
    ]
    for copy in copies:
        copy.wait()


def relayout_kernel(
    atoms_hbm,
    first_rows_hbm,
    wave_hbm,
    proj_hbm,
    rows_out,
    grid_ref,
    table_ref,
    margin_ref,
    to_a_ref,
    to_c_ref,
    wave_ref,
    atoms_ref,
    first_rows_ref,
    rows_ref,
    entry_ref,
    proj_ref,
    proj_scr,
    wave_sems,
    other_sems,
    *,
    domain_count,
):
    planes, width_y = wave_ref.shape[1:3]
    entry_count = rows_ref.shape[0]
    index, odd = own_domain()

    def plane_copy(plane):
        at_plane = (slice(None), pl.ds(plane, 1))
        return pltpu.make_async_copy(
            wave_hbm.at[at_plane], wave_ref.at[at_plane], wave_sems.at[plane]
        )

    atoms_copy = start_rows(atoms_hbm, atoms_ref, other_sems.at[0])
    first_copy = start_rows(first_rows_hbm, first_rows_ref, other_sems.at[1])
    for plane in range(planes):
        plane_copy(plane).start()
    proj_copy = start_rows(proj_hbm, proj_ref, other_sems.at[2])
    proj_scr[:, ATOM_DEV * 8 :, :] = jnp.zeros(
        (GROUPS, LANES - ATOM_DEV * 8, proj_scr.shape[2]), f32
    )
    atoms_copy.wait()
    first_copy.wait()
    for entry in range(entry_count):
        atom = atoms_ref[entry]
        owner = lax.shift_right_logical(atom * 171, 11)
        above = lax.rem(owner - index + 1 + domain_count, domain_count)
        group = jnp.where(odd == 1, above, 2 - above)
        slot = group * ATOM_DEV + atom - owner * ATOM_DEV
        entry_ref[slot] = entry
        rows_ref[slot] = first_rows_ref[entry]
    rows_copy = start_rows(rows_ref, rows_out, other_sems.at[3])

    def one_plane(plane, carry):
        plane_copy(plane).wait()
        plane_to_rows(wave_ref, plane, grid_ref, (plane + PAD) * width_y * 8)
        return carry

    lax.fori_loop(0, planes, one_plane, 0)
    proj_copy.wait()
    for group in range(GROUPS):
        for s in range(ATOM_DEV):
            entry = entry_ref[group * ATOM_DEV + s]
            proj_scr[group, s * 8 : s * 8 + 8, :] = proj_ref[entry].astype(f32)
        table = proj_scr[group].astype(bf16)
        table_ref[group] = table
        (sums,) = measure(
            rows_ref,
            group,
            table,
            [lambda base: at_row(grid_ref, base + PAD * width_y * 8)],
        )
        margin_ref[group] = sums
        if group < 2:
            to_a_ref[group] = sums
        else:
            to_c_ref[...] = sums
    rows_copy.wait()


def forward_kernel(margin_ref, from_a_ref, to_b_ref):
    to_b_ref[0] = margin_ref[2]
    to_b_ref[1] = margin_ref[1] + from_a_ref[0]


def third_shift(center, offset):
    return pltpu.roll(center, (-offset) % center.shape[-1], 1)


def circulant(near, far, center, length):
    row = lax.broadcasted_iota(jnp.int32, (length, length), 0)
    column = lax.broadcasted_iota(jnp.int32, (length, length), 1)
    distance = lax.bitwise_and(row - column, length - 1)
    table = jnp.where((distance == 1) | (distance == length - 1), near, 0.0)
    table = jnp.where((distance == 2) | (distance == length - 2), far, table)
    return jnp.where(distance == 0, center, table).astype(bf16)


def gradient_kernel(
    rows_in,
    grid_in,
    halo_a_ref,
    table_ref,
    coupling_hbm,
    weight_hbm,
    _,
    grid_ref,
    margin_ref,
    mixing_ref,
    factor_ref,
    y_ref,
    rows_ref,
    coupling_ref,
    weight_ref,
    sems,
):
    del grid_in
    copies = [
        start_rows(rows_in, rows_ref, sems.at[0]),
        start_rows(coupling_hbm, coupling_ref, sems.at[1]),
        start_rows(weight_hbm, weight_ref, sems.at[2]),
    ]
    width_y = LANES
    edge = PAD * width_y * 8
    planes = y_ref.shape[0] // (width_y * 8)

    def one_plane(plane, carry):
        base = pl.multiple_of(plane * width_y * 8, 8)
        row = [at_row(grid_ref, base + edge + (y % width_y) * 8) for y in range(-2, 2)]
        for y in range(width_y):
            row.append(at_row(grid_ref, base + edge + ((y + 2) % width_y) * 8))
            near = row[y + 3] - row[y + 1]
            far = row[y + 4] - row[y]
            y_ref[pl.ds(base + y * 8, 8), :] = (2.0 / 3.0) * near - (1.0 / 12.0) * far
        return carry

    lax.fori_loop(0, planes, one_plane, 0)

    def along_y(base):
        return at_row(y_ref, base)

    def along_z(base):
        center = at_row(grid_ref, base + edge)
        near = third_shift(center, 1) - third_shift(center, -1)
        far = third_shift(center, 2) - third_shift(center, -2)
        return (2.0 / 3.0) * near - (1.0 / 12.0) * far

    _, odd = own_domain()
    for i in range(PAD):
        plane = i + (planes + PAD) * (1 - odd)
        plane_to_rows(halo_a_ref, i, grid_ref, plane * width_y * 8)

    for copy in copies:
        copy.wait()
    for group in range(GROUPS):
        second, third = measure(rows_ref, group, table_ref[group], [along_y, along_z])
        margin_ref[0, group] = second
        margin_ref[1, group] = third

    bands = weight_ref.shape[1]
    band = lax.broadcasted_iota(jnp.int32, (bands, bands), 0)
    other = lax.broadcasted_iota(jnp.int32, (bands, bands), 1)
    weights = jnp.broadcast_to(weight_ref[...], (bands, bands))
    column = jnp.sum(jnp.where(band == other, weights, 0.0), axis=1, keepdims=True)
    factor_ref[...] = jnp.broadcast_to(-2.0 * column, factor_ref.shape)

    proj_count = coupling_ref.shape[0]
    symmetric = 0.5 * (coupling_ref[...] + coupling_ref[...].T)
    index = lax.broadcasted_iota(jnp.int32, (proj_count, LANES), 0)
    lane = lax.broadcasted_iota(jnp.int32, (proj_count, LANES), 1)
    spread = (lax.bitwise_and(lane, proj_count - 1) == index).astype(f32)
    tiled = jnp.dot(
        symmetric, spread, precision=lax.Precision.HIGHEST, preferred_element_type=f32
    )
    for a in range(LANES // proj_count):
        keep = (lax.shift_right_logical(lane, 3) == a) & (lane < ATOM_DEV * proj_count)
        mixing_ref[a * proj_count : (a + 1) * proj_count, :] = jnp.where(keep, tiled, 0.0)


def first_kernel(
    rows_in,
    grid_in,
    halo_b_ref,
    table_ref,
    yz_ref,
    grid_ref,
    force_ref,
    rows_ref,
    rows_sem,
):
    del grid_in
    rows_copy = start_rows(rows_in, rows_ref, rows_sem)
    width_y = halo_b_ref.shape[2]
    hop = width_y * 8
    planes = grid_ref.shape[0] // hop - 2 * PAD
    _, odd = own_domain()

    for i in range(PAD):
        plane_to_rows(halo_b_ref, i, grid_ref, (i + (planes + PAD) * odd) * hop)

    def along_x(base):
        near = at_row(grid_ref, base + 3 * hop) - at_row(grid_ref, base + hop)
        far = at_row(grid_ref, base + 4 * hop) - at_row(grid_ref, base)
        return (2.0 / 3.0) * near - (1.0 / 12.0) * far

    rows_copy.wait()
    for group in range(GROUPS):
        (first,) = measure(rows_ref, group, table_ref[group], [along_x])
        force_ref[group, 0] = first
        force_ref[group, 1] = yz_ref[0, group]
        force_ref[group, 2] = yz_ref[1, group]


def combine_kernel(
    margin_ref,
    from_a_ref,
    from_b_ref,
    from_c_ref,
    mixing_ref,
    factor_ref,
    force_ref,
    scaled_ref,
    copies_ref,
    *,
    domain_count,
):
    totals = jnp.concatenate(
        [
            margin_ref[0] + from_a_ref[1] + from_c_ref[...],
            margin_ref[1] + from_a_ref[0] + from_b_ref[0],
            margin_ref[2] + from_b_ref[1],
        ],
        axis=0,
    )
    scaled = jnp.dot(
        totals, mixing_ref[...], precision=lax.Precision.HIGHEST, preferred_element_type=f32
    )
    parts = []
    for group in range(GROUPS):
        one = scaled[group * 8 : group * 8 + 8]
        scaled_ref[group] = one
        weighted = factor_ref[...] * one
        for k in range(3):
            parts.append(jnp.sum(force_ref[group, k] * weighted, axis=0, keepdims=True))
    summed = jnp.concatenate(parts, axis=0)
    for step in (1, 2, 4):
        summed = summed + pltpu.roll(summed, LANES - step, 1)
    component = lax.bitwise_and(lax.broadcasted_iota(jnp.int32, (1, LANES), 1), 7)
    copies_ref[...] = jnp.zeros(copies_ref.shape, f32)
    bands = copies_ref.shape[0] // domain_count
    index, odd = own_domain()
    owners = (
        index + 1 - 2 * odd,
        index,
        lax.rem(index - 1 + 2 * odd + domain_count, domain_count),
    )
    for group, owner in enumerate(owners):
        row = jnp.zeros((1, LANES), f32)
        for k in range(3):
            value = summed[group * 3 + k : group * 3 + k + 1]
            value = pltpu.roll(value, k, 1) if k else value
            row = row + jnp.where(component == k, value, 0.0)
        for b in range(bands):
            copies_ref[owner * bands + b] = row


def total_kernel(gathered_ref, forces_ref):
    atoms = forces_ref.shape[1]
    row = jnp.sum(jnp.sum(gathered_ref[...], axis=0), axis=0, keepdims=True)
    lane = lax.broadcasted_iota(jnp.int32, (8, LANES), 1)
    component = lax.broadcasted_iota(jnp.int32, (8, LANES), 0)
    split = jnp.where(lax.bitwise_and(lane, 7) == component, row, 0.0)
    source = lax.broadcasted_iota(jnp.int32, (LANES, LANES), 0)
    target = lax.broadcasted_iota(jnp.int32, (LANES, LANES), 1)
    collect = (lax.shift_right_logical(source, 3) == target).astype(f32)
    forces = jnp.dot(
        split, collect, precision=lax.Precision.HIGHEST, preferred_element_type=f32
    )
    forces_ref[...] = forces[:3, :atoms]


def apply_kernel(
    rows_in,
    wave_hbm,
    pot_hbm,
    halo_a_ref,
    halo_b_ref,
    table_ref,
    scaled_ref,
    out_hbm,
    out_ref,
    add_ref,
    wave_ref,
    pot_ref,
    rows_ref,
    sems,
    edge_sems,
):
    bands, planes, width_y, width_z = out_ref.shape
    lane = lax.broadcasted_iota(jnp.int32, (8, LANES), 1)

    def wave_copy(plane):
        return pltpu.make_async_copy(
            wave_hbm.at[:, pl.ds(plane, 1)],
            wave_ref.at[:, pl.ds(plane + PAD, 1)],
            sems.at[0, plane],
        )

    def out_copy(plane):
        at_plane = (slice(None), pl.ds(plane, 1))
        return pltpu.make_async_copy(
            out_ref.at[at_plane], out_hbm.at[at_plane], sems.at[1, plane]
        )

    rows_copy = start_rows(rows_in, rows_ref, edge_sems.at[0])
    _, odd = own_domain()
    far_end = planes + PAD
    edge_copies = [
        start_rows(halo_a_ref, wave_ref.at[:, pl.ds(far_end * (1 - odd), PAD)], edge_sems.at[1]),
        start_rows(halo_b_ref, wave_ref.at[:, pl.ds(far_end * odd, PAD)], edge_sems.at[2]),
        start_rows(pot_hbm, pot_ref, edge_sems.at[3]),
    ]
    for plane in range(planes):
        wave_copy(plane).start()

    def clear(plane, carry):
        size = width_y * 8
        add_ref[pl.ds(pl.multiple_of(plane * size, size), size), :] = jnp.zeros((size, LANES), f32)
        return carry

    lax.fori_loop(0, planes, clear, 0)
    rows_copy.wait()

    for group in range(GROUPS):
        scaled = scaled_ref[group]
        blocks = [
            jnp.where(lax.shift_right_logical(lane, 3) == s, scaled, 0.0)
            for s in range(ATOM_DEV)
        ]
        coef = jnp.concatenate(blocks, axis=0).astype(bf16)
        terms = jnp.dot(coef, table_ref[group], preferred_element_type=f32)
        for s in range(ATOM_DEV):
            base = pl.multiple_of(rows_ref[group * ATOM_DEV + s] * 8, 8)
            for k in range(8):
                where = pl.ds(base + k * 8, 8)
                add_ref[where, :] = (
                    add_ref[where, :] + terms[s * 8 : s * 8 + 8, k * LANES : (k + 1) * LANES]
                )

    along_y = circulant(-16.0, 1.0, 0.0, width_y)
    along_z = circulant(-16.0, 1.0, 90.0, width_z)
    for copy in edge_copies:
        copy.wait()
    for plane in range(PAD):
        wave_copy(plane).wait()

    def finish(plane, carry):
        @pl.when(plane + PAD < planes)
        def _():
            wave_copy(plane + PAD).wait()

        for b in range(bands):
            wave = wave_ref[b, plane + PAD]
            summed = jnp.dot(
                jnp.concatenate([wave, along_y], axis=1),
                jnp.concatenate([along_z, wave], axis=0),
                preferred_element_type=f32,
            )
            near = wave_ref[b, plane + 1].astype(f32) + wave_ref[b, plane + 3].astype(f32)
            far = wave_ref[b, plane].astype(f32) + wave_ref[b, plane + 4].astype(f32)
            value = (summed + far - 16.0 * near) * (1.0 / 24.0)
            value = value + pot_ref[plane] * wave.astype(f32)
            added = add_ref[pl.ds(plane * width_y * 8 + b, width_y, stride=8), :]
            out_ref[b, plane] = (value + added).astype(bf16)
        out_copy(plane).start()
        return carry

    lax.fori_loop(0, planes, finish, 0)
    for plane in range(planes):
        out_copy(plane).wait()


VMEM = pl.BlockSpec(memory_space=pltpu.VMEM)
SMEM = pl.BlockSpec(memory_space=pltpu.SMEM)
HBM = pl.BlockSpec(memory_space=pltpu.HBM)
ANY = pl.BlockSpec(memory_space=pl.ANY)
MIB = 2**20


def in_hbm(x):
    return pltpu.with_memory_space_constraint(x, pltpu.HBM)


def call(kernel, name, outs, ins, out_specs, scratch=(), limit=8, **kwargs):
    return pl.pallas_call(
        kernel,
        out_shape=tuple(
            pltpu.HBM(shape, dtype) if spec is HBM else jax.ShapeDtypeStruct(shape, dtype)
            for (shape, dtype), spec in zip(outs, out_specs)
        ),
        in_specs=ins,
        out_specs=tuple(out_specs),
        scratch_shapes=list(scratch),
        compiler_params=pltpu.CompilerParams(vmem_limit_bytes=limit * MIB),
        cost_estimate=pl.CostEstimate(flops=1000, bytes_accessed=1000, transcendentals=0),
        name=name,
        **kwargs,
    )


def per_device(
    wavefunctions, potential, projectors, margin_atoms, tile_rows, coupling, band_weights
):
    band_count, plane_count, width_y, width_z = wavefunctions.shape
    entry_count, proj_count, tile_len = projectors.shape
    assert (band_count, proj_count, width_y, width_z) == (8, 8, 128, LANES)
    assert entry_count == GROUPS * ATOM_DEV
    grid_rows = (plane_count + 2 * PAD) * width_y * 8
    domain_count = lax.axis_size("dom")
    block = ((8, LANES), f32)
    pair = ((2, 8, LANES), f32)
    blocks = ((GROUPS, 8, LANES), f32)
    edge = ((band_count, PAD, width_y, width_z), bf16)
    slots = ((entry_count,), jnp.int32)
    slots_smem = pltpu.SMEM((entry_count,), jnp.int32)

    to_a, to_b = call(
        edge_kernel,
        "edges",
        [edge, edge],
        [HBM],
        [VMEM, VMEM],
        [pltpu.SemaphoreType.DMA((2,))],
    )(in_hbm(wavefunctions))
    halo_a = swap_a(to_a)
    halo_b = swap_b(to_b)

    rows, grid, table, margins, margins_to_a, margins_to_c = call(
        functools.partial(relayout_kernel, domain_count=domain_count),
        "relayout",
        [
            slots,
            ((grid_rows, LANES), f32),
            ((GROUPS, LANES, tile_len), bf16),
            blocks,
            pair,
            block,
        ],
        [HBM] * 4,
        [ANY] + [VMEM] * 5,
        [
            pltpu.VMEM(wavefunctions.shape, bf16),
            slots_smem,
            slots_smem,
            slots_smem,
            slots_smem,
            pltpu.VMEM(projectors.shape, bf16),
            pltpu.VMEM((GROUPS, LANES, tile_len), f32),
            pltpu.SemaphoreType.DMA((plane_count,)),
            pltpu.SemaphoreType.DMA((4,)),
        ],
    )(*map(in_hbm, (margin_atoms, tile_rows, wavefunctions, projectors)))

    from_a = swap_a(margins_to_a)
    from_c = send_c(margins_to_c)
    (margins_to_b,) = call(forward_kernel, "forward", [pair], [VMEM] * 2, [VMEM], limit=2)(
        margins, from_a
    )
    from_b = swap_b(margins_to_b)

    grid, yz_margins, mixing, factor = call(
        gradient_kernel,
        "gradient",
        [
            ((grid_rows, LANES), f32),
            ((2, GROUPS, 8, LANES), f32),
            ((LANES, LANES), f32),
            block,
        ],
        [ANY] + [VMEM] * 3 + [HBM] * 2 + [VMEM],
        [VMEM] * 4,
        [
            pltpu.VMEM((plane_count * width_y * 8, LANES), f32),
            slots_smem,
            pltpu.VMEM(coupling.shape, f32),
            pltpu.VMEM((1, band_count), f32),
            pltpu.SemaphoreType.DMA((3,)),
        ],
        input_output_aliases={1: 0},
    )(
        rows,
        grid,
        halo_a,
        table,
        in_hbm(coupling),
        in_hbm(band_weights[None, :]),
        margins_to_b,
    )

    _, force_margins = call(
        first_kernel,
        "first",
        [((grid_rows, LANES), f32), ((GROUPS, 3, 8, LANES), f32)],
        [ANY] + [VMEM] * 4,
        [VMEM] * 2,
        [slots_smem, pltpu.SemaphoreType.DMA],
        input_output_aliases={1: 0},
    )(rows, grid, halo_b, table, yz_margins)

    device_count = domain_count * lax.axis_size("band")
    scaled, copies = call(
        functools.partial(combine_kernel, domain_count=domain_count),
        "combine",
        [blocks, ((device_count, 1, LANES), f32)],
        [VMEM] * 7,
        [VMEM] * 2,
        limit=2,
    )(margins, from_a, from_b, from_c, mixing, factor, force_margins)
    gathered = lax.all_to_all(copies, ("dom", "band"), 0, 0)

    (applied,) = call(
        apply_kernel,
        "apply",
        [(wavefunctions.shape, bf16)],
        [ANY, HBM, HBM] + [VMEM] * 4,
        [HBM],
        [
            pltpu.VMEM(wavefunctions.shape, bf16),
            pltpu.VMEM((plane_count * width_y * 8, LANES), f32),
            pltpu.VMEM((band_count, plane_count + 2 * PAD, width_y, width_z), bf16),
            pltpu.VMEM(potential.shape, f32),
            slots_smem,
            pltpu.SemaphoreType.DMA((2, plane_count)),
            pltpu.SemaphoreType.DMA((4,)),
        ],
        limit=16,
    )(rows, in_hbm(wavefunctions), in_hbm(potential), halo_a, halo_b, table, scaled)

    (forces,) = call(
        total_kernel, "total", [((3, ATOM_DEV), f32)], [VMEM], [VMEM], limit=2
    )(gathered.reshape(device_count // 8, 8, LANES))
    return (applied, forces)


def solution(mesh):
    placed = (
        P("band", "dom", None, None),
        P("dom", None, None),
        P("dom", None, None),
        P("dom"),
        P("dom"),
        P(),
        P("band"),
    )
    return jax.shard_map(
        per_device,
        mesh=mesh,
        in_specs=placed,
        out_specs=(P("band", "dom", None, None), P(None, "dom")),
        check_vma=False,
    )
```

```python
import functools

import jax
import jax.numpy as jnp
from jax import lax
from jax.experimental import pallas as pl
from jax.experimental.pallas import tpu as pltpu
from jax.sharding import PartitionSpec as P

ATOM_DEV = 12
GROUPS = 3
LANES = 128
PAD = 2

f32 = jnp.float32
bf16 = jnp.bfloat16


def partner_a(i):
    return i ^ 1


def partner_b(i, count):
    return (i + 1 if i % 2 else i - 1) % count


def swap_a(x):
    return lax.ppermute(x, "dom", [(i, partner_a(i)) for i in range(lax.axis_size("dom"))])


def swap_b(x):
    count = lax.axis_size("dom")
    return lax.ppermute(x, "dom", [(i, partner_b(i, count)) for i in range(count)])


def send_c(x):
    count = lax.axis_size("dom")
    return lax.ppermute(x, "dom", [(i, partner_a(partner_b(i, count))) for i in range(count)])


def own_domain():
    index = lax.axis_index("dom")
    return index, lax.bitwise_and(index, 1)


def plane_to_rows(src, plane, dst, base):
    width_y = src.shape[2]
    for y0 in range(0, width_y, 16):
        for b in range(8):
            dst[pl.ds(base + y0 * 8 + b, 16, stride=8), :] = src[b, plane, y0 : y0 + 16, :].astype(f32)


def at_row(ref, base):
    return ref[pl.ds(pl.multiple_of(base, 8), 8), :]


def diagonal_blocks(product, field):
    lane = lax.broadcasted_iota(jnp.int32, (8, LANES), 1)
    total = jnp.zeros((8, LANES), f32)
    for s in range(ATOM_DEV):
        start = (field * ATOM_DEV + s) * 8
        total = total + jnp.where(
            lax.shift_right_logical(lane, 3) == s, product[start : start + 8, :], 0.0
        )
    return total


def measure(rows_ref, group, table, fields):
    stacked = []
    for field in fields:
        for s in range(ATOM_DEV):
            base = pl.multiple_of(rows_ref[group * ATOM_DEV + s] * 8, 8)
            stacked.append(jnp.concatenate([field(base + k * 8) for k in range(8)], axis=1))
    values = jnp.concatenate(stacked, axis=0).astype(bf16)
    product = lax.dot_general(
        values, table, (((1,), (1,)), ((), ())), preferred_element_type=f32
    )
    return [diagonal_blocks(product, q) for q in range(len(fields))]


def start_rows(rows_in, rows_ref, sem):
    copy = pltpu.make_async_copy(rows_in, rows_ref, sem)
    copy.start()
    return copy


def edge_kernel(wave_ref, to_a_ref, to_b_ref, sems):
    planes = wave_ref.shape[1]
    _, odd = own_domain()
    upper = planes - PAD
    copies = [
        start_rows(wave_ref.at[:, pl.ds(upper * (1 - odd), PAD)], to_a_ref, sems.at[0]),
        start_rows(wave_ref.at[:, pl.ds(upper * odd, PAD)], to_b_ref, sems.at[1]),
    ]
    for copy in copies:
        copy.wait()


def relayout_kernel(
    atoms_hbm,
    first_rows_hbm,
    wave_hbm,
    proj_hbm,
    rows_out,
    grid_ref,
    table_ref,
    margin_ref,
    to_a_ref,
    to_c_ref,
    wave_ref,
    atoms_ref,
    first_rows_ref,
    rows_ref,
    entry_ref,
    proj_ref,
    proj_scr,
    wave_sems,
    other_sems,
    *,
    domain_count,
):
    planes, width_y = wave_ref.shape[1:3]
    entry_count = rows_ref.shape[0]
    index, odd = own_domain()

    def plane_copy(plane):
        at_plane = (slice(None), pl.ds(plane, 1))
        return pltpu.make_async_copy(
            wave_hbm.at[at_plane], wave_ref.at[at_plane], wave_sems.at[plane]
        )

    atoms_copy = start_rows(atoms_hbm, atoms_ref, other_sems.at[0])
    first_copy = start_rows(first_rows_hbm, first_rows_ref, other_sems.at[1])
    for plane in range(planes):
        plane_copy(plane).start()
    proj_copy = start_rows(proj_hbm, proj_ref, other_sems.at[2])
    proj_scr[:, ATOM_DEV * 8 :, :] = jnp.zeros(
        (GROUPS, LANES - ATOM_DEV * 8, proj_scr.shape[2]), f32
    )
    atoms_copy.wait()
    first_copy.wait()
    for entry in range(entry_count):
        atom = atoms_ref[entry]
        owner = lax.shift_right_logical(atom * 171, 11)
        above = lax.rem(owner - index + 1 + domain_count, domain_count)
        group = jnp.where(odd == 1, above, 2 - above)
        slot = group * ATOM_DEV + atom - owner * ATOM_DEV
        entry_ref[slot] = entry
        rows_ref[slot] = first_rows_ref[entry]
    rows_copy = start_rows(rows_ref, rows_out, other_sems.at[3])

    def one_plane(plane, carry):
        plane_copy(plane).wait()
        plane_to_rows(wave_ref, plane, grid_ref, (plane + PAD) * width_y * 8)
        return carry

    lax.fori_loop(0, planes, one_plane, 0)
    proj_copy.wait()
    for group in range(GROUPS):
        for s in range(ATOM_DEV):
            entry = entry_ref[group * ATOM_DEV + s]
            proj_scr[group, s * 8 : s * 8 + 8, :] = proj_ref[entry].astype(f32)
        table = proj_scr[group].astype(bf16)
        table_ref[group] = table
        (sums,) = measure(
            rows_ref,
            group,
            table,
            [lambda base: at_row(grid_ref, base + PAD * width_y * 8)],
        )
        margin_ref[group] = sums
        if group < 2:
            to_a_ref[group] = sums
        else:
            to_c_ref[...] = jnp.zeros(to_c_ref.shape, f32)
            to_c_ref[0] = sums
    rows_copy.wait()


def forward_kernel(margin_ref, from_a_ref, to_b_ref):
    to_b_ref[0] = margin_ref[2]
    to_b_ref[1] = margin_ref[1] + from_a_ref[0]
    to_b_ref[2:] = jnp.zeros((to_b_ref.shape[0] - 2, 8, LANES), f32)


def third_shift(center, offset):
    return pltpu.roll(center, (-offset) % center.shape[-1], 1)


def circulant(near, far, center, length):
    row = lax.broadcasted_iota(jnp.int32, (length, length), 0)
    column = lax.broadcasted_iota(jnp.int32, (length, length), 1)
    distance = lax.bitwise_and(row - column, length - 1)
    table = jnp.where((distance == 1) | (distance == length - 1), near, 0.0)
    table = jnp.where((distance == 2) | (distance == length - 2), far, table)
    return jnp.where(distance == 0, center, table).astype(bf16)


def gradient_kernel(
    rows_in,
    grid_in,
    halo_a_ref,
    table_ref,
    coupling_hbm,
    weight_hbm,
    _,
    grid_ref,
    margin_ref,
    mixing_ref,
    factor_ref,
    y_ref,
    rows_ref,
    coupling_ref,
    weight_ref,
    sems,
):
    del grid_in
    copies = [
        start_rows(rows_in, rows_ref, sems.at[0]),
        start_rows(coupling_hbm, coupling_ref, sems.at[1]),
        start_rows(weight_hbm, weight_ref, sems.at[2]),
    ]
    width_y = LANES
    edge = PAD * width_y * 8
    planes = y_ref.shape[0] // (width_y * 8)

    def one_plane(plane, carry):
        base = pl.multiple_of(plane * width_y * 8, 8)
        row = [at_row(grid_ref, base + edge + (y % width_y) * 8) for y in range(-2, 2)]
        for y in range(width_y):
            row.append(at_row(grid_ref, base + edge + ((y + 2) % width_y) * 8))
            near = row[y + 3] - row[y + 1]
            far = row[y + 4] - row[y]
            y_ref[pl.ds(base + y * 8, 8), :] = (2.0 / 3.0) * near - (1.0 / 12.0) * far
        return carry

    lax.fori_loop(0, planes, one_plane, 0)

    def along_y(base):
        return at_row(y_ref, base)

    def along_z(base):
        center = at_row(grid_ref, base + edge)
        near = third_shift(center, 1) - third_shift(center, -1)
        far = third_shift(center, 2) - third_shift(center, -2)
        return (2.0 / 3.0) * near - (1.0 / 12.0) * far

    _, odd = own_domain()
    for i in range(PAD):
        plane = i + (planes + PAD) * (1 - odd)
        plane_to_rows(halo_a_ref, i, grid_ref, plane * width_y * 8)

    for copy in copies:
        copy.wait()
    for group in range(GROUPS):
        second, third = measure(rows_ref, group, table_ref[group], [along_y, along_z])
        margin_ref[0, group] = second
        margin_ref[1, group] = third

    bands = weight_ref.shape[1]
    band = lax.broadcasted_iota(jnp.int32, (bands, bands), 0)
    other = lax.broadcasted_iota(jnp.int32, (bands, bands), 1)
    weights = jnp.broadcast_to(weight_ref[...], (bands, bands))
    column = jnp.sum(jnp.where(band == other, weights, 0.0), axis=1, keepdims=True)
    factor_ref[...] = jnp.broadcast_to(-2.0 * column, factor_ref.shape)

    proj_count = coupling_ref.shape[0]
    symmetric = 0.5 * (coupling_ref[...] + coupling_ref[...].T)
    index = lax.broadcasted_iota(jnp.int32, (proj_count, LANES), 0)
    lane = lax.broadcasted_iota(jnp.int32, (proj_count, LANES), 1)
    spread = (lax.bitwise_and(lane, proj_count - 1) == index).astype(f32)
    tiled = jnp.dot(
        symmetric, spread, precision=lax.Precision.HIGHEST, preferred_element_type=f32
    )
    for a in range(LANES // proj_count):
        keep = (lax.shift_right_logical(lane, 3) == a) & (lane < ATOM_DEV * proj_count)
        mixing_ref[a * proj_count : (a + 1) * proj_count, :] = jnp.where(keep, tiled, 0.0)


def along_x(grid_ref, hop):
    def field(base):
        near = at_row(grid_ref, base + 3 * hop) - at_row(grid_ref, base + hop)
        far = at_row(grid_ref, base + 4 * hop) - at_row(grid_ref, base)
        return (2.0 / 3.0) * near - (1.0 / 12.0) * far

    return field


def first_kernel(
    rows_in,
    grid_in,
    halo_b_ref,
    table_ref,
    yz_ref,
    grid_ref,
    force_ref,
    rows_ref,
    rows_sem,
):
    del grid_in
    rows_copy = start_rows(rows_in, rows_ref, rows_sem)
    width_y = halo_b_ref.shape[2]
    hop = width_y * 8
    planes = grid_ref.shape[0] // hop - 2 * PAD
    _, odd = own_domain()

    for i in range(PAD):
        plane_to_rows(halo_b_ref, i, grid_ref, (i + (planes + PAD) * odd) * hop)
    rows_copy.wait()
    (force_ref[0],) = measure(rows_ref, 0, table_ref[0], [along_x(grid_ref, hop)])
    for k in range(2):
        force_ref[1 + k] = yz_ref[k, 0]


def rest_kernel(rows_in, grid_ref, table_ref, yz_ref, _, force_ref, rows_ref, rows_sem):
    rows_copy = start_rows(rows_in, rows_ref, rows_sem)
    rows_copy.wait()
    for group in range(1, GROUPS):
        (force_ref[group - 1, 0],) = measure(
            rows_ref, group, table_ref[group], [along_x(grid_ref, LANES * 8)]
        )
        for k in range(2):
            force_ref[group - 1, 1 + k] = yz_ref[k, group]


def pieces(x, count):
    out = []
    for _ in range(count):
        piece = x.astype(bf16)
        out.append(piece)
        x = x - piece.astype(f32)
    return out


def combine_kernel(
    margin_ref,
    from_a_ref,
    from_b_ref,
    from_c_ref,
    mixing_ref,
    factor_ref,
    force_ref,
    force_from_a_ref,
    scaled_ref,
    copies_ref,
):
    totals = jnp.concatenate(
        [
            margin_ref[0] + from_a_ref[1] + from_c_ref[0],
            margin_ref[1] + from_a_ref[0] + from_b_ref[0],
            margin_ref[2] + from_b_ref[1],
        ],
        axis=0,
    )
    count = totals.shape[0]
    upper, lower = pieces(totals, 2)
    mixed = [
        jnp.dot(
            jnp.concatenate([upper, lower], axis=0), mixing, preferred_element_type=f32
        )
        for mixing in pieces(mixing_ref[...], 2)
    ]
    scaled = mixed[0][:count] + (mixed[0][count:] + mixed[1][:count])
    parts = []
    for group in range(GROUPS):
        one = scaled[group * 8 : group * 8 + 8]
        scaled_ref[group] = one
        if group == 0:
            continue
        weighted = factor_ref[...] * one
        for k in range(3):
            force = force_ref[group - 1, k]
            if group == 1:
                force = force + force_from_a_ref[k]
            parts.append(jnp.sum(force * weighted, axis=0, keepdims=True))
    summed = jnp.concatenate(parts, axis=0)
    for step in (1, 2, 4):
        summed = summed + pltpu.roll(summed, LANES - step, 1)
    component = lax.bitwise_and(lax.broadcasted_iota(jnp.int32, (1, LANES), 1), 7)
    tiles = copies_ref.shape[0] // 2
    _, odd = own_domain()
    for group, half in ((1, 1 - odd), (2, odd)):
        row = jnp.zeros((1, LANES), f32)
        for k in range(3):
            part = (group - 1) * 3 + k
            value = summed[part : part + 1]
            value = pltpu.roll(value, k, 1) if k else value
            row = row + jnp.where(component == k, value, 0.0)
        for tile in range(tiles):
            copies_ref[half * tiles + tile] = jnp.broadcast_to(row, (8, LANES))


def total_kernel(gathered_ref, forces_ref):
    atoms = forces_ref.shape[1]
    row = jnp.sum(jnp.sum(gathered_ref[...], axis=0), axis=0, keepdims=True)
    lane = lax.broadcasted_iota(jnp.int32, (8, LANES), 1)
    component = lax.broadcasted_iota(jnp.int32, (8, LANES), 0)
    split = jnp.where(lax.bitwise_and(lane, 7) == component, row, 0.0)
    source = lax.broadcasted_iota(jnp.int32, (LANES, LANES), 0)
    target = lax.broadcasted_iota(jnp.int32, (LANES, LANES), 1)
    collect = (lax.shift_right_logical(source, 3) == target).astype(f32)
    forces = sum(
        jnp.dot(piece, collect.astype(bf16), preferred_element_type=f32)
        for piece in pieces(split, 3)
    )
    forces_ref[...] = forces[:3, :atoms]


def apply_kernel(
    rows_in,
    wave_hbm,
    pot_hbm,
    halo_a_ref,
    halo_b_ref,
    table_ref,
    scaled_ref,
    out_hbm,
    out_ref,
    add_ref,
    wave_ref,
    pot_ref,
    rows_ref,
    sems,
    edge_sems,
):
    bands, planes, width_y, width_z = out_ref.shape
    lane = lax.broadcasted_iota(jnp.int32, (8, LANES), 1)

    def wave_copy(plane):
        return pltpu.make_async_copy(
            wave_hbm.at[:, pl.ds(plane, 1)],
            wave_ref.at[:, pl.ds(plane + PAD, 1)],
            sems.at[0, plane],
        )

    def out_copy(plane):
        at_plane = (slice(None), pl.ds(plane, 1))
        return pltpu.make_async_copy(
            out_ref.at[at_plane], out_hbm.at[at_plane], sems.at[1, plane]
        )

    rows_copy = start_rows(rows_in, rows_ref, edge_sems.at[0])
    _, odd = own_domain()
    far_end = planes + PAD
    edge_copies = [
        start_rows(halo_a_ref, wave_ref.at[:, pl.ds(far_end * (1 - odd), PAD)], edge_sems.at[1]),
        start_rows(halo_b_ref, wave_ref.at[:, pl.ds(far_end * odd, PAD)], edge_sems.at[2]),
        start_rows(pot_hbm, pot_ref, edge_sems.at[3]),
    ]
    for plane in range(planes):
        wave_copy(plane).start()

    def clear(plane, carry):
        size = width_y * 8
        add_ref[pl.ds(pl.multiple_of(plane * size, size), size), :] = jnp.zeros((size, LANES), f32)
        return carry

    lax.fori_loop(0, planes, clear, 0)
    rows_copy.wait()

    for group in range(GROUPS):
        scaled = scaled_ref[group]
        blocks = [
            jnp.where(lax.shift_right_logical(lane, 3) == s, scaled, 0.0)
            for s in range(ATOM_DEV)
        ]
        coef = jnp.concatenate(blocks, axis=0).astype(bf16)
        terms = jnp.dot(coef, table_ref[group], preferred_element_type=f32)
        for s in range(ATOM_DEV):
            base = pl.multiple_of(rows_ref[group * ATOM_DEV + s] * 8, 8)
            for k in range(8):
                where = pl.ds(base + k * 8, 8)
                add_ref[where, :] = (
                    add_ref[where, :] + terms[s * 8 : s * 8 + 8, k * LANES : (k + 1) * LANES]
                )

    along_y = circulant(-16.0, 1.0, 0.0, width_y)
    along_z = circulant(-16.0, 1.0, 90.0, width_z)
    for copy in edge_copies:
        copy.wait()
    for plane in range(PAD):
        wave_copy(plane).wait()

    def finish(plane, carry):
        @pl.when(plane + PAD < planes)
        def _():
            wave_copy(plane + PAD).wait()

        for b in range(bands):
            wave = wave_ref[b, plane + PAD]
            summed = jnp.dot(
                jnp.concatenate([wave, along_y], axis=1),
                jnp.concatenate([along_z, wave], axis=0),
                preferred_element_type=f32,
            )
            near = wave_ref[b, plane + 1].astype(f32) + wave_ref[b, plane + 3].astype(f32)
            far = wave_ref[b, plane].astype(f32) + wave_ref[b, plane + 4].astype(f32)
            value = (summed + far - 16.0 * near) * (1.0 / 24.0)
            value = value + pot_ref[plane] * wave.astype(f32)
            added = add_ref[pl.ds(plane * width_y * 8 + b, width_y, stride=8), :]
            out_ref[b, plane] = (value + added).astype(bf16)
        out_copy(plane).start()
        return carry

    lax.fori_loop(0, planes, finish, 0)
    for plane in range(planes):
        out_copy(plane).wait()


VMEM = pl.BlockSpec(memory_space=pltpu.VMEM)
SMEM = pl.BlockSpec(memory_space=pltpu.SMEM)
HBM = pl.BlockSpec(memory_space=pltpu.HBM)
ANY = pl.BlockSpec(memory_space=pl.ANY)
MIB = 2**20


def in_hbm(x):
    return pltpu.with_memory_space_constraint(x, pltpu.HBM)


def call(kernel, name, outs, ins, out_specs, scratch=(), limit=8, **kwargs):
    return pl.pallas_call(
        kernel,
        out_shape=tuple(
            pltpu.HBM(shape, dtype) if spec is HBM else jax.ShapeDtypeStruct(shape, dtype)
            for (shape, dtype), spec in zip(outs, out_specs)
        ),
        in_specs=ins,
        out_specs=tuple(out_specs),
        scratch_shapes=list(scratch),
        compiler_params=pltpu.CompilerParams(vmem_limit_bytes=limit * MIB),
        cost_estimate=pl.CostEstimate(flops=1000, bytes_accessed=1000, transcendentals=0),
        name=name,
        **kwargs,
    )


def per_device(
    wavefunctions, potential, projectors, margin_atoms, tile_rows, coupling, band_weights
):
    band_count, plane_count, width_y, width_z = wavefunctions.shape
    entry_count, proj_count, tile_len = projectors.shape
    assert (band_count, proj_count, width_y, width_z) == (8, 8, 128, LANES)
    assert entry_count == GROUPS * ATOM_DEV
    grid_rows = (plane_count + 2 * PAD) * width_y * 8
    domain_count = lax.axis_size("dom")
    block = ((8, LANES), f32)
    pair = ((2, 8, LANES), f32)
    blocks = ((GROUPS, 8, LANES), f32)
    edge = ((band_count, PAD, width_y, width_z), bf16)
    slots = ((entry_count,), jnp.int32)
    slots_smem = pltpu.SMEM((entry_count,), jnp.int32)

    to_a, to_b = call(
        edge_kernel,
        "edges",
        [edge, edge],
        [HBM],
        [VMEM, VMEM],
        [pltpu.SemaphoreType.DMA((2,))],
    )(in_hbm(wavefunctions))
    halo_b = swap_b(to_b)
    halo_a = swap_a(to_a)

    rows, grid, table, margins, margins_to_a, margins_to_c = call(
        functools.partial(relayout_kernel, domain_count=domain_count),
        "relayout",
        [
            slots,
            ((grid_rows, LANES), f32),
            ((GROUPS, LANES, tile_len), bf16),
            blocks,
            pair,
            ((6, 8, LANES), f32),
        ],
        [HBM] * 4,
        [ANY] + [VMEM] * 5,
        [
            pltpu.VMEM(wavefunctions.shape, bf16),
            slots_smem,
            slots_smem,
            slots_smem,
            slots_smem,
            pltpu.VMEM(projectors.shape, bf16),
            pltpu.VMEM((GROUPS, LANES, tile_len), f32),
            pltpu.SemaphoreType.DMA((plane_count,)),
            pltpu.SemaphoreType.DMA((4,)),
        ],
    )(*map(in_hbm, (margin_atoms, tile_rows, wavefunctions, projectors)))

    from_a = swap_a(margins_to_a)
    (margins_to_b,) = call(forward_kernel, "forward", [((4, 8, LANES), f32)], [VMEM] * 2, [VMEM], limit=2)(
        margins, from_a
    )
    from_b = swap_b(margins_to_b)
    from_c = send_c(margins_to_c)

    grid, yz_margins, mixing, factor = call(
        gradient_kernel,
        "gradient",
        [
            ((grid_rows, LANES), f32),
            ((2, GROUPS, 8, LANES), f32),
            ((LANES, LANES), f32),
            block,
        ],
        [ANY] + [VMEM] * 3 + [HBM] * 2 + [VMEM],
        [VMEM] * 4,
        [
            pltpu.VMEM((plane_count * width_y * 8, LANES), f32),
            slots_smem,
            pltpu.VMEM(coupling.shape, f32),
            pltpu.VMEM((1, band_count), f32),
            pltpu.SemaphoreType.DMA((3,)),
        ],
        input_output_aliases={1: 0},
    )(
        rows,
        grid,
        halo_a,
        table,
        in_hbm(coupling),
        in_hbm(band_weights[None, :]),
        margins_to_b,
    )

    grid, force_to_a = call(
        first_kernel,
        "first",
        [((grid_rows, LANES), f32), blocks],
        [ANY] + [VMEM] * 4,
        [VMEM] * 2,
        [slots_smem, pltpu.SemaphoreType.DMA],
        input_output_aliases={1: 0},
    )(rows, grid, halo_b, table, yz_margins)
    force_from_a = swap_a(force_to_a)
    (force_margins,) = call(
        rest_kernel,
        "rest",
        [((2, 3, 8, LANES), f32)],
        [ANY] + [VMEM] * 4,
        [VMEM],
        [slots_smem, pltpu.SemaphoreType.DMA],
    )(rows, grid, table, yz_margins, force_to_a)

    bands = lax.axis_size("band")
    pairs = [
        [dom * bands + band for dom in (i, partner_b(i, domain_count)) for band in range(bands)]
        for i in range(1, domain_count, 2)
    ]
    scaled, copies = call(
        combine_kernel,
        "combine",
        [blocks, ((2 * bands // 8, 8, LANES), f32)],
        [VMEM] * 8,
        [VMEM] * 2,
        limit=2,
    )(margins, from_a, from_b, from_c, mixing, factor, force_margins, force_from_a)
    gathered = lax.all_to_all(
        copies.reshape(2 * bands, 1, LANES), ("dom", "band"), 0, 0, axis_index_groups=pairs
    )

    (applied,) = call(
        apply_kernel,
        "apply",
        [(wavefunctions.shape, bf16)],
        [ANY, HBM, HBM] + [VMEM] * 4,
        [HBM],
        [
            pltpu.VMEM(wavefunctions.shape, bf16),
            pltpu.VMEM((plane_count * width_y * 8, LANES), f32),
            pltpu.VMEM((band_count, plane_count + 2 * PAD, width_y, width_z), bf16),
            pltpu.VMEM(potential.shape, f32),
            slots_smem,
            pltpu.SemaphoreType.DMA((2, plane_count)),
            pltpu.SemaphoreType.DMA((4,)),
        ],
        limit=16,
    )(rows, in_hbm(wavefunctions), in_hbm(potential), halo_a, halo_b, table, scaled)

    (forces,) = call(
        total_kernel, "total", [((3, ATOM_DEV), f32)], [VMEM], [VMEM], limit=2
    )(gathered.reshape(2 * bands // 8, 8, LANES))
    return (applied, forces)


def solution(mesh):
    placed = (
        P("band", "dom", None, None),
        P("dom", None, None),
        P("dom", None, None),
        P("dom"),
        P("dom"),
        P(),
        P("band"),
    )
    return jax.shard_map(
        per_device,
        mesh=mesh,
        in_specs=placed,
        out_specs=(P("band", "dom", None, None), P(None, "dom")),
        check_vma=False,
    )
```

```python
import functools

import jax
import jax.numpy as jnp
from jax import lax
from jax.experimental import pallas as pl
from jax.experimental.pallas import tpu as pltpu
from jax.sharding import PartitionSpec as P

ATOM_DEV = 12
GROUPS = 3
LANES = 128
PAD = 2

f32 = jnp.float32
bf16 = jnp.bfloat16


def partner_a(i):
    return i ^ 1


def partner_b(i, count):
    return (i + 1 if i % 2 else i - 1) % count


def swap_a(x):
    return lax.ppermute(x, "dom", [(i, partner_a(i)) for i in range(lax.axis_size("dom"))])


def swap_b(x):
    count = lax.axis_size("dom")
    return lax.ppermute(x, "dom", [(i, partner_b(i, count)) for i in range(count)])


def send_c(x):
    count = lax.axis_size("dom")
    return lax.ppermute(x, "dom", [(i, partner_a(partner_b(i, count))) for i in range(count)])


def own_domain():
    index = lax.axis_index("dom")
    return index, lax.bitwise_and(index, 1)


def plane_to_rows(sources, plane, dst, base):
    bands, _, width_y, _ = sources[0].shape
    for y0 in range(0, width_y, 16):
        for i, source in enumerate(sources):
            for b in range(bands):
                part = source[b, plane, y0 : y0 + 16, :].astype(f32)
                dst[pl.ds(base + y0 * 8 + i * bands + b, 16, stride=8), :] = part


def at_row(ref, base):
    return ref[pl.ds(pl.multiple_of(base, 8), 8), :]


def diagonal_blocks(product, field):
    lane = lax.broadcasted_iota(jnp.int32, (8, LANES), 1)
    total = jnp.zeros((8, LANES), f32)
    for s in range(ATOM_DEV):
        start = (field * ATOM_DEV + s) * 8
        total = total + jnp.where(
            lax.shift_right_logical(lane, 3) == s, product[start : start + 8, :], 0.0
        )
    return total


def tile_values(rows_ref, group, field):
    tiles = []
    for s in range(ATOM_DEV):
        base = pl.multiple_of(rows_ref[group * ATOM_DEV + s] * 8, 8)
        tiles.append(jnp.concatenate([field(base + k * 8) for k in range(8)], axis=1))
    return jnp.concatenate(tiles, axis=0)


def z_gradient_values(rows_ref, group, grid_ref, offset, stencil):
    rows = []
    for s in range(ATOM_DEV):
        base = pl.multiple_of(rows_ref[group * ATOM_DEV + s] * 8, 8)
        rows.append(grid_ref[pl.ds(base + offset, 64), :])
    values = jnp.concatenate(rows, axis=0).astype(bf16)
    values = jnp.dot(values, stencil, preferred_element_type=f32) * (1.0 / 12.0)
    tiles = []
    for s in range(ATOM_DEV):
        start = s * 64
        tiles.append(
            jnp.concatenate(
                [values[start + k * 8 : start + k * 8 + 8, :] for k in range(8)], axis=1
            )
        )
    return jnp.concatenate(tiles, axis=0)


def contract(fields, table):
    values = jnp.concatenate(fields, axis=0).astype(bf16)
    product = lax.dot_general(
        values, table, (((1,), (1,)), ((), ())), preferred_element_type=f32
    )
    return [diagonal_blocks(product, q) for q in range(len(fields))]


def measure(rows_ref, group, table, field):
    return contract([tile_values(rows_ref, group, field)], table)[0]


def start_copy(source, target, sem):
    copy = pltpu.make_async_copy(source, target, sem)
    copy.start()
    return copy


def edge_kernel(wave_ref, to_b_ref, *rest):
    *to_a_refs, sems = rest
    planes = wave_ref.shape[1]
    _, odd = own_domain()
    upper = planes - PAD
    copies = [start_copy(wave_ref.at[:, pl.ds(upper * odd, PAD)], to_b_ref, sems.at[0])]
    for i, to_a_ref in enumerate(to_a_refs):
        count = to_a_ref.shape[0]
        source = wave_ref.at[pl.ds(i * count, count), pl.ds(upper * (1 - odd), PAD)]
        copies.append(start_copy(source, to_a_ref, sems.at[1 + i]))
    for copy in copies:
        copy.wait()


def relayout_kernel(
    atoms_hbm,
    first_rows_hbm,
    wave_hbm,
    proj_hbm,
    rows_ref,
    grid_ref,
    table_ref,
    margin_ref,
    to_a_ref,
    to_c_ref,
    wave_ref,
    atoms_ref,
    first_rows_ref,
    entry_ref,
    proj_ref,
    proj_scr,
    wave_sems,
    other_sems,
    *,
    domain_count,
):
    planes, width_y = wave_ref.shape[1:3]
    entry_count = rows_ref.shape[0]
    index, odd = own_domain()

    def plane_copy(plane):
        at_plane = (slice(None), pl.ds(plane, 1))
        return pltpu.make_async_copy(
            wave_hbm.at[at_plane], wave_ref.at[at_plane], wave_sems.at[plane]
        )

    atoms_copy = start_copy(atoms_hbm, atoms_ref, other_sems.at[0])
    first_copy = start_copy(first_rows_hbm, first_rows_ref, other_sems.at[1])
    for plane in range(planes):
        plane_copy(plane).start()
    proj_copy = start_copy(proj_hbm, proj_ref, other_sems.at[2])
    proj_scr[:, ATOM_DEV * 8 :, :] = jnp.zeros(
        (GROUPS, LANES - ATOM_DEV * 8, proj_scr.shape[2]), f32
    )
    atoms_copy.wait()
    first_copy.wait()

    def place(entry):
        atom = atoms_ref[entry]
        owner = lax.shift_right_logical(atom * 171, 11)
        above = lax.rem(owner - index + 1 + domain_count, domain_count)
        group = jnp.where(odd == 1, above, 2 - above)
        slot = group * ATOM_DEV + atom - owner * ATOM_DEV
        entry_ref[slot] = entry
        rows_ref[slot] = first_rows_ref[entry]

    for entry in range(entry_count):
        place(entry)

    def one_plane(plane, carry):
        plane_copy(plane).wait()
        plane_to_rows([wave_ref], plane, grid_ref, (plane + PAD) * width_y * 8)
        return carry

    lax.fori_loop(0, planes, one_plane, 0)
    proj_copy.wait()
    for group in range(GROUPS):
        for s in range(ATOM_DEV):
            entry = entry_ref[group * ATOM_DEV + s]
            proj_scr[group, s * 8 : s * 8 + 8, :] = proj_ref[entry].astype(f32)
        table = proj_scr[group].astype(bf16)
        table_ref[group] = table
        sums = measure(
            rows_ref, group, table, lambda base: at_row(grid_ref, base + PAD * width_y * 8)
        )
        margin_ref[group] = sums
        if group < 2:
            to_a_ref[group] = sums
        else:
            to_c_ref[...] = jnp.zeros(to_c_ref.shape, f32)
            to_c_ref[0] = sums


def forward_kernel(margin_ref, from_a_ref, to_b_ref):
    to_b_ref[0] = margin_ref[2]
    to_b_ref[1] = margin_ref[1] + from_a_ref[0]
    to_b_ref[2:] = jnp.zeros((to_b_ref.shape[0] - 2, 8, LANES), f32)


def circulant(near, far, center, length):
    row = lax.broadcasted_iota(jnp.int32, (length, length), 0)
    column = lax.broadcasted_iota(jnp.int32, (length, length), 1)
    distance = lax.bitwise_and(row - column, length - 1)
    table = jnp.where((distance == 1) | (distance == length - 1), near, 0.0)
    table = jnp.where((distance == 2) | (distance == length - 2), far, table)
    return jnp.where(distance == 0, center, table).astype(bf16)


def first_circulant(length):
    row = lax.broadcasted_iota(jnp.int32, (length, length), 0)
    column = lax.broadcasted_iota(jnp.int32, (length, length), 1)
    distance = lax.bitwise_and(row - column, length - 1)
    table = jnp.zeros((length, length), f32)
    for offset, factor in ((1, 8.0), (2, -1.0), (length - 1, -8.0), (length - 2, 1.0)):
        table = jnp.where(distance == offset, factor, table)
    return table.astype(bf16)


def gradient_kernel(
    rows_ref,
    grid_in,
    halo_a0_ref,
    halo_a1_ref,
    table_ref,
    coupling_hbm,
    weight_hbm,
    _,
    grid_ref,
    margin_ref,
    mixing_ref,
    factor_ref,
    y_ref,
    coupling_ref,
    weight_ref,
    sems,
):
    del grid_in
    copies = [
        start_copy(coupling_hbm, coupling_ref, sems.at[0]),
        start_copy(weight_hbm, weight_ref, sems.at[1]),
    ]
    width_y = LANES
    edge = PAD * width_y * 8
    planes = y_ref.shape[0] // (width_y * 8)

    def one_plane(plane, carry):
        base = pl.multiple_of(plane * width_y * 8, 8)
        row = [at_row(grid_ref, base + edge + (y % width_y) * 8) for y in range(-2, 2)]
        for y in range(width_y):
            row.append(at_row(grid_ref, base + edge + ((y + 2) % width_y) * 8))
            near = row[y + 3] - row[y + 1]
            far = row[y + 4] - row[y]
            y_ref[pl.ds(base + y * 8, 8), :] = (2.0 / 3.0) * near - (1.0 / 12.0) * far
        return carry

    lax.fori_loop(0, planes, one_plane, 0)

    _, odd = own_domain()
    for i in range(PAD):
        plane = i + (planes + PAD) * (1 - odd)
        plane_to_rows([halo_a0_ref, halo_a1_ref], i, grid_ref, plane * width_y * 8)

    for copy in copies:
        copy.wait()
    stencil = first_circulant(width_y)
    for group in range(GROUPS):
        second, third = contract(
            [
                tile_values(rows_ref, group, lambda base: at_row(y_ref, base)),
                z_gradient_values(rows_ref, group, grid_ref, edge, stencil),
            ],
            table_ref[group],
        )
        margin_ref[0, group] = second
        margin_ref[1, group] = third

    bands = weight_ref.shape[1]
    band = lax.broadcasted_iota(jnp.int32, (bands, bands), 0)
    other = lax.broadcasted_iota(jnp.int32, (bands, bands), 1)
    weights = jnp.broadcast_to(weight_ref[...], (bands, bands))
    column = jnp.sum(jnp.where(band == other, weights, 0.0), axis=1, keepdims=True)
    factor_ref[...] = jnp.broadcast_to(-2.0 * column, factor_ref.shape)

    proj_count = coupling_ref.shape[0]
    symmetric = 0.5 * (coupling_ref[...] + coupling_ref[...].T)
    index = lax.broadcasted_iota(jnp.int32, (proj_count, LANES), 0)
    lane = lax.broadcasted_iota(jnp.int32, (proj_count, LANES), 1)
    spread = (lax.bitwise_and(lane, proj_count - 1) == index).astype(f32)
    tiled = jnp.dot(
        symmetric, spread, precision=lax.Precision.HIGHEST, preferred_element_type=f32
    )
    for a in range(LANES // proj_count):
        keep = (lax.shift_right_logical(lane, 3) == a) & (lane < ATOM_DEV * proj_count)
        mixing_ref[a * proj_count : (a + 1) * proj_count, :] = jnp.where(keep, tiled, 0.0)


def along_x(grid_ref, hop):
    def field(base):
        near = at_row(grid_ref, base + 3 * hop) - at_row(grid_ref, base + hop)
        far = at_row(grid_ref, base + 4 * hop) - at_row(grid_ref, base)
        return (2.0 / 3.0) * near - (1.0 / 12.0) * far

    return field


def first_kernel(
    rows_ref,
    grid_in,
    halo_b_ref,
    table_ref,
    yz_ref,
    grid_ref,
    force_ref,
):
    del grid_in
    width_y = halo_b_ref.shape[2]
    hop = width_y * 8
    planes = grid_ref.shape[0] // hop - 2 * PAD
    _, odd = own_domain()

    for i in range(PAD):
        plane_to_rows([halo_b_ref], i, grid_ref, (i + (planes + PAD) * odd) * hop)
    force_ref[0] = measure(rows_ref, 0, table_ref[0], along_x(grid_ref, hop))
    for k in range(2):
        force_ref[1 + k] = yz_ref[k, 0]


def pieces(x, count):
    out = []
    for _ in range(count):
        piece = x.astype(bf16)
        out.append(piece)
        x = x - piece.astype(f32)
    return out


def rest_kernel(
    rows_ref,
    grid_ref,
    table_ref,
    yz_ref,
    margin_ref,
    from_a_ref,
    from_b_ref,
    from_c_ref,
    mixing_ref,
    factor_ref,
    _,
    scaled_ref,
    weighted_ref,
    parts_ref,
):
    forces = []
    for group in range(1, GROUPS):
        first = measure(rows_ref, group, table_ref[group], along_x(grid_ref, LANES * 8))
        forces.append([first, yz_ref[0, group], yz_ref[1, group]])
    totals = jnp.concatenate(
        [
            margin_ref[0] + from_a_ref[1] + from_c_ref[0],
            margin_ref[1] + from_a_ref[0] + from_b_ref[0],
            margin_ref[2] + from_b_ref[1],
        ],
        axis=0,
    )
    count = totals.shape[0]
    upper, lower = pieces(totals, 2)
    mixed = [
        jnp.dot(
            jnp.concatenate([upper, lower], axis=0), mixing, preferred_element_type=f32
        )
        for mixing in pieces(mixing_ref[...], 2)
    ]
    scaled = mixed[0][:count] + (mixed[0][count:] + mixed[1][:count])
    for group in range(GROUPS):
        scaled_ref[group] = scaled[group * 8 : group * 8 + 8]
    weighted = [factor_ref[...] * scaled[group * 8 : group * 8 + 8] for group in (1, 2)]
    weighted_ref[...] = weighted[0]
    parts_ref[...] = jnp.concatenate(
        [
            jnp.sum(force * weight, axis=0, keepdims=True)
            for weight, force_group in zip(weighted, forces)
            for force in force_group
        ]
        + [jnp.zeros((2, LANES), f32)],
        axis=0,
    )


def combine_kernel(parts_ref, weighted_ref, force_from_a_ref, copies_ref):
    from_a = [
        jnp.sum(force_from_a_ref[k] * weighted_ref[...], axis=0, keepdims=True) for k in range(3)
    ]
    summed = parts_ref[...] + jnp.concatenate(from_a + [jnp.zeros((5, LANES), f32)], axis=0)
    for step in (1, 2, 4):
        summed = summed + pltpu.roll(summed, LANES - step, 1)
    component = lax.bitwise_and(lax.broadcasted_iota(jnp.int32, (1, LANES), 1), 7)
    tiles = copies_ref.shape[0] // 2
    _, odd = own_domain()
    for group, half in ((1, 1 - odd), (2, odd)):
        row = jnp.zeros((1, LANES), f32)
        for k in range(3):
            part = (group - 1) * 3 + k
            value = summed[part : part + 1]
            value = pltpu.roll(value, k, 1) if k else value
            row = row + jnp.where(component == k, value, 0.0)
        for tile in range(tiles):
            copies_ref[half * tiles + tile] = jnp.broadcast_to(row, (8, LANES))


def total_kernel(gathered_ref, forces_ref):
    atoms = forces_ref.shape[1]
    row = jnp.sum(jnp.sum(gathered_ref[...], axis=0), axis=0, keepdims=True)
    lane = lax.broadcasted_iota(jnp.int32, (8, LANES), 1)
    component = lax.broadcasted_iota(jnp.int32, (8, LANES), 0)
    split = jnp.where(lax.bitwise_and(lane, 7) == component, row, 0.0)
    source = lax.broadcasted_iota(jnp.int32, (LANES, LANES), 0)
    target = lax.broadcasted_iota(jnp.int32, (LANES, LANES), 1)
    collect = (lax.shift_right_logical(source, 3) == target).astype(f32)
    forces = sum(
        jnp.dot(piece, collect.astype(bf16), preferred_element_type=f32)
        for piece in pieces(split, 3)
    )
    forces_ref[...] = forces[:3, :atoms]


def apply_kernel(
    rows_ref,
    wave_hbm,
    pot_hbm,
    halo_a0_ref,
    halo_a1_ref,
    halo_b_ref,
    table_ref,
    scaled_ref,
    out_hbm,
    out_ref,
    add_ref,
    wave_ref,
    pot_ref,
    sems,
    edge_sems,
):
    bands, planes, width_y, width_z = out_ref.shape
    lane = lax.broadcasted_iota(jnp.int32, (8, LANES), 1)

    def wave_copy(plane):
        return pltpu.make_async_copy(
            wave_hbm.at[:, pl.ds(plane, 1)],
            wave_ref.at[:, pl.ds(plane + PAD, 1)],
            sems.at[0, plane],
        )

    def out_copy(plane):
        at_plane = (slice(None), pl.ds(plane, 1))
        return pltpu.make_async_copy(
            out_ref.at[at_plane], out_hbm.at[at_plane], sems.at[1, plane]
        )

    _, odd = own_domain()
    far_end = planes + PAD
    edge_copies = [
        start_copy(
            halo_a0_ref,
            wave_ref.at[pl.ds(0, bands // 2), pl.ds(far_end * (1 - odd), PAD)],
            edge_sems.at[1],
        ),
        start_copy(
            halo_a1_ref,
            wave_ref.at[pl.ds(bands // 2, bands // 2), pl.ds(far_end * (1 - odd), PAD)],
            edge_sems.at[0],
        ),
        start_copy(halo_b_ref, wave_ref.at[:, pl.ds(far_end * odd, PAD)], edge_sems.at[2]),
        start_copy(pot_hbm, pot_ref, edge_sems.at[3]),
    ]
    for plane in range(planes):
        wave_copy(plane).start()

    def clear(plane, carry):
        size = width_y * 8
        add_ref[pl.ds(pl.multiple_of(plane * size, size), size), :] = jnp.zeros((size, LANES), f32)
        return carry

    lax.fori_loop(0, planes, clear, 0)

    for group in range(GROUPS):
        scaled = scaled_ref[group]
        blocks = [
            jnp.where(lax.shift_right_logical(lane, 3) == s, scaled, 0.0)
            for s in range(ATOM_DEV)
        ]
        coef = jnp.concatenate(blocks, axis=0).astype(bf16)
        terms = jnp.dot(coef, table_ref[group], preferred_element_type=f32)
        for s in range(ATOM_DEV):
            base = pl.multiple_of(rows_ref[group * ATOM_DEV + s] * 8, 8)
            for k in range(8):
                where = pl.ds(base + k * 8, 8)
                add_ref[where, :] = (
                    add_ref[where, :] + terms[s * 8 : s * 8 + 8, k * LANES : (k + 1) * LANES]
                )

    along_y = circulant(-16.0, 1.0, 0.0, width_y)
    along_z = circulant(-16.0, 1.0, 90.0, width_z)
    for copy in edge_copies:
        copy.wait()
    for plane in range(PAD):
        wave_copy(plane).wait()

    def finish(plane, carry):
        @pl.when(plane + PAD < planes)
        def _():
            wave_copy(plane + PAD).wait()

        for b in range(bands):
            wave = wave_ref[b, plane + PAD]
            summed = jnp.dot(
                jnp.concatenate([wave, along_y], axis=1),
                jnp.concatenate([along_z, wave], axis=0),
                preferred_element_type=f32,
            )
            near = wave_ref[b, plane + 1].astype(f32) + wave_ref[b, plane + 3].astype(f32)
            far = wave_ref[b, plane].astype(f32) + wave_ref[b, plane + 4].astype(f32)
            value = (summed + far - 16.0 * near) * (1.0 / 24.0)
            value = value + pot_ref[plane] * wave.astype(f32)
            added = add_ref[pl.ds(plane * width_y * 8 + b, width_y, stride=8), :]
            out_ref[b, plane] = (value + added).astype(bf16)
        out_copy(plane).start()
        return carry

    lax.fori_loop(0, planes, finish, 0)
    for plane in range(planes):
        out_copy(plane).wait()


VMEM = pl.BlockSpec(memory_space=pltpu.VMEM)
SMEM = pl.BlockSpec(memory_space=pltpu.SMEM)
HBM = pl.BlockSpec(memory_space=pltpu.HBM)
ANY = pl.BlockSpec(memory_space=pl.ANY)
MIB = 2**20


def out_type(shape, dtype, spec):
    if spec is HBM:
        return pltpu.HBM(shape, dtype)
    if spec is SMEM:
        return pltpu.SMEM(shape, dtype)
    return jax.ShapeDtypeStruct(shape, dtype)


def in_hbm(x):
    return pltpu.with_memory_space_constraint(x, pltpu.HBM)


def call(kernel, name, outs, ins, out_specs, scratch=(), limit=8, **kwargs):
    return pl.pallas_call(
        kernel,
        out_shape=tuple(
            out_type(shape, dtype, spec)
            for (shape, dtype), spec in zip(outs, out_specs)
        ),
        in_specs=ins,
        out_specs=tuple(out_specs),
        scratch_shapes=list(scratch),
        compiler_params=pltpu.CompilerParams(vmem_limit_bytes=limit * MIB),
        cost_estimate=pl.CostEstimate(flops=1000, bytes_accessed=1000, transcendentals=0),
        name=name,
        **kwargs,
    )


def per_device(
    wavefunctions, potential, projectors, margin_atoms, tile_rows, coupling, band_weights
):
    band_count, plane_count, width_y, width_z = wavefunctions.shape
    entry_count, proj_count, tile_len = projectors.shape
    assert (band_count, proj_count, width_y, width_z) == (8, 8, 128, LANES)
    assert entry_count == GROUPS * ATOM_DEV
    grid_rows = (plane_count + 2 * PAD) * width_y * 8
    domain_count = lax.axis_size("dom")
    block = ((8, LANES), f32)
    pair = ((2, 8, LANES), f32)
    blocks = ((GROUPS, 8, LANES), f32)
    edge = ((band_count, PAD, width_y, width_z), bf16)
    slots = ((entry_count,), jnp.int32)
    slots_smem = pltpu.SMEM((entry_count,), jnp.int32)

    half_edge = ((band_count // 2, PAD, width_y, width_z), bf16)
    to_b, *to_a = call(
        edge_kernel,
        "edges",
        [edge, half_edge, half_edge],
        [HBM],
        [VMEM] * 3,
        [pltpu.SemaphoreType.DMA((3,))],
    )(in_hbm(wavefunctions))
    halo_b = swap_b(to_b)
    halo_a = [swap_a(part) for part in to_a]

    rows, grid, table, margins, margins_to_a, margins_to_c = call(
        functools.partial(relayout_kernel, domain_count=domain_count),
        "relayout",
        [
            slots,
            ((grid_rows, LANES), f32),
            ((GROUPS, LANES, tile_len), bf16),
            blocks,
            pair,
            ((6, 8, LANES), f32),
        ],
        [HBM] * 4,
        [SMEM] + [VMEM] * 5,
        [
            pltpu.VMEM(wavefunctions.shape, bf16),
            slots_smem,
            slots_smem,
            slots_smem,
            pltpu.VMEM(projectors.shape, bf16),
            pltpu.VMEM((GROUPS, LANES, tile_len), f32),
            pltpu.SemaphoreType.DMA((plane_count,)),
            pltpu.SemaphoreType.DMA((3,)),
        ],
    )(*map(in_hbm, (margin_atoms, tile_rows, wavefunctions, projectors)))

    rows = pltpu.with_memory_space_constraint(rows, pltpu.SMEM)
    from_a = swap_a(margins_to_a)
    (margins_to_b,) = call(forward_kernel, "forward", [((4, 8, LANES), f32)], [VMEM] * 2, [VMEM], limit=2)(
        margins, from_a
    )
    from_b = swap_b(margins_to_b)
    from_c = send_c(margins_to_c)

    grid, yz_margins, mixing, factor = call(
        gradient_kernel,
        "gradient",
        [
            ((grid_rows, LANES), f32),
            ((2, GROUPS, 8, LANES), f32),
            ((LANES, LANES), f32),
            block,
        ],
        [SMEM] + [VMEM] * 4 + [HBM] * 2 + [VMEM],
        [VMEM] * 4,
        [
            pltpu.VMEM((plane_count * width_y * 8, LANES), f32),
            pltpu.VMEM(coupling.shape, f32),
            pltpu.VMEM((1, band_count), f32),
            pltpu.SemaphoreType.DMA((2,)),
        ],
        input_output_aliases={1: 0},
    )(
        rows,
        grid,
        *halo_a,
        table,
        in_hbm(coupling),
        in_hbm(band_weights[None, :]),
        margins_to_b,
    )

    grid, force_to_a = call(
        first_kernel,
        "first",
        [((grid_rows, LANES), f32), blocks],
        [SMEM] + [VMEM] * 4,
        [VMEM] * 2,
        input_output_aliases={1: 0},
    )(rows, grid, halo_b, table, yz_margins)
    force_from_a = swap_a(force_to_a)
    scaled, weighted, parts = call(
        rest_kernel,
        "rest",
        [blocks, block, block],
        [SMEM] + [VMEM] * 10,
        [VMEM] * 3,
    )(
        rows,
        grid,
        table,
        yz_margins,
        margins,
        from_a,
        from_b,
        from_c,
        mixing,
        factor,
        force_to_a,
    )

    bands = lax.axis_size("band")
    pairs = [
        [dom * bands + band for dom in (i, partner_b(i, domain_count)) for band in range(bands)]
        for i in range(1, domain_count, 2)
    ]
    (copies,) = call(
        combine_kernel,
        "combine",
        [((2 * bands // 8, 8, LANES), f32)],
        [VMEM] * 3,
        [VMEM],
        limit=2,
    )(parts, weighted, force_from_a)
    gathered = lax.all_to_all(
        copies.reshape(2 * bands, 1, LANES), ("dom", "band"), 0, 0, axis_index_groups=pairs
    )

    (applied,) = call(
        apply_kernel,
        "apply",
        [(wavefunctions.shape, bf16)],
        [SMEM, HBM, HBM] + [VMEM] * 5,
        [HBM],
        [
            pltpu.VMEM(wavefunctions.shape, bf16),
            pltpu.VMEM((plane_count * width_y * 8, LANES), f32),
            pltpu.VMEM((band_count, plane_count + 2 * PAD, width_y, width_z), bf16),
            pltpu.VMEM(potential.shape, f32),
            pltpu.SemaphoreType.DMA((2, plane_count)),
            pltpu.SemaphoreType.DMA((4,)),
        ],
        limit=16,
    )(rows, in_hbm(wavefunctions), in_hbm(potential), *halo_a, halo_b, table, scaled)

    (forces,) = call(
        total_kernel, "total", [((3, ATOM_DEV), f32)], [VMEM], [VMEM], limit=2
    )(gathered.reshape(2 * bands // 8, 8, LANES))
    return (applied, forces)


def solution(mesh):
    placed = (
        P("band", "dom", None, None),
        P("dom", None, None),
        P("dom", None, None),
        P("dom"),
        P("dom"),
        P(),
        P("band"),
    )
    return jax.shard_map(
        per_device,
        mesh=mesh,
        in_specs=placed,
        out_specs=(P("band", "dom", None, None), P(None, "dom")),
        check_vma=False,
    )
```

```python
import functools

import jax
import jax.numpy as jnp
from jax import lax
from jax.experimental import pallas as pl
from jax.experimental.pallas import tpu as pltpu
from jax.sharding import PartitionSpec as P

ATOM_DEV = 12
GROUPS = 3
LANES = 128
PAD = 2

f32 = jnp.float32
bf16 = jnp.bfloat16


def partner_a(i):
    return i ^ 1


def partner_b(i, count):
    return (i + 1 if i % 2 else i - 1) % count


def swap_a(x):
    return lax.ppermute(x, "dom", [(i, partner_a(i)) for i in range(lax.axis_size("dom"))])


def swap_b(x):
    count = lax.axis_size("dom")
    return lax.ppermute(x, "dom", [(i, partner_b(i, count)) for i in range(count)])


def send_c(x):
    count = lax.axis_size("dom")
    return lax.ppermute(x, "dom", [(i, partner_a(partner_b(i, count))) for i in range(count)])


def own_domain():
    index = lax.axis_index("dom")
    return index, lax.bitwise_and(index, 1)


def plane_to_rows(sources, plane, dst, base):
    bands, _, width_y, _ = sources[0].shape
    for y0 in range(0, width_y, 16):
        for i, source in enumerate(sources):
            for b in range(bands):
                part = source[b, plane, y0 : y0 + 16, :].astype(f32)
                dst[pl.ds(base + y0 * 8 + i * bands + b, 16, stride=8), :] = part


def at_row(ref, base):
    return ref[pl.ds(pl.multiple_of(base, 8), 8), :]


def diagonal_blocks(product, field):
    lane = lax.broadcasted_iota(jnp.int32, (8, LANES), 1)
    total = jnp.zeros((8, LANES), f32)
    for s in range(ATOM_DEV):
        start = (field * ATOM_DEV + s) * 8
        total = total + jnp.where(
            lax.shift_right_logical(lane, 3) == s, product[start : start + 8, :], 0.0
        )
    return total


def tile_values(rows_ref, group, field):
    tiles = []
    for s in range(ATOM_DEV):
        base = pl.multiple_of(rows_ref[group * ATOM_DEV + s] * 8, 8)
        tiles.append(jnp.concatenate([field(base + k * 8) for k in range(8)], axis=1))
    return jnp.concatenate(tiles, axis=0)


def z_gradient_values(rows_ref, group, grid_ref, offset, stencil):
    rows = []
    for s in range(ATOM_DEV):
        base = pl.multiple_of(rows_ref[group * ATOM_DEV + s] * 8, 8)
        rows.append(grid_ref[pl.ds(base + offset, 64), :])
    values = jnp.concatenate(rows, axis=0).astype(bf16)
    values = jnp.dot(values, stencil, preferred_element_type=f32) * (1.0 / 12.0)
    tiles = []
    for s in range(ATOM_DEV):
        start = s * 64
        tiles.append(
            jnp.concatenate(
                [values[start + k * 8 : start + k * 8 + 8, :] for k in range(8)], axis=1
            )
        )
    return jnp.concatenate(tiles, axis=0)


def contract(fields, table):
    values = jnp.concatenate(fields, axis=0).astype(bf16)
    product = lax.dot_general(
        values, table, (((1,), (1,)), ((), ())), preferred_element_type=f32
    )
    return [diagonal_blocks(product, q) for q in range(len(fields))]


def measure(rows_ref, group, table, field):
    return contract([tile_values(rows_ref, group, field)], table)[0]


def start_copy(source, target, sem):
    copy = pltpu.make_async_copy(source, target, sem)
    copy.start()
    return copy


def edge_kernel(wave_hbm, to_b_ref, sem):
    planes = wave_hbm.shape[1]
    _, odd = own_domain()
    start_copy(wave_hbm.at[:, pl.ds((planes - PAD) * odd, PAD)], to_b_ref, sem).wait()


def relayout_kernel(
    atoms_hbm,
    first_rows_hbm,
    wave_hbm,
    proj_hbm,
    _,
    rows_ref,
    grid_ref,
    table_ref,
    margin_ref,
    to_a_ref,
    to_c_ref,
    edge_a0_ref,
    edge_a1_ref,
    wave_ref,
    atoms_ref,
    first_rows_ref,
    entry_ref,
    proj_ref,
    proj_scr,
    wave_sems,
    other_sems,
    *,
    domain_count,
):
    planes, width_y = wave_ref.shape[1:3]
    entry_count = rows_ref.shape[0]
    index, odd = own_domain()

    def plane_copy(plane):
        at_plane = (slice(None), pl.ds(plane, 1))
        return pltpu.make_async_copy(
            wave_hbm.at[at_plane], wave_ref.at[at_plane], wave_sems.at[plane]
        )

    atoms_copy = start_copy(atoms_hbm, atoms_ref, other_sems.at[0])
    first_copy = start_copy(first_rows_hbm, first_rows_ref, other_sems.at[1])
    for plane in range(planes):
        plane_copy(plane).start()
    proj_copy = start_copy(proj_hbm, proj_ref, other_sems.at[2])
    edge_copies = []
    for i, edge_ref in enumerate((edge_a0_ref, edge_a1_ref)):
        count = edge_ref.shape[0]
        source = wave_hbm.at[pl.ds(i * count, count), pl.ds((planes - PAD) * (1 - odd), PAD)]
        edge_copies.append(start_copy(source, edge_ref, other_sems.at[3 + i]))
    proj_scr[:, ATOM_DEV * 8 :, :] = jnp.zeros(
        (GROUPS, LANES - ATOM_DEV * 8, proj_scr.shape[2]), f32
    )
    atoms_copy.wait()
    first_copy.wait()

    def place(entry):
        atom = atoms_ref[entry]
        owner = lax.shift_right_logical(atom * 171, 11)
        above = lax.rem(owner - index + 1 + domain_count, domain_count)
        group = jnp.where(odd == 1, above, 2 - above)
        slot = group * ATOM_DEV + atom - owner * ATOM_DEV
        entry_ref[slot] = entry
        rows_ref[slot] = first_rows_ref[entry]

    for entry in range(entry_count):
        place(entry)

    def one_plane(plane, carry):
        plane_copy(plane).wait()
        plane_to_rows([wave_ref], plane, grid_ref, (plane + PAD) * width_y * 8)
        return carry

    lax.fori_loop(0, planes, one_plane, 0)
    proj_copy.wait()
    for group in range(GROUPS):
        for s in range(ATOM_DEV):
            entry = entry_ref[group * ATOM_DEV + s]
            proj_scr[group, s * 8 : s * 8 + 8, :] = proj_ref[entry].astype(f32)
        table = proj_scr[group].astype(bf16)
        table_ref[group] = table
        sums = measure(
            rows_ref, group, table, lambda base: at_row(grid_ref, base + PAD * width_y * 8)
        )
        margin_ref[group] = sums
        if group < 2:
            to_a_ref[group] = sums
        else:
            to_c_ref[...] = jnp.zeros(to_c_ref.shape, f32)
            to_c_ref[0] = sums
    for copy in edge_copies:
        copy.wait()


def forward_kernel(margin_ref, from_a_ref, to_b_ref):
    to_b_ref[0] = margin_ref[2]
    to_b_ref[1] = margin_ref[1] + from_a_ref[0]
    to_b_ref[2:] = jnp.zeros((to_b_ref.shape[0] - 2, 8, LANES), f32)


def circulant(near, far, center, length):
    row = lax.broadcasted_iota(jnp.int32, (length, length), 0)
    column = lax.broadcasted_iota(jnp.int32, (length, length), 1)
    distance = lax.bitwise_and(row - column, length - 1)
    table = jnp.where((distance == 1) | (distance == length - 1), near, 0.0)
    table = jnp.where((distance == 2) | (distance == length - 2), far, table)
    return jnp.where(distance == 0, center, table).astype(bf16)


def first_circulant(length):
    row = lax.broadcasted_iota(jnp.int32, (length, length), 0)
    column = lax.broadcasted_iota(jnp.int32, (length, length), 1)
    distance = lax.bitwise_and(row - column, length - 1)
    table = jnp.zeros((length, length), f32)
    for offset, factor in ((1, 8.0), (2, -1.0), (length - 1, -8.0), (length - 2, 1.0)):
        table = jnp.where(distance == offset, factor, table)
    return table.astype(bf16)


def gradient_kernel(
    rows_ref,
    grid_in,
    halo_a0_ref,
    halo_a1_ref,
    table_ref,
    coupling_hbm,
    weight_hbm,
    _,
    grid_ref,
    margin_ref,
    mixing_ref,
    factor_ref,
    y_ref,
    coupling_ref,
    weight_ref,
    sems,
):
    del grid_in
    copies = [
        start_copy(coupling_hbm, coupling_ref, sems.at[0]),
        start_copy(weight_hbm, weight_ref, sems.at[1]),
    ]
    width_y = LANES
    edge = PAD * width_y * 8
    planes = y_ref.shape[0] // (width_y * 8)

    def one_plane(plane, carry):
        base = pl.multiple_of(plane * width_y * 8, 8)
        row = [at_row(grid_ref, base + edge + (y % width_y) * 8) for y in range(-2, 2)]
        for y in range(width_y):
            row.append(at_row(grid_ref, base + edge + ((y + 2) % width_y) * 8))
            near = row[y + 3] - row[y + 1]
            far = row[y + 4] - row[y]
            y_ref[pl.ds(base + y * 8, 8), :] = (2.0 / 3.0) * near - (1.0 / 12.0) * far
        return carry

    lax.fori_loop(0, planes, one_plane, 0)

    _, odd = own_domain()
    for i in range(PAD):
        plane = i + (planes + PAD) * (1 - odd)
        plane_to_rows([halo_a0_ref, halo_a1_ref], i, grid_ref, plane * width_y * 8)

    for copy in copies:
        copy.wait()
    stencil = first_circulant(width_y)
    for group in range(GROUPS):
        second, third = contract(
            [
                tile_values(rows_ref, group, lambda base: at_row(y_ref, base)),
                z_gradient_values(rows_ref, group, grid_ref, edge, stencil),
            ],
            table_ref[group],
        )
        margin_ref[0, group] = second
        margin_ref[1, group] = third

    bands = weight_ref.shape[1]
    band = lax.broadcasted_iota(jnp.int32, (bands, bands), 0)
    other = lax.broadcasted_iota(jnp.int32, (bands, bands), 1)
    weights = jnp.broadcast_to(weight_ref[...], (bands, bands))
    column = jnp.sum(jnp.where(band == other, weights, 0.0), axis=1, keepdims=True)
    factor_ref[...] = jnp.broadcast_to(-2.0 * column, factor_ref.shape)

    proj_count = coupling_ref.shape[0]
    symmetric = 0.5 * (coupling_ref[...] + coupling_ref[...].T)
    index = lax.broadcasted_iota(jnp.int32, (proj_count, LANES), 0)
    lane = lax.broadcasted_iota(jnp.int32, (proj_count, LANES), 1)
    spread = (lax.bitwise_and(lane, proj_count - 1) == index).astype(f32)
    tiled = jnp.dot(
        symmetric, spread, precision=lax.Precision.HIGHEST, preferred_element_type=f32
    )
    for a in range(LANES // proj_count):
        keep = (lax.shift_right_logical(lane, 3) == a) & (lane < ATOM_DEV * proj_count)
        mixing_ref[a * proj_count : (a + 1) * proj_count, :] = jnp.where(keep, tiled, 0.0)


def along_x(grid_ref, hop):
    def field(base):
        near = at_row(grid_ref, base + 3 * hop) - at_row(grid_ref, base + hop)
        far = at_row(grid_ref, base + 4 * hop) - at_row(grid_ref, base)
        return (2.0 / 3.0) * near - (1.0 / 12.0) * far

    return field


def first_kernel(
    rows_ref,
    grid_in,
    halo_b_ref,
    table_ref,
    yz_ref,
    grid_ref,
    force_ref,
):
    del grid_in
    width_y = halo_b_ref.shape[2]
    hop = width_y * 8
    planes = grid_ref.shape[0] // hop - 2 * PAD
    _, odd = own_domain()

    for i in range(PAD):
        plane_to_rows([halo_b_ref], i, grid_ref, (i + (planes + PAD) * odd) * hop)
    force_ref[0] = measure(rows_ref, 0, table_ref[0], along_x(grid_ref, hop))
    for k in range(2):
        force_ref[1 + k] = yz_ref[k, 0]


def pieces(x, count):
    out = []
    for _ in range(count):
        piece = x.astype(bf16)
        out.append(piece)
        x = x - piece.astype(f32)
    return out


def rest_kernel(
    rows_ref,
    grid_ref,
    table_ref,
    yz_ref,
    margin_ref,
    from_a_ref,
    from_b_ref,
    from_c_ref,
    mixing_ref,
    factor_ref,
    _,
    scaled_ref,
    weighted_ref,
    parts_ref,
):
    forces = []
    for group in range(1, GROUPS):
        first = measure(rows_ref, group, table_ref[group], along_x(grid_ref, LANES * 8))
        forces.append([first, yz_ref[0, group], yz_ref[1, group]])
    totals = jnp.concatenate(
        [
            margin_ref[0] + from_a_ref[1] + from_c_ref[0],
            margin_ref[1] + from_a_ref[0] + from_b_ref[0],
            margin_ref[2] + from_b_ref[1],
        ],
        axis=0,
    )
    count = totals.shape[0]
    upper, lower = pieces(totals, 2)
    mixed = [
        jnp.dot(
            jnp.concatenate([upper, lower], axis=0), mixing, preferred_element_type=f32
        )
        for mixing in pieces(mixing_ref[...], 2)
    ]
    scaled = mixed[0][:count] + (mixed[0][count:] + mixed[1][:count])
    for group in range(GROUPS):
        scaled_ref[group] = scaled[group * 8 : group * 8 + 8]
    weighted = [factor_ref[...] * scaled[group * 8 : group * 8 + 8] for group in (1, 2)]
    weighted_ref[...] = weighted[0]
    parts_ref[...] = jnp.concatenate(
        [
            jnp.sum(force * weight, axis=0, keepdims=True)
            for weight, force_group in zip(weighted, forces)
            for force in force_group
        ]
        + [jnp.zeros((2, LANES), f32)],
        axis=0,
    )


def combine_kernel(parts_ref, weighted_ref, force_from_a_ref, copies_ref):
    from_a = [
        jnp.sum(force_from_a_ref[k] * weighted_ref[...], axis=0, keepdims=True) for k in range(3)
    ]
    own = parts_ref[0:3] + jnp.concatenate(from_a, axis=0)
    bands = copies_ref.shape[0] // 2
    _, odd = own_domain()
    for value, half in ((own, 1 - odd), (parts_ref[3:6], odd)):
        for band in range(bands):
            copies_ref[half * bands + band] = value


def total_kernel(gathered_ref, forces_ref):
    atoms = forces_ref.shape[1]
    rows = jnp.sum(gathered_ref[...], axis=0)
    source = lax.broadcasted_iota(jnp.int32, (LANES, LANES), 0)
    target = lax.broadcasted_iota(jnp.int32, (LANES, LANES), 1)
    collect = (lax.shift_right_logical(source, 3) == target).astype(bf16)
    forces = sum(jnp.dot(piece, collect, preferred_element_type=f32) for piece in pieces(rows, 3))
    forces_ref[...] = forces[:, :atoms]


def apply_kernel(
    rows_ref,
    wave_hbm,
    pot_hbm,
    halo_a0_ref,
    halo_a1_ref,
    halo_b_ref,
    table_ref,
    scaled_ref,
    out_hbm,
    out_ref,
    add_ref,
    wave_ref,
    pot_ref,
    sems,
    edge_sems,
):
    bands, planes, width_y, width_z = out_ref.shape
    lane = lax.broadcasted_iota(jnp.int32, (8, LANES), 1)

    def wave_copy(plane):
        return pltpu.make_async_copy(
            wave_hbm.at[:, pl.ds(plane, 1)],
            wave_ref.at[:, pl.ds(plane + PAD, 1)],
            sems.at[0, plane],
        )

    def out_copy(plane):
        at_plane = (slice(None), pl.ds(plane, 1))
        return pltpu.make_async_copy(
            out_ref.at[at_plane], out_hbm.at[at_plane], sems.at[1, plane]
        )

    _, odd = own_domain()
    far_end = planes + PAD
    edge_copies = [
        start_copy(
            halo_a0_ref,
            wave_ref.at[pl.ds(0, bands // 2), pl.ds(far_end * (1 - odd), PAD)],
            edge_sems.at[1],
        ),
        start_copy(
            halo_a1_ref,
            wave_ref.at[pl.ds(bands // 2, bands // 2), pl.ds(far_end * (1 - odd), PAD)],
            edge_sems.at[0],
        ),
        start_copy(halo_b_ref, wave_ref.at[:, pl.ds(far_end * odd, PAD)], edge_sems.at[2]),
        start_copy(pot_hbm, pot_ref, edge_sems.at[3]),
    ]
    for plane in range(planes):
        wave_copy(plane).start()

    def clear(plane, carry):
        size = width_y * 8
        add_ref[pl.ds(pl.multiple_of(plane * size, size), size), :] = jnp.zeros((size, LANES), f32)
        return carry

    lax.fori_loop(0, planes, clear, 0)

    for group in range(GROUPS):
        scaled = scaled_ref[group]
        blocks = [
            jnp.where(lax.shift_right_logical(lane, 3) == s, scaled, 0.0)
            for s in range(ATOM_DEV)
        ]
        coef = jnp.concatenate(blocks, axis=0).astype(bf16)
        terms = jnp.dot(coef, table_ref[group], preferred_element_type=f32)
        for s in range(ATOM_DEV):
            base = pl.multiple_of(rows_ref[group * ATOM_DEV + s] * 8, 8)
            for k in range(8):
                where = pl.ds(base + k * 8, 8)
                add_ref[where, :] = (
                    add_ref[where, :] + terms[s * 8 : s * 8 + 8, k * LANES : (k + 1) * LANES]
                )

    along_y = circulant(-16.0, 1.0, 0.0, width_y)
    along_z = circulant(-16.0, 1.0, 90.0, width_z)
    for copy in edge_copies:
        copy.wait()
    for plane in range(PAD):
        wave_copy(plane).wait()

    def finish(plane, carry):
        @pl.when(plane + PAD < planes)
        def _():
            wave_copy(plane + PAD).wait()

        for b in range(bands):
            wave = wave_ref[b, plane + PAD]
            summed = jnp.dot(
                jnp.concatenate([wave, along_y], axis=1),
                jnp.concatenate([along_z, wave], axis=0),
                preferred_element_type=f32,
            )
            near = wave_ref[b, plane + 1].astype(f32) + wave_ref[b, plane + 3].astype(f32)
            far = wave_ref[b, plane].astype(f32) + wave_ref[b, plane + 4].astype(f32)
            value = (summed + far - 16.0 * near) * (1.0 / 24.0)
            value = value + pot_ref[plane] * wave.astype(f32)
            added = add_ref[pl.ds(plane * width_y * 8 + b, width_y, stride=8), :]
            out_ref[b, plane] = (value + added).astype(bf16)
        out_copy(plane).start()
        return carry

    lax.fori_loop(0, planes, finish, 0)
    for plane in range(planes):
        out_copy(plane).wait()


VMEM = pl.BlockSpec(memory_space=pltpu.VMEM)
SMEM = pl.BlockSpec(memory_space=pltpu.SMEM)
HBM = pl.BlockSpec(memory_space=pltpu.HBM)
ANY = pl.BlockSpec(memory_space=pl.ANY)
MIB = 2**20


def out_type(shape, dtype, spec):
    if spec is HBM:
        return pltpu.HBM(shape, dtype)
    if spec is SMEM:
        return pltpu.SMEM(shape, dtype)
    return jax.ShapeDtypeStruct(shape, dtype)


def in_hbm(x):
    return pltpu.with_memory_space_constraint(x, pltpu.HBM)


def call(kernel, name, outs, ins, out_specs, scratch=(), limit=8, **kwargs):
    return pl.pallas_call(
        kernel,
        out_shape=tuple(
            out_type(shape, dtype, spec)
            for (shape, dtype), spec in zip(outs, out_specs)
        ),
        in_specs=ins,
        out_specs=tuple(out_specs),
        scratch_shapes=list(scratch),
        compiler_params=pltpu.CompilerParams(vmem_limit_bytes=limit * MIB),
        cost_estimate=pl.CostEstimate(flops=1000, bytes_accessed=1000, transcendentals=0),
        name=name,
        **kwargs,
    )


def per_device(
    wavefunctions, potential, projectors, margin_atoms, tile_rows, coupling, band_weights
):
    band_count, plane_count, width_y, width_z = wavefunctions.shape
    entry_count, proj_count, tile_len = projectors.shape
    assert (band_count, proj_count, width_y, width_z) == (8, 8, 128, LANES)
    assert entry_count == GROUPS * ATOM_DEV
    grid_rows = (plane_count + 2 * PAD) * width_y * 8
    domain_count = lax.axis_size("dom")
    block = ((8, LANES), f32)
    pair = ((2, 8, LANES), f32)
    blocks = ((GROUPS, 8, LANES), f32)
    edge = ((band_count, PAD, width_y, width_z), bf16)
    slots = ((entry_count,), jnp.int32)
    slots_smem = pltpu.SMEM((entry_count,), jnp.int32)

    half_edge = ((band_count // 2, PAD, width_y, width_z), bf16)
    (to_b,) = call(
        edge_kernel, "edges", [edge], [HBM], [VMEM], [pltpu.SemaphoreType.DMA]
    )(in_hbm(wavefunctions))
    halo_b = swap_b(to_b)

    rows, grid, table, margins, margins_to_a, margins_to_c, *to_a = call(
        functools.partial(relayout_kernel, domain_count=domain_count),
        "relayout",
        [
            slots,
            ((grid_rows, LANES), f32),
            ((GROUPS, LANES, tile_len), bf16),
            blocks,
            pair,
            ((6, 8, LANES), f32),
            half_edge,
            half_edge,
        ],
        [HBM] * 4 + [VMEM],
        [SMEM] + [VMEM] * 7,
        [
            pltpu.VMEM(wavefunctions.shape, bf16),
            slots_smem,
            slots_smem,
            slots_smem,
            pltpu.VMEM(projectors.shape, bf16),
            pltpu.VMEM((GROUPS, LANES, tile_len), f32),
            pltpu.SemaphoreType.DMA((plane_count,)),
            pltpu.SemaphoreType.DMA((5,)),
        ],
    )(*map(in_hbm, (margin_atoms, tile_rows, wavefunctions, projectors)), to_b)

    rows = pltpu.with_memory_space_constraint(rows, pltpu.SMEM)
    from_a = swap_a(margins_to_a)
    halo_a = [swap_a(part) for part in to_a]
    (margins_to_b,) = call(forward_kernel, "forward", [((4, 8, LANES), f32)], [VMEM] * 2, [VMEM], limit=2)(
        margins, from_a
    )
    from_b = swap_b(margins_to_b)
    from_c = send_c(margins_to_c)

    grid, yz_margins, mixing, factor = call(
        gradient_kernel,
        "gradient",
        [
            ((grid_rows, LANES), f32),
            ((2, GROUPS, 8, LANES), f32),
            ((LANES, LANES), f32),
            block,
        ],
        [SMEM] + [VMEM] * 4 + [HBM] * 2 + [VMEM],
        [VMEM] * 4,
        [
            pltpu.VMEM((plane_count * width_y * 8, LANES), f32),
            pltpu.VMEM(coupling.shape, f32),
            pltpu.VMEM((1, band_count), f32),
            pltpu.SemaphoreType.DMA((2,)),
        ],
        input_output_aliases={1: 0},
    )(
        rows,
        grid,
        *halo_a,
        table,
        in_hbm(coupling),
        in_hbm(band_weights[None, :]),
        margins_to_b,
    )

    grid, force_to_a = call(
        first_kernel,
        "first",
        [((grid_rows, LANES), f32), blocks],
        [SMEM] + [VMEM] * 4,
        [VMEM] * 2,
        input_output_aliases={1: 0},
    )(rows, grid, halo_b, table, yz_margins)
    force_from_a = swap_a(force_to_a)
    scaled, weighted, parts = call(
        rest_kernel,
        "rest",
        [blocks, block, block],
        [SMEM] + [VMEM] * 10,
        [VMEM] * 3,
    )(
        rows,
        grid,
        table,
        yz_margins,
        margins,
        from_a,
        from_b,
        from_c,
        mixing,
        factor,
        force_to_a,
    )

    bands = lax.axis_size("band")
    pairs = [
        [dom * bands + band for dom in (i, partner_b(i, domain_count)) for band in range(bands)]
        for i in range(1, domain_count, 2)
    ]
    (copies,) = call(
        combine_kernel,
        "combine",
        [((2 * bands, 3, LANES), f32)],
        [VMEM] * 3,
        [VMEM],
        limit=2,
    )(parts, weighted, force_from_a)
    gathered = lax.all_to_all(copies, ("dom", "band"), 0, 0, axis_index_groups=pairs)

    (applied,) = call(
        apply_kernel,
        "apply",
        [(wavefunctions.shape, bf16)],
        [SMEM, HBM, HBM] + [VMEM] * 5,
        [HBM],
        [
            pltpu.VMEM(wavefunctions.shape, bf16),
            pltpu.VMEM((plane_count * width_y * 8, LANES), f32),
            pltpu.VMEM((band_count, plane_count + 2 * PAD, width_y, width_z), bf16),
            pltpu.VMEM(potential.shape, f32),
            pltpu.SemaphoreType.DMA((2, plane_count)),
            pltpu.SemaphoreType.DMA((4,)),
        ],
        limit=16,
    )(rows, in_hbm(wavefunctions), in_hbm(potential), *halo_a, halo_b, table, scaled)

    (forces,) = call(
        total_kernel, "total", [((3, ATOM_DEV), f32)], [VMEM], [VMEM], limit=2
    )(gathered)
    return (applied, forces)


def solution(mesh):
    placed = (
        P("band", "dom", None, None),
        P("dom", None, None),
        P("dom", None, None),
        P("dom"),
        P("dom"),
        P(),
        P("band"),
    )
    return jax.shard_map(
        per_device,
        mesh=mesh,
        in_specs=placed,
        out_specs=(P("band", "dom", None, None), P(None, "dom")),
        check_vma=False,
    )
```

```python
import functools

import jax
import jax.numpy as jnp
from jax import lax
from jax.experimental import pallas as pl
from jax.experimental.pallas import tpu as pltpu
from jax.sharding import PartitionSpec as P

ATOM_DEV = 12
GROUPS = 3
LANES = 128
PAD = 2

f32 = jnp.float32
bf16 = jnp.bfloat16


def partner_a(i):
    return i ^ 1


def partner_b(i, count):
    return (i + 1 if i % 2 else i - 1) % count


def swap_a(x):
    return lax.ppermute(x, "dom", [(i, partner_a(i)) for i in range(lax.axis_size("dom"))])


def swap_b(x):
    count = lax.axis_size("dom")
    return lax.ppermute(x, "dom", [(i, partner_b(i, count)) for i in range(count)])


def send_c(x):
    count = lax.axis_size("dom")
    return lax.ppermute(x, "dom", [(i, partner_a(partner_b(i, count))) for i in range(count)])


def own_domain():
    index = lax.axis_index("dom")
    return index, lax.bitwise_and(index, 1)


def plane_to_rows(sources, plane, dst, base):
    bands, _, width_y, _ = sources[0].shape
    for y0 in range(0, width_y, 16):
        for i, source in enumerate(sources):
            for b in range(bands):
                part = source[b, plane, y0 : y0 + 16, :].astype(f32)
                dst[pl.ds(base + y0 * 8 + i * bands + b, 16, stride=8), :] = part


def at_row(ref, base):
    return ref[pl.ds(pl.multiple_of(base, 8), 8), :]


def diagonal_blocks(product, field):
    lane = lax.broadcasted_iota(jnp.int32, (8, LANES), 1)
    total = jnp.zeros((8, LANES), f32)
    for s in range(ATOM_DEV):
        start = (field * ATOM_DEV + s) * 8
        total = total + jnp.where(
            lax.shift_right_logical(lane, 3) == s, product[start : start + 8, :], 0.0
        )
    return total


def tile_values(rows_ref, group, field):
    tiles = []
    for s in range(ATOM_DEV):
        base = pl.multiple_of(rows_ref[group * ATOM_DEV + s] * 8, 8)
        tiles.append(jnp.concatenate([field(base + k * 8) for k in range(8)], axis=1))
    return jnp.concatenate(tiles, axis=0)


def z_gradient_values(rows_ref, group, grid_ref, offset, stencil):
    rows = []
    for s in range(ATOM_DEV):
        base = pl.multiple_of(rows_ref[group * ATOM_DEV + s] * 8, 8)
        rows.append(grid_ref[pl.ds(base + offset, 64), :])
    values = jnp.concatenate(rows, axis=0).astype(bf16)
    values = jnp.dot(values, stencil, preferred_element_type=f32) * (1.0 / 12.0)
    tiles = []
    for s in range(ATOM_DEV):
        start = s * 64
        tiles.append(
            jnp.concatenate(
                [values[start + k * 8 : start + k * 8 + 8, :] for k in range(8)], axis=1
            )
        )
    return jnp.concatenate(tiles, axis=0)


def contract(fields, table):
    values = jnp.concatenate(fields, axis=0).astype(bf16)
    product = lax.dot_general(
        values, table, (((1,), (1,)), ((), ())), preferred_element_type=f32
    )
    return [diagonal_blocks(product, q) for q in range(len(fields))]


def measure(rows_ref, group, table, field):
    return contract([tile_values(rows_ref, group, field)], table)[0]


def start_copy(source, target, sem):
    copy = pltpu.make_async_copy(source, target, sem)
    copy.start()
    return copy


def edge_kernel(wave_hbm, to_b_ref, sem):
    planes = wave_hbm.shape[1]
    _, odd = own_domain()
    start_copy(wave_hbm.at[:, pl.ds((planes - PAD) * odd, PAD)], to_b_ref, sem).wait()


def relayout_kernel(
    atoms_hbm,
    first_rows_hbm,
    wave_hbm,
    proj_hbm,
    _,
    rows_ref,
    grid_ref,
    table_ref,
    margin_ref,
    to_a_ref,
    to_c_ref,
    edge_a0_ref,
    edge_a1_ref,
    wave_ref,
    atoms_ref,
    first_rows_ref,
    entry_ref,
    proj_ref,
    proj_scr,
    wave_sems,
    other_sems,
    *,
    domain_count,
):
    planes, width_y = wave_ref.shape[1:3]
    entry_count = rows_ref.shape[0]
    index, odd = own_domain()

    def plane_copy(plane):
        at_plane = (slice(None), pl.ds(plane, 1))
        return pltpu.make_async_copy(
            wave_hbm.at[at_plane], wave_ref.at[at_plane], wave_sems.at[plane]
        )

    atoms_copy = start_copy(atoms_hbm, atoms_ref, other_sems.at[0])
    first_copy = start_copy(first_rows_hbm, first_rows_ref, other_sems.at[1])
    for plane in range(planes):
        plane_copy(plane).start()
    proj_copy = start_copy(proj_hbm, proj_ref, other_sems.at[2])
    edge_copies = []
    for i, edge_ref in enumerate((edge_a0_ref, edge_a1_ref)):
        count = edge_ref.shape[0]
        source = wave_hbm.at[pl.ds(i * count, count), pl.ds((planes - PAD) * (1 - odd), PAD)]
        edge_copies.append(start_copy(source, edge_ref, other_sems.at[3 + i]))
    proj_scr[:, ATOM_DEV * 8 :, :] = jnp.zeros(
        (GROUPS, LANES - ATOM_DEV * 8, proj_scr.shape[2]), f32
    )
    atoms_copy.wait()
    first_copy.wait()

    def place(entry):
        atom = atoms_ref[entry]
        owner = lax.shift_right_logical(atom * 171, 11)
        above = lax.rem(owner - index + 1 + domain_count, domain_count)
        group = jnp.where(odd == 1, above, 2 - above)
        slot = group * ATOM_DEV + atom - owner * ATOM_DEV
        entry_ref[slot] = entry
        rows_ref[slot] = first_rows_ref[entry]

    for entry in range(entry_count):
        place(entry)

    def one_plane(plane, carry):
        plane_copy(plane).wait()
        plane_to_rows([wave_ref], plane, grid_ref, (plane + PAD) * width_y * 8)
        return carry

    lax.fori_loop(0, planes, one_plane, 0)
    proj_copy.wait()
    for group in range(GROUPS):
        for s in range(ATOM_DEV):
            entry = entry_ref[group * ATOM_DEV + s]
            proj_scr[group, s * 8 : s * 8 + 8, :] = proj_ref[entry].astype(f32)
        table = proj_scr[group].astype(bf16)
        table_ref[group] = table
        sums = measure(
            rows_ref, group, table, lambda base: at_row(grid_ref, base + PAD * width_y * 8)
        )
        margin_ref[group] = sums
        if group < 2:
            to_a_ref[group] = sums
        else:
            to_c_ref[...] = jnp.zeros(to_c_ref.shape, f32)
            to_c_ref[0] = sums
    for copy in edge_copies:
        copy.wait()


def forward_kernel(margin_ref, from_a_ref, to_b_ref):
    to_b_ref[0] = margin_ref[2]
    to_b_ref[1] = margin_ref[1] + from_a_ref[0]
    to_b_ref[2:] = jnp.zeros((to_b_ref.shape[0] - 2, 8, LANES), f32)


def circulant(near, far, center, length):
    row = lax.broadcasted_iota(jnp.int32, (length, length), 0)
    column = lax.broadcasted_iota(jnp.int32, (length, length), 1)
    distance = lax.bitwise_and(row - column, length - 1)
    table = jnp.where((distance == 1) | (distance == length - 1), near, 0.0)
    table = jnp.where((distance == 2) | (distance == length - 2), far, table)
    return jnp.where(distance == 0, center, table).astype(bf16)


def first_circulant(length):
    row = lax.broadcasted_iota(jnp.int32, (length, length), 0)
    column = lax.broadcasted_iota(jnp.int32, (length, length), 1)
    distance = lax.bitwise_and(row - column, length - 1)
    table = jnp.zeros((length, length), f32)
    for offset, factor in ((1, 8.0), (2, -1.0), (length - 1, -8.0), (length - 2, 1.0)):
        table = jnp.where(distance == offset, factor, table)
    return table.astype(bf16)


def gradient_kernel(
    rows_ref,
    grid_in,
    halo_a0_ref,
    halo_a1_ref,
    table_ref,
    coupling_hbm,
    weight_hbm,
    _,
    grid_ref,
    margin_ref,
    mixing_ref,
    factor_ref,
    y_ref,
    coupling_ref,
    weight_ref,
    sems,
):
    del grid_in
    copies = [
        start_copy(coupling_hbm, coupling_ref, sems.at[0]),
        start_copy(weight_hbm, weight_ref, sems.at[1]),
    ]
    width_y = LANES
    edge = PAD * width_y * 8
    planes = y_ref.shape[0] // (width_y * 8)

    def one_plane(plane, carry):
        base = pl.multiple_of(plane * width_y * 8, 8)
        row = [at_row(grid_ref, base + edge + (y % width_y) * 8) for y in range(-2, 2)]
        for y in range(width_y):
            row.append(at_row(grid_ref, base + edge + ((y + 2) % width_y) * 8))
            near = row[y + 3] - row[y + 1]
            far = row[y + 4] - row[y]
            y_ref[pl.ds(base + y * 8, 8), :] = (2.0 / 3.0) * near - (1.0 / 12.0) * far
        return carry

    lax.fori_loop(0, planes, one_plane, 0)

    _, odd = own_domain()
    for i in range(PAD):
        plane = i + (planes + PAD) * (1 - odd)
        plane_to_rows([halo_a0_ref, halo_a1_ref], i, grid_ref, plane * width_y * 8)

    for copy in copies:
        copy.wait()
    stencil = first_circulant(width_y)
    for group in range(GROUPS):
        second, third = contract(
            [
                tile_values(rows_ref, group, lambda base: at_row(y_ref, base)),
                z_gradient_values(rows_ref, group, grid_ref, edge, stencil),
            ],
            table_ref[group],
        )
        margin_ref[0, group] = second
        margin_ref[1, group] = third

    bands = weight_ref.shape[1]
    band = lax.broadcasted_iota(jnp.int32, (bands, bands), 0)
    other = lax.broadcasted_iota(jnp.int32, (bands, bands), 1)
    weights = jnp.broadcast_to(weight_ref[...], (bands, bands))
    column = jnp.sum(jnp.where(band == other, weights, 0.0), axis=1, keepdims=True)
    factor_ref[...] = jnp.broadcast_to(-2.0 * column, factor_ref.shape)

    proj_count = coupling_ref.shape[0]
    symmetric = 0.5 * (coupling_ref[...] + coupling_ref[...].T)
    index = lax.broadcasted_iota(jnp.int32, (proj_count, LANES), 0)
    lane = lax.broadcasted_iota(jnp.int32, (proj_count, LANES), 1)
    spread = (lax.bitwise_and(lane, proj_count - 1) == index).astype(f32)
    tiled = jnp.dot(
        symmetric, spread, precision=lax.Precision.HIGHEST, preferred_element_type=f32
    )
    for a in range(LANES // proj_count):
        keep = (lax.shift_right_logical(lane, 3) == a) & (lane < ATOM_DEV * proj_count)
        mixing_ref[a * proj_count : (a + 1) * proj_count, :] = jnp.where(keep, tiled, 0.0)


def along_x(grid_ref, hop):
    def field(base):
        near = at_row(grid_ref, base + 3 * hop) - at_row(grid_ref, base + hop)
        far = at_row(grid_ref, base + 4 * hop) - at_row(grid_ref, base)
        return (2.0 / 3.0) * near - (1.0 / 12.0) * far

    return field


def first_kernel(
    rows_ref,
    grid_in,
    halo_b_ref,
    table_ref,
    yz_ref,
    grid_ref,
    force_ref,
):
    del grid_in
    width_y = halo_b_ref.shape[2]
    hop = width_y * 8
    planes = grid_ref.shape[0] // hop - 2 * PAD
    _, odd = own_domain()

    for i in range(PAD):
        plane_to_rows([halo_b_ref], i, grid_ref, (i + (planes + PAD) * odd) * hop)
    force_ref[0] = measure(rows_ref, 0, table_ref[0], along_x(grid_ref, hop))
    for k in range(2):
        force_ref[1 + k] = yz_ref[k, 0]


def pieces(x, count):
    out = []
    for _ in range(count):
        piece = x.astype(bf16)
        out.append(piece)
        x = x - piece.astype(f32)
    return out


def rest_kernel(
    rows_ref,
    grid_ref,
    table_ref,
    yz_ref,
    margin_ref,
    from_a_ref,
    from_b_ref,
    from_c_ref,
    mixing_ref,
    factor_ref,
    _,
    scaled_ref,
    weighted_ref,
    parts_ref,
):
    forces = []
    for group in range(1, GROUPS):
        first = measure(rows_ref, group, table_ref[group], along_x(grid_ref, LANES * 8))
        forces.append([first, yz_ref[0, group], yz_ref[1, group]])
    totals = jnp.concatenate(
        [
            margin_ref[0] + from_a_ref[1] + from_c_ref[0],
            margin_ref[1] + from_a_ref[0] + from_b_ref[0],
            margin_ref[2] + from_b_ref[1],
        ],
        axis=0,
    )
    count = totals.shape[0]
    upper, lower = pieces(totals, 2)
    mixed = [
        jnp.dot(
            jnp.concatenate([upper, lower], axis=0), mixing, preferred_element_type=f32
        )
        for mixing in pieces(mixing_ref[...], 2)
    ]
    scaled = mixed[0][:count] + (mixed[0][count:] + mixed[1][:count])
    for group in range(GROUPS):
        scaled_ref[group] = scaled[group * 8 : group * 8 + 8]
    weighted = [factor_ref[...] * scaled[group * 8 : group * 8 + 8] for group in (1, 2)]
    weighted_ref[...] = weighted[0]
    parts_ref[...] = jnp.concatenate(
        [
            jnp.sum(force * weight, axis=0, keepdims=True)
            for weight, force_group in zip(weighted, forces)
            for force in force_group
        ]
        + [jnp.zeros((2, LANES), f32)],
        axis=0,
    )


def combine_kernel(parts_ref, weighted_ref, force_from_a_ref, copies_ref):
    from_a = [
        jnp.sum(force_from_a_ref[k] * weighted_ref[...], axis=0, keepdims=True) for k in range(3)
    ]
    own = parts_ref[0:3] + jnp.concatenate(from_a, axis=0)
    bands = copies_ref.shape[0] // 2
    _, odd = own_domain()
    for value, half in ((own, 1 - odd), (parts_ref[3:6], odd)):
        for band in range(bands):
            copies_ref[half * bands + band] = value


def total_kernel(gathered_ref, forces_ref):
    atoms = forces_ref.shape[1]
    rows = jnp.sum(gathered_ref[...], axis=0)
    rows = jnp.concatenate([rows, jnp.zeros((8 - rows.shape[0], LANES), f32)], axis=0)
    source = lax.broadcasted_iota(jnp.int32, (LANES, LANES), 0)
    target = lax.broadcasted_iota(jnp.int32, (LANES, LANES), 1)
    collect = (lax.shift_right_logical(source, 3) == target).astype(bf16)
    split = jnp.concatenate([piece.astype(f32) for piece in pieces(rows, 3)], axis=0)
    products = jnp.dot(split.astype(bf16), collect, preferred_element_type=f32)
    forces = products[0:8] + (products[8:16] + products[16:24])
    forces_ref[...] = forces[:3, :atoms]


def apply_kernel(
    rows_ref,
    wave_hbm,
    pot_hbm,
    halo_a0_ref,
    halo_a1_ref,
    halo_b_ref,
    table_ref,
    scaled_ref,
    out_hbm,
    out_ref,
    add_ref,
    wave_ref,
    pot_ref,
    sems,
    edge_sems,
):
    bands, planes, width_y, width_z = out_ref.shape
    lane = lax.broadcasted_iota(jnp.int32, (8, LANES), 1)

    def wave_copy(plane):
        return pltpu.make_async_copy(
            wave_hbm.at[:, pl.ds(plane, 1)],
            wave_ref.at[:, pl.ds(plane + PAD, 1)],
            sems.at[0, plane],
        )

    def out_copy(plane):
        at_plane = (slice(None), pl.ds(plane, 1))
        return pltpu.make_async_copy(
            out_ref.at[at_plane], out_hbm.at[at_plane], sems.at[1, plane]
        )

    _, odd = own_domain()
    far_end = planes + PAD
    edge_copies = [
        start_copy(
            halo_a0_ref,
            wave_ref.at[pl.ds(0, bands // 2), pl.ds(far_end * (1 - odd), PAD)],
            edge_sems.at[1],
        ),
        start_copy(
            halo_a1_ref,
            wave_ref.at[pl.ds(bands // 2, bands // 2), pl.ds(far_end * (1 - odd), PAD)],
            edge_sems.at[0],
        ),
        start_copy(halo_b_ref, wave_ref.at[:, pl.ds(far_end * odd, PAD)], edge_sems.at[2]),
        start_copy(pot_hbm, pot_ref, edge_sems.at[3]),
    ]
    for plane in range(planes):
        wave_copy(plane).start()

    def clear(plane, carry):
        size = width_y * 8
        add_ref[pl.ds(pl.multiple_of(plane * size, size), size), :] = jnp.zeros((size, LANES), f32)
        return carry

    lax.fori_loop(0, planes, clear, 0)

    for group in range(GROUPS):
        scaled = scaled_ref[group]
        blocks = [
            jnp.where(lax.shift_right_logical(lane, 3) == s, scaled, 0.0)
            for s in range(ATOM_DEV)
        ]
        coef = jnp.concatenate(blocks, axis=0).astype(bf16)
        terms = jnp.dot(coef, table_ref[group], preferred_element_type=f32)
        for s in range(ATOM_DEV):
            base = pl.multiple_of(rows_ref[group * ATOM_DEV + s] * 8, 8)
            for k in range(8):
                where = pl.ds(base + k * 8, 8)
                add_ref[where, :] = (
                    add_ref[where, :] + terms[s * 8 : s * 8 + 8, k * LANES : (k + 1) * LANES]
                )

    along_y = circulant(-16.0, 1.0, 0.0, width_y)
    along_z = circulant(-16.0, 1.0, 90.0, width_z)
    for copy in edge_copies:
        copy.wait()
    for plane in range(PAD):
        wave_copy(plane).wait()

    def finish(plane, carry):
        @pl.when(plane + PAD < planes)
        def _():
            wave_copy(plane + PAD).wait()

        for b in range(bands):
            wave = wave_ref[b, plane + PAD]
            summed = jnp.dot(
                jnp.concatenate([wave, along_y], axis=1),
                jnp.concatenate([along_z, wave], axis=0),
                preferred_element_type=f32,
            )
            near = wave_ref[b, plane + 1].astype(f32) + wave_ref[b, plane + 3].astype(f32)
            far = wave_ref[b, plane].astype(f32) + wave_ref[b, plane + 4].astype(f32)
            value = (summed + far - 16.0 * near) * (1.0 / 24.0)
            value = value + pot_ref[plane] * wave.astype(f32)
            added = add_ref[pl.ds(plane * width_y * 8 + b, width_y, stride=8), :]
            out_ref[b, plane] = (value + added).astype(bf16)
        out_copy(plane).start()
        return carry

    lax.fori_loop(0, planes, finish, 0)
    for plane in range(planes):
        out_copy(plane).wait()


VMEM = pl.BlockSpec(memory_space=pltpu.VMEM)
SMEM = pl.BlockSpec(memory_space=pltpu.SMEM)
HBM = pl.BlockSpec(memory_space=pltpu.HBM)
ANY = pl.BlockSpec(memory_space=pl.ANY)
MIB = 2**20


def out_type(shape, dtype, spec):
    if spec is HBM:
        return pltpu.HBM(shape, dtype)
    if spec is SMEM:
        return pltpu.SMEM(shape, dtype)
    return jax.ShapeDtypeStruct(shape, dtype)


def in_hbm(x):
    return pltpu.with_memory_space_constraint(x, pltpu.HBM)


def call(kernel, name, outs, ins, out_specs, scratch=(), limit=8, **kwargs):
    return pl.pallas_call(
        kernel,
        out_shape=tuple(
            out_type(shape, dtype, spec)
            for (shape, dtype), spec in zip(outs, out_specs)
        ),
        in_specs=ins,
        out_specs=tuple(out_specs),
        scratch_shapes=list(scratch),
        compiler_params=pltpu.CompilerParams(vmem_limit_bytes=limit * MIB),
        cost_estimate=pl.CostEstimate(flops=1000, bytes_accessed=1000, transcendentals=0),
        name=name,
        **kwargs,
    )


def per_device(
    wavefunctions, potential, projectors, margin_atoms, tile_rows, coupling, band_weights
):
    band_count, plane_count, width_y, width_z = wavefunctions.shape
    entry_count, proj_count, tile_len = projectors.shape
    assert (band_count, proj_count, width_y, width_z) == (8, 8, 128, LANES)
    assert entry_count == GROUPS * ATOM_DEV
    grid_rows = (plane_count + 2 * PAD) * width_y * 8 + 8
    domain_count = lax.axis_size("dom")
    block = ((8, LANES), f32)
    pair = ((2, 8, LANES), f32)
    blocks = ((GROUPS, 8, LANES), f32)
    edge = ((band_count, PAD, width_y, width_z), bf16)
    slots = ((entry_count,), jnp.int32)
    slots_smem = pltpu.SMEM((entry_count,), jnp.int32)

    half_edge = ((band_count // 2, PAD, width_y, width_z), bf16)
    (to_b,) = call(
        edge_kernel, "edges", [edge], [HBM], [VMEM], [pltpu.SemaphoreType.DMA]
    )(in_hbm(wavefunctions))
    halo_b = swap_b(to_b)

    rows, grid, table, margins, margins_to_a, margins_to_c, *to_a = call(
        functools.partial(relayout_kernel, domain_count=domain_count),
        "relayout",
        [
            slots,
            ((grid_rows, LANES), f32),
            ((GROUPS, LANES, tile_len), bf16),
            blocks,
            pair,
            ((6, 8, LANES), f32),
            half_edge,
            half_edge,
        ],
        [HBM] * 4 + [VMEM],
        [SMEM] + [VMEM] * 7,
        [
            pltpu.VMEM(wavefunctions.shape, bf16),
            slots_smem,
            slots_smem,
            slots_smem,
            pltpu.VMEM(projectors.shape, bf16),
            pltpu.VMEM((GROUPS, LANES, tile_len), f32),
            pltpu.SemaphoreType.DMA((plane_count,)),
            pltpu.SemaphoreType.DMA((5,)),
        ],
    )(*map(in_hbm, (margin_atoms, tile_rows, wavefunctions, projectors)), to_b)

    rows = pltpu.with_memory_space_constraint(rows, pltpu.SMEM)
    from_a = swap_a(margins_to_a)
    halo_a = [swap_a(part) for part in to_a]
    (margins_to_b,) = call(forward_kernel, "forward", [((4, 8, LANES), f32)], [VMEM] * 2, [VMEM], limit=2)(
        margins, from_a
    )
    from_b = swap_b(margins_to_b)
    from_c = send_c(margins_to_c)

    grid, yz_margins, mixing, factor = call(
        gradient_kernel,
        "gradient",
        [
            ((grid_rows, LANES), f32),
            ((2, GROUPS, 8, LANES), f32),
            ((LANES, LANES), f32),
            block,
        ],
        [SMEM] + [VMEM] * 4 + [HBM] * 2 + [VMEM],
        [VMEM] * 4,
        [
            pltpu.VMEM((plane_count * width_y * 8, LANES), f32),
            pltpu.VMEM(coupling.shape, f32),
            pltpu.VMEM((1, band_count), f32),
            pltpu.SemaphoreType.DMA((2,)),
        ],
        input_output_aliases={1: 0},
    )(
        rows,
        grid,
        *halo_a,
        table,
        in_hbm(coupling),
        in_hbm(band_weights[None, :]),
        margins_to_b,
    )

    grid, force_to_a = call(
        first_kernel,
        "first",
        [((grid_rows, LANES), f32), blocks],
        [SMEM] + [VMEM] * 4,
        [VMEM] * 2,
        input_output_aliases={1: 0},
    )(rows, grid, halo_b, table, yz_margins)
    force_from_a = swap_a(force_to_a)
    scaled, weighted, parts = call(
        rest_kernel,
        "rest",
        [blocks, block, block],
        [SMEM] + [VMEM] * 10,
        [VMEM] * 3,
    )(
        rows,
        grid,
        table,
        yz_margins,
        margins,
        from_a,
        from_b,
        from_c,
        mixing,
        factor,
        force_to_a,
    )

    bands = lax.axis_size("band")
    pairs = [
        [dom * bands + band for dom in (i, partner_b(i, domain_count)) for band in range(bands)]
        for i in range(1, domain_count, 2)
    ]
    (copies,) = call(
        combine_kernel,
        "combine",
        [((2 * bands, 3, LANES), f32)],
        [VMEM] * 3,
        [VMEM],
        limit=2,
    )(parts, weighted, force_from_a)
    gathered = lax.all_to_all(copies, ("dom", "band"), 0, 0, axis_index_groups=pairs)

    (applied,) = call(
        apply_kernel,
        "apply",
        [(wavefunctions.shape, bf16)],
        [SMEM, HBM, HBM] + [VMEM] * 5,
        [HBM],
        [
            pltpu.VMEM(wavefunctions.shape, bf16),
            pltpu.VMEM((plane_count * width_y * 8 + 8, LANES), f32),
            pltpu.VMEM((band_count, plane_count + 2 * PAD, width_y, width_z), bf16),
            pltpu.VMEM(potential.shape, f32),
            pltpu.SemaphoreType.DMA((2, plane_count)),
            pltpu.SemaphoreType.DMA((4,)),
        ],
        limit=16,
    )(rows, in_hbm(wavefunctions), in_hbm(potential), *halo_a, halo_b, table, scaled)

    (forces,) = call(
        total_kernel, "total", [((3, ATOM_DEV), f32)], [VMEM], [VMEM], limit=2
    )(gathered)
    return (applied, forces)


def solution(mesh):
    placed = (
        P("band", "dom", None, None),
        P("dom", None, None),
        P("dom", None, None),
        P("dom"),
        P("dom"),
        P(),
        P("band"),
    )
    return jax.shard_map(
        per_device,
        mesh=mesh,
        in_specs=placed,
        out_specs=(P("band", "dom", None, None), P(None, "dom")),
        check_vma=False,
    )
```

```python
import functools

import jax
import jax.numpy as jnp
from jax import lax
from jax.experimental import pallas as pl
from jax.experimental.pallas import tpu as pltpu
from jax.sharding import PartitionSpec as P

ATOM_DEV = 12
GROUPS = 3
LANES = 128
PAD = 2

f32 = jnp.float32
bf16 = jnp.bfloat16


def partner_a(i):
    return i ^ 1


def partner_b(i, count):
    return (i + 1 if i % 2 else i - 1) % count


def swap_a(x):
    return lax.ppermute(x, "dom", [(i, partner_a(i)) for i in range(lax.axis_size("dom"))])


def swap_b(x):
    count = lax.axis_size("dom")
    return lax.ppermute(x, "dom", [(i, partner_b(i, count)) for i in range(count)])


def send_c(x):
    count = lax.axis_size("dom")
    return lax.ppermute(x, "dom", [(i, partner_a(partner_b(i, count))) for i in range(count)])


def own_domain():
    index = lax.axis_index("dom")
    return index, lax.bitwise_and(index, 1)


def plane_to_rows(sources, plane, dst, base):
    bands, _, width_y, _ = sources[0].shape
    for y0 in range(0, width_y, 16):
        for i, source in enumerate(sources):
            for b in range(bands):
                part = source[b, plane, y0 : y0 + 16, :].astype(f32)
                dst[pl.ds(base + y0 * 8 + i * bands + b, 16, stride=8), :] = part


def at_row(ref, base):
    return ref[pl.ds(pl.multiple_of(base, 8), 8), :]


def diagonal_blocks(product, field):
    lane = lax.broadcasted_iota(jnp.int32, (8, LANES), 1)
    total = jnp.zeros((8, LANES), f32)
    for s in range(ATOM_DEV):
        start = (field * ATOM_DEV + s) * 8
        total = total + jnp.where(
            lax.shift_right_logical(lane, 3) == s, product[start : start + 8, :], 0.0
        )
    return total


def tile_values(rows_ref, group, field):
    tiles = []
    for s in range(ATOM_DEV):
        base = pl.multiple_of(rows_ref[group * ATOM_DEV + s] * 8, 8)
        tiles.append(jnp.concatenate([field(base + k * 8) for k in range(8)], axis=1))
    return jnp.concatenate(tiles, axis=0)


def z_gradient_values(rows_ref, group, grid_ref, offset, stencil):
    rows = []
    for s in range(ATOM_DEV):
        base = pl.multiple_of(rows_ref[group * ATOM_DEV + s] * 8, 8)
        rows.append(grid_ref[pl.ds(base + offset, 64), :])
    values = jnp.concatenate(rows, axis=0).astype(bf16)
    values = jnp.dot(values, stencil, preferred_element_type=f32) * (1.0 / 12.0)
    tiles = []
    for s in range(ATOM_DEV):
        start = s * 64
        tiles.append(
            jnp.concatenate(
                [values[start + k * 8 : start + k * 8 + 8, :] for k in range(8)], axis=1
            )
        )
    return jnp.concatenate(tiles, axis=0)


def contract(fields, table):
    values = jnp.concatenate(fields, axis=0).astype(bf16)
    product = lax.dot_general(
        values, table, (((1,), (1,)), ((), ())), preferred_element_type=f32
    )
    return [diagonal_blocks(product, q) for q in range(len(fields))]


def measure(rows_ref, group, table, field):
    return contract([tile_values(rows_ref, group, field)], table)[0]


def start_copy(source, target, sem):
    copy = pltpu.make_async_copy(source, target, sem)
    copy.start()
    return copy


def edge_kernel(wave_hbm, to_b_ref, sem):
    planes = wave_hbm.shape[1]
    _, odd = own_domain()
    start_copy(wave_hbm.at[:, pl.ds((planes - PAD) * odd, PAD)], to_b_ref, sem).wait()


def relayout_kernel(
    atoms_hbm,
    first_rows_hbm,
    wave_hbm,
    proj_hbm,
    _,
    rows_ref,
    grid_ref,
    table_ref,
    margin_ref,
    to_a_ref,
    to_c_ref,
    edge_a0_ref,
    edge_a1_ref,
    wave_ref,
    atoms_ref,
    first_rows_ref,
    entry_ref,
    proj_ref,
    proj_scr,
    wave_sems,
    other_sems,
    *,
    domain_count,
):
    planes, width_y = wave_ref.shape[1:3]
    entry_count = rows_ref.shape[0]
    index, odd = own_domain()

    def plane_copy(plane):
        at_plane = (slice(None), pl.ds(plane, 1))
        return pltpu.make_async_copy(
            wave_hbm.at[at_plane], wave_ref.at[at_plane], wave_sems.at[plane]
        )

    atoms_copy = start_copy(atoms_hbm, atoms_ref, other_sems.at[0])
    first_copy = start_copy(first_rows_hbm, first_rows_ref, other_sems.at[1])
    for plane in range(planes):
        plane_copy(plane).start()
    proj_copy = start_copy(proj_hbm, proj_ref, other_sems.at[2])
    edge_copies = []
    for i, edge_ref in enumerate((edge_a0_ref, edge_a1_ref)):
        count = edge_ref.shape[0]
        source = wave_hbm.at[pl.ds(i * count, count), pl.ds((planes - PAD) * (1 - odd), PAD)]
        edge_copies.append(start_copy(source, edge_ref, other_sems.at[3 + i]))
    proj_scr[:, ATOM_DEV * 8 :, :] = jnp.zeros(
        (GROUPS, LANES - ATOM_DEV * 8, proj_scr.shape[2]), f32
    )
    atoms_copy.wait()
    first_copy.wait()

    def place(entry):
        atom = atoms_ref[entry]
        owner = lax.shift_right_logical(atom * 171, 11)
        above = lax.rem(owner - index + 1 + domain_count, domain_count)
        group = jnp.where(odd == 1, above, 2 - above)
        slot = group * ATOM_DEV + atom - owner * ATOM_DEV
        entry_ref[slot] = entry
        rows_ref[slot] = first_rows_ref[entry]

    for entry in range(entry_count):
        place(entry)

    def one_plane(plane, carry):
        plane_copy(plane).wait()
        plane_to_rows([wave_ref], plane, grid_ref, (plane + PAD) * width_y * 8)
        return carry

    lax.fori_loop(0, planes, one_plane, 0)
    proj_copy.wait()
    for group in range(GROUPS):
        for s in range(ATOM_DEV):
            entry = entry_ref[group * ATOM_DEV + s]
            proj_scr[group, s * 8 : s * 8 + 8, :] = proj_ref[entry].astype(f32)
        table = proj_scr[group].astype(bf16)
        table_ref[group] = table
        sums = measure(
            rows_ref, group, table, lambda base: at_row(grid_ref, base + PAD * width_y * 8)
        )
        margin_ref[group] = sums
        if group < 2:
            to_a_ref[group] = sums
        else:
            to_c_ref[...] = jnp.zeros(to_c_ref.shape, f32)
            to_c_ref[0] = sums
    for copy in edge_copies:
        copy.wait()


def forward_kernel(margin_ref, from_a_ref, to_b_ref):
    to_b_ref[0] = margin_ref[2]
    to_b_ref[1] = margin_ref[1] + from_a_ref[0]
    to_b_ref[2:] = jnp.zeros((to_b_ref.shape[0] - 2, 8, LANES), f32)


def circulant(near, far, center, length):
    row = lax.broadcasted_iota(jnp.int32, (length, length), 0)
    column = lax.broadcasted_iota(jnp.int32, (length, length), 1)
    distance = lax.bitwise_and(row - column, length - 1)
    table = jnp.where((distance == 1) | (distance == length - 1), near, 0.0)
    table = jnp.where((distance == 2) | (distance == length - 2), far, table)
    return jnp.where(distance == 0, center, table).astype(bf16)


def first_circulant(length):
    row = lax.broadcasted_iota(jnp.int32, (length, length), 0)
    column = lax.broadcasted_iota(jnp.int32, (length, length), 1)
    distance = lax.bitwise_and(row - column, length - 1)
    table = jnp.zeros((length, length), f32)
    for offset, factor in ((1, 8.0), (2, -1.0), (length - 1, -8.0), (length - 2, 1.0)):
        table = jnp.where(distance == offset, factor, table)
    return table.astype(bf16)


def gradient_kernel(
    rows_ref,
    grid_in,
    halo_a0_ref,
    halo_a1_ref,
    table_ref,
    coupling_hbm,
    weight_hbm,
    _,
    grid_ref,
    margin_ref,
    mixing_ref,
    factor_ref,
    y_ref,
    coupling_ref,
    weight_ref,
    sems,
):
    del grid_in
    copies = [
        start_copy(coupling_hbm, coupling_ref, sems.at[0]),
        start_copy(weight_hbm, weight_ref, sems.at[1]),
    ]
    width_y = LANES
    edge = PAD * width_y * 8
    planes = y_ref.shape[0] // (width_y * 8)

    def one_plane(plane, carry):
        base = pl.multiple_of(plane * width_y * 8, 8)
        row = [at_row(grid_ref, base + edge + (y % width_y) * 8) for y in range(-2, 2)]
        for y in range(width_y):
            row.append(at_row(grid_ref, base + edge + ((y + 2) % width_y) * 8))
            y_ref[pl.ds(base + y * 8, 8), :] = 8.0 * (row[y + 3] - row[y + 1]) - (
                row[y + 4] - row[y]
            )
        return carry

    lax.fori_loop(0, planes, one_plane, 0)

    _, odd = own_domain()
    for i in range(PAD):
        plane = i + (planes + PAD) * (1 - odd)
        plane_to_rows([halo_a0_ref, halo_a1_ref], i, grid_ref, plane * width_y * 8)

    for copy in copies:
        copy.wait()
    stencil = first_circulant(width_y)
    for group in range(GROUPS):
        second, third = contract(
            [
                tile_values(rows_ref, group, lambda base: at_row(y_ref, base)) * (1.0 / 12.0),
                z_gradient_values(rows_ref, group, grid_ref, edge, stencil),
            ],
            table_ref[group],
        )
        margin_ref[0, group] = second
        margin_ref[1, group] = third

    bands = weight_ref.shape[1]
    band = lax.broadcasted_iota(jnp.int32, (bands, bands), 0)
    other = lax.broadcasted_iota(jnp.int32, (bands, bands), 1)
    weights = jnp.broadcast_to(weight_ref[...], (bands, bands))
    column = jnp.sum(jnp.where(band == other, weights, 0.0), axis=1, keepdims=True)
    factor_ref[...] = jnp.broadcast_to(-2.0 * column, factor_ref.shape)

    proj_count = coupling_ref.shape[0]
    symmetric = 0.5 * (coupling_ref[...] + coupling_ref[...].T)
    index = lax.broadcasted_iota(jnp.int32, (proj_count, LANES), 0)
    lane = lax.broadcasted_iota(jnp.int32, (proj_count, LANES), 1)
    spread = (lax.bitwise_and(lane, proj_count - 1) == index).astype(f32)
    tiled = jnp.dot(
        symmetric, spread, precision=lax.Precision.HIGHEST, preferred_element_type=f32
    )
    for a in range(LANES // proj_count):
        keep = (lax.shift_right_logical(lane, 3) == a) & (lane < ATOM_DEV * proj_count)
        mixing_ref[a * proj_count : (a + 1) * proj_count, :] = jnp.where(keep, tiled, 0.0)


def along_x(grid_ref, hop):
    def field(base):
        near = at_row(grid_ref, base + 3 * hop) - at_row(grid_ref, base + hop)
        far = at_row(grid_ref, base + 4 * hop) - at_row(grid_ref, base)
        return (2.0 / 3.0) * near - (1.0 / 12.0) * far

    return field


def first_kernel(
    rows_ref,
    grid_in,
    halo_b_ref,
    table_ref,
    yz_ref,
    grid_ref,
    force_ref,
):
    del grid_in
    width_y = halo_b_ref.shape[2]
    hop = width_y * 8
    planes = grid_ref.shape[0] // hop - 2 * PAD
    _, odd = own_domain()

    for i in range(PAD):
        plane_to_rows([halo_b_ref], i, grid_ref, (i + (planes + PAD) * odd) * hop)
    force_ref[0] = measure(rows_ref, 0, table_ref[0], along_x(grid_ref, hop))
    for k in range(2):
        force_ref[1 + k] = yz_ref[k, 0]


def pieces(x, count):
    out = []
    for _ in range(count):
        piece = x.astype(bf16)
        out.append(piece)
        x = x - piece.astype(f32)
    return out


def rest_kernel(
    rows_ref,
    grid_ref,
    table_ref,
    yz_ref,
    margin_ref,
    from_a_ref,
    from_b_ref,
    from_c_ref,
    mixing_ref,
    factor_ref,
    _,
    scaled_ref,
    weighted_ref,
    parts_ref,
):
    forces = []
    for group in range(1, GROUPS):
        first = measure(rows_ref, group, table_ref[group], along_x(grid_ref, LANES * 8))
        forces.append([first, yz_ref[0, group], yz_ref[1, group]])
    totals = jnp.concatenate(
        [
            margin_ref[0] + from_a_ref[1] + from_c_ref[0],
            margin_ref[1] + from_a_ref[0] + from_b_ref[0],
            margin_ref[2] + from_b_ref[1],
        ],
        axis=0,
    )
    count = totals.shape[0]
    upper, lower = pieces(totals, 2)
    mixed = [
        jnp.dot(
            jnp.concatenate([upper, lower], axis=0), mixing, preferred_element_type=f32
        )
        for mixing in pieces(mixing_ref[...], 2)
    ]
    scaled = mixed[0][:count] + (mixed[0][count:] + mixed[1][:count])
    for group in range(GROUPS):
        scaled_ref[group] = scaled[group * 8 : group * 8 + 8]
    weighted = [factor_ref[...] * scaled[group * 8 : group * 8 + 8] for group in (1, 2)]
    weighted_ref[...] = weighted[0]
    parts_ref[...] = jnp.concatenate(
        [
            jnp.sum(force * weight, axis=0, keepdims=True)
            for weight, force_group in zip(weighted, forces)
            for force in force_group
        ]
        + [jnp.zeros((2, LANES), f32)],
        axis=0,
    )


def combine_kernel(parts_ref, weighted_ref, force_from_a_ref, copies_ref):
    from_a = [
        jnp.sum(force_from_a_ref[k] * weighted_ref[...], axis=0, keepdims=True) for k in range(3)
    ]
    own = parts_ref[0:3] + jnp.concatenate(from_a, axis=0)
    bands = copies_ref.shape[0] // 2
    _, odd = own_domain()
    for value, half in ((own, 1 - odd), (parts_ref[3:6], odd)):
        for band in range(bands):
            copies_ref[half * bands + band] = value


def total_kernel(gathered_ref, forces_ref):
    atoms = forces_ref.shape[1]
    rows = jnp.sum(gathered_ref[...], axis=0)
    rows = jnp.concatenate([rows, jnp.zeros((8 - rows.shape[0], LANES), f32)], axis=0)
    source = lax.broadcasted_iota(jnp.int32, (LANES, LANES), 0)
    target = lax.broadcasted_iota(jnp.int32, (LANES, LANES), 1)
    collect = (lax.shift_right_logical(source, 3) == target).astype(bf16)
    split = jnp.concatenate([piece.astype(f32) for piece in pieces(rows, 3)], axis=0)
    products = jnp.dot(split.astype(bf16), collect, preferred_element_type=f32)
    forces = products[0:8] + (products[8:16] + products[16:24])
    forces_ref[...] = forces[:3, :atoms]


def apply_kernel(
    rows_ref,
    wave_hbm,
    pot_hbm,
    halo_a0_ref,
    halo_a1_ref,
    halo_b_ref,
    table_ref,
    scaled_ref,
    out_hbm,
    out_ref,
    add_ref,
    wave_ref,
    pot_ref,
    sems,
    edge_sems,
):
    bands, planes, width_y, width_z = out_ref.shape
    lane = lax.broadcasted_iota(jnp.int32, (8, LANES), 1)

    def wave_copy(plane):
        return pltpu.make_async_copy(
            wave_hbm.at[:, pl.ds(plane, 1)],
            wave_ref.at[:, pl.ds(plane + PAD, 1)],
            sems.at[0, plane],
        )

    def out_copy(plane):
        at_plane = (slice(None), pl.ds(plane, 1))
        return pltpu.make_async_copy(
            out_ref.at[at_plane], out_hbm.at[at_plane], sems.at[1, plane]
        )

    _, odd = own_domain()
    far_end = planes + PAD
    edge_copies = [
        start_copy(
            halo_a0_ref,
            wave_ref.at[pl.ds(0, bands // 2), pl.ds(far_end * (1 - odd), PAD)],
            edge_sems.at[1],
        ),
        start_copy(
            halo_a1_ref,
            wave_ref.at[pl.ds(bands // 2, bands // 2), pl.ds(far_end * (1 - odd), PAD)],
            edge_sems.at[0],
        ),
        start_copy(halo_b_ref, wave_ref.at[:, pl.ds(far_end * odd, PAD)], edge_sems.at[2]),
        start_copy(pot_hbm, pot_ref, edge_sems.at[3]),
    ]
    for plane in range(planes):
        wave_copy(plane).start()

    def clear(plane, carry):
        size = width_y * 8
        add_ref[pl.ds(pl.multiple_of(plane * size, size), size), :] = jnp.zeros((size, LANES), f32)
        return carry

    lax.fori_loop(0, planes, clear, 0)

    for group in range(GROUPS):
        scaled = scaled_ref[group]
        blocks = [
            jnp.where(lax.shift_right_logical(lane, 3) == s, scaled, 0.0)
            for s in range(ATOM_DEV)
        ]
        coef = jnp.concatenate(blocks, axis=0).astype(bf16)
        terms = jnp.dot(coef, table_ref[group], preferred_element_type=f32)
        for s in range(ATOM_DEV):
            base = pl.multiple_of(rows_ref[group * ATOM_DEV + s] * 8, 8)
            for k in range(8):
                where = pl.ds(base + k * 8, 8)
                add_ref[where, :] = (
                    add_ref[where, :] + terms[s * 8 : s * 8 + 8, k * LANES : (k + 1) * LANES]
                )

    along_y = circulant(-16.0, 1.0, 0.0, width_y)
    along_z = circulant(-16.0, 1.0, 90.0, width_z)
    for copy in edge_copies:
        copy.wait()
    for plane in range(PAD):
        wave_copy(plane).wait()

    def finish(plane, carry):
        @pl.when(plane + PAD < planes)
        def _():
            wave_copy(plane + PAD).wait()

        for b in range(bands):
            wave = wave_ref[b, plane + PAD]
            summed = jnp.dot(
                jnp.concatenate([wave, along_y], axis=1),
                jnp.concatenate([along_z, wave], axis=0),
                preferred_element_type=f32,
            )
            near = wave_ref[b, plane + 1].astype(f32) + wave_ref[b, plane + 3].astype(f32)
            far = wave_ref[b, plane].astype(f32) + wave_ref[b, plane + 4].astype(f32)
            value = (summed + far - 16.0 * near) * (1.0 / 24.0)
            value = value + pot_ref[plane] * wave.astype(f32)
            added = add_ref[pl.ds(plane * width_y * 8 + b, width_y, stride=8), :]
            out_ref[b, plane] = (value + added).astype(bf16)
        out_copy(plane).start()
        return carry

    lax.fori_loop(0, planes, finish, 0)
    for plane in range(planes):
        out_copy(plane).wait()


VMEM = pl.BlockSpec(memory_space=pltpu.VMEM)
SMEM = pl.BlockSpec(memory_space=pltpu.SMEM)
HBM = pl.BlockSpec(memory_space=pltpu.HBM)
ANY = pl.BlockSpec(memory_space=pl.ANY)
MIB = 2**20


def out_type(shape, dtype, spec):
    if spec is HBM:
        return pltpu.HBM(shape, dtype)
    if spec is SMEM:
        return pltpu.SMEM(shape, dtype)
    return jax.ShapeDtypeStruct(shape, dtype)


def in_hbm(x):
    return pltpu.with_memory_space_constraint(x, pltpu.HBM)


def call(kernel, name, outs, ins, out_specs, scratch=(), limit=8, **kwargs):
    return pl.pallas_call(
        kernel,
        out_shape=tuple(
            out_type(shape, dtype, spec)
            for (shape, dtype), spec in zip(outs, out_specs)
        ),
        in_specs=ins,
        out_specs=tuple(out_specs),
        scratch_shapes=list(scratch),
        compiler_params=pltpu.CompilerParams(vmem_limit_bytes=limit * MIB),
        cost_estimate=pl.CostEstimate(flops=1000, bytes_accessed=1000, transcendentals=0),
        name=name,
        **kwargs,
    )


def per_device(
    wavefunctions, potential, projectors, margin_atoms, tile_rows, coupling, band_weights
):
    band_count, plane_count, width_y, width_z = wavefunctions.shape
    entry_count, proj_count, tile_len = projectors.shape
    assert (band_count, proj_count, width_y, width_z) == (8, 8, 128, LANES)
    assert entry_count == GROUPS * ATOM_DEV
    grid_rows = (plane_count + 2 * PAD) * width_y * 8 + 8
    domain_count = lax.axis_size("dom")
    block = ((8, LANES), f32)
    pair = ((2, 8, LANES), f32)
    blocks = ((GROUPS, 8, LANES), f32)
    edge = ((band_count, PAD, width_y, width_z), bf16)
    slots = ((entry_count,), jnp.int32)
    slots_smem = pltpu.SMEM((entry_count,), jnp.int32)

    half_edge = ((band_count // 2, PAD, width_y, width_z), bf16)
    (to_b,) = call(
        edge_kernel, "edges", [edge], [HBM], [VMEM], [pltpu.SemaphoreType.DMA]
    )(in_hbm(wavefunctions))
    halo_b = swap_b(to_b)

    rows, grid, table, margins, margins_to_a, margins_to_c, *to_a = call(
        functools.partial(relayout_kernel, domain_count=domain_count),
        "relayout",
        [
            slots,
            ((grid_rows, LANES), f32),
            ((GROUPS, LANES, tile_len), bf16),
            blocks,
            pair,
            ((6, 8, LANES), f32),
            half_edge,
            half_edge,
        ],
        [HBM] * 4 + [VMEM],
        [SMEM] + [VMEM] * 7,
        [
            pltpu.VMEM(wavefunctions.shape, bf16),
            slots_smem,
            slots_smem,
            slots_smem,
            pltpu.VMEM(projectors.shape, bf16),
            pltpu.VMEM((GROUPS, LANES, tile_len), f32),
            pltpu.SemaphoreType.DMA((plane_count,)),
            pltpu.SemaphoreType.DMA((5,)),
        ],
    )(*map(in_hbm, (margin_atoms, tile_rows, wavefunctions, projectors)), to_b)

    rows = pltpu.with_memory_space_constraint(rows, pltpu.SMEM)
    from_a = swap_a(margins_to_a)
    halo_a = [swap_a(part) for part in to_a]
    (margins_to_b,) = call(forward_kernel, "forward", [((4, 8, LANES), f32)], [VMEM] * 2, [VMEM], limit=2)(
        margins, from_a
    )
    from_b = swap_b(margins_to_b)
    from_c = send_c(margins_to_c)

    grid, yz_margins, mixing, factor = call(
        gradient_kernel,
        "gradient",
        [
            ((grid_rows, LANES), f32),
            ((2, GROUPS, 8, LANES), f32),
            ((LANES, LANES), f32),
            block,
        ],
        [SMEM] + [VMEM] * 4 + [HBM] * 2 + [VMEM],
        [VMEM] * 4,
        [
            pltpu.VMEM((plane_count * width_y * 8, LANES), f32),
            pltpu.VMEM(coupling.shape, f32),
            pltpu.VMEM((1, band_count), f32),
            pltpu.SemaphoreType.DMA((2,)),
        ],
        input_output_aliases={1: 0},
    )(
        rows,
        grid,
        *halo_a,
        table,
        in_hbm(coupling),
        in_hbm(band_weights[None, :]),
        margins_to_b,
    )

    grid, force_to_a = call(
        first_kernel,
        "first",
        [((grid_rows, LANES), f32), blocks],
        [SMEM] + [VMEM] * 4,
        [VMEM] * 2,
        input_output_aliases={1: 0},
    )(rows, grid, halo_b, table, yz_margins)
    force_from_a = swap_a(force_to_a)
    scaled, weighted, parts = call(
        rest_kernel,
        "rest",
        [blocks, block, block],
        [SMEM] + [VMEM] * 10,
        [VMEM] * 3,
    )(
        rows,
        grid,
        table,
        yz_margins,
        margins,
        from_a,
        from_b,
        from_c,
        mixing,
        factor,
        force_to_a,
    )

    bands = lax.axis_size("band")
    pairs = [
        [dom * bands + band for dom in (i, partner_b(i, domain_count)) for band in range(bands)]
        for i in range(1, domain_count, 2)
    ]
    (copies,) = call(
        combine_kernel,
        "combine",
        [((2 * bands, 3, LANES), f32)],
        [VMEM] * 3,
        [VMEM],
        limit=2,
    )(parts, weighted, force_from_a)
    gathered = lax.all_to_all(copies, ("dom", "band"), 0, 0, axis_index_groups=pairs)

    (applied,) = call(
        apply_kernel,
        "apply",
        [(wavefunctions.shape, bf16)],
        [SMEM, HBM, HBM] + [VMEM] * 5,
        [HBM],
        [
            pltpu.VMEM(wavefunctions.shape, bf16),
            pltpu.VMEM((plane_count * width_y * 8 + 8, LANES), f32),
            pltpu.VMEM((band_count, plane_count + 2 * PAD, width_y, width_z), bf16),
            pltpu.VMEM(potential.shape, f32),
            pltpu.SemaphoreType.DMA((2, plane_count)),
            pltpu.SemaphoreType.DMA((4,)),
        ],
        limit=16,
    )(rows, in_hbm(wavefunctions), in_hbm(potential), *halo_a, halo_b, table, scaled)

    (forces,) = call(
        total_kernel, "total", [((3, ATOM_DEV), f32)], [VMEM], [VMEM], limit=2
    )(gathered)
    return (applied, forces)


def solution(mesh):
    placed = (
        P("band", "dom", None, None),
        P("dom", None, None),
        P("dom", None, None),
        P("dom"),
        P("dom"),
        P(),
        P("band"),
    )
    return jax.shard_map(
        per_device,
        mesh=mesh,
        in_specs=placed,
        out_specs=(P("band", "dom", None, None), P(None, "dom")),
        check_vma=False,
    )
```
